32 devices in a mesh: grp: 2 (over x), view: 16 (over z, y, core).
Axes of the slice: x: 2, y: 2, z: 4, core: 2. Of those that a mesh axis runs over, the one named last changes fastest.
Arguments:
- volume: float32 [64, 16, 2, 512], P(('grp', 'view')), may hold values from 0 to 2
- footprint: bfloat16 [64, 2, 512, 896], P(('grp', 'view')), may hold values from -0.1875 to 0.1875
- measured: bfloat16 [256, 64, 896], P(('grp', 'view')), may hold values from 0 to 3
- angle_index: int32 [256], P(('grp', 'view')), may hold values from 0 to 1
- cover: int32 [256, 4], P(('grp', 'view')), may hold values from 0 to 63, as said below
- offset: int32 [256, 4], P(('grp', 'view')), may hold values from 0 to 48
- count: int32 [256], P(('grp', 'view')), may hold values from 1 to 4
Outputs:
- gradient: float32 [64, 16, 2, 512], P(('grp', 'view'))
The draws below stay inside these ranges and needn't reach their ends.
Inputs may be any that keep to these rules, and one draw needn't show every extreme that they name: Let p = v // 8. cover[v,k] lies between max(p - 4, 0) * 2 and min(p + 5, 32) * 2 - 1, and both ends are named by some slot 0 of p's views.
All inputs are finite; a program needn't handle non-finite values.
Results may differ from the reference program's by a relative error of at most 0.0019.
Values may be sent and summed in bfloat16 or wider, within the bound.
No kernel may reach another device: no remote copies, remote signals or barrier semaphores. Data moves between devices by JAX's collectives and lax.ppermute only.
A program may use at most 64 MiB of HBM per device.

```python
import jax
import jax.numpy as jnp
from jax import lax

VX = 512
YW = 2
DC = 896
DR = 64
BZ = 16
KMAX = 4
REACH = 4
A_DEV = 2
BLK_DEV = 2
V_DEV = 8
NBLOCKS = 64
VIEWS = 256
ANGLES = 64


def draw_cover(key, part):
    devices_all = VIEWS // V_DEV
    views_iota = jnp.arange(VIEWS, dtype=jnp.int32)
    owner = views_iota // V_DEV
    lowest = jnp.maximum(owner - REACH, 0) * BLK_DEV
    highest = jnp.minimum(owner + REACH + 1, devices_all) * BLK_DEV
    spread = highest - lowest
    raw = jax.random.randint(key, (VIEWS, KMAX), 0, 1048576, dtype=jnp.int32)
    picked = lowest[:, None] + raw % spread[:, None]
    first_slot = jnp.arange(KMAX, dtype=jnp.int32)[None, :] == 0
    local_view = (views_iota % V_DEV)[:, None]
    picked = jnp.where(first_slot & (local_view == 0), lowest[:, None], picked)
    picked = jnp.where(first_slot & (local_view == 1), highest[:, None] - 1, picked)
    return picked.astype(jnp.int32)


def plant(values, key, least, top_value):
    dims = values.shape
    place = [jax.random.randint(jax.random.fold_in(key, axis), (), 0, dims[axis]) for axis in range(len(dims))]
    values = values.at[tuple(place)].set(least)
    longest = dims.index(max(dims))
    place[longest] = (place[longest] + 1) % dims[longest]
    return values.at[tuple(place)].set(top_value)


def level_of(rng, extent, cuts, least, top_value):
    loudness, own = 1.0, jax.random.fold_in(rng, 6)
    for dim, shards_of in cuts:
        draws = jnp.exp(jax.random.uniform(jax.random.fold_in(own, dim), (shards_of,), jnp.float32, least / len(cuts), top_value / len(cuts)))
        loudness = loudness * jnp.repeat(draws, extent[dim] // shards_of).reshape([-1 if axis == dim else 1 for axis in range(len(extent))])
    return loudness


def normal_values(rng, extent, width, bound, shards=(), held_as=jnp.bfloat16):
    drawn = width * jax.random.normal(rng, extent, jnp.float32)
    if shards:
        drawn = drawn * level_of(rng, extent, shards, -0.22, 0.18)
    return jnp.clip(drawn, -bound, bound).astype(held_as)


def setup_inputs(seed: int = 0) -> dict:
    key_list = jax.random.split(jax.random.key(seed), 8)
    volume = jnp.clip(2.0 * jax.random.uniform(key_list[0], (NBLOCKS, BZ, YW, VX), jnp.float32) ** level_of(key_list[0], (NBLOCKS, BZ, YW, VX), ((0, 32),), -0.2, 0.2), 0.0, 2.0)
    footprint = normal_values(key_list[1], (ANGLES, YW, VX, DC), (YW * VX) ** -0.5, 0.1875, ((0, 32),))
    measured = jnp.clip(3.0 * jax.random.uniform(key_list[2], (VIEWS, DR, DC), jnp.float32) ** level_of(key_list[2], (VIEWS, DR, DC), ((0, 32),), -0.2, 0.2), 0.0, 3.0).astype(jnp.bfloat16)
    angle_index = plant(jax.random.randint(key_list[3], (VIEWS,), 0, A_DEV), jax.random.fold_in(key_list[3], 1), 0, A_DEV - 1).astype(jnp.int32)
    cover = draw_cover(jax.random.fold_in(key_list[7], 71), 0)
    offset = plant(jax.random.randint(key_list[5], (VIEWS, KMAX), 0, DR - BZ + 1), jax.random.fold_in(key_list[5], 1), 0, DR - BZ).astype(jnp.int32)
    count = plant(jax.random.randint(key_list[6], (VIEWS,), 1, KMAX + 1), jax.random.fold_in(key_list[6], 1), 1, KMAX).astype(jnp.int32)
    return {"volume": volume, "footprint": footprint, "measured": measured, "angle_index": angle_index, "cover": cover, "offset": offset, "count": count}


DELTA = 0.5
PRIOR_WEIGHT = 2.0


def reference(volume, footprint, measured, angle_index, cover, offset, count):
    vol_bf = volume.astype(jnp.bfloat16)
    nviews = measured.shape[0]
    zero_index = jnp.zeros((), jnp.int32)

    def view_step(grad, input_arrays):
        view_number, gantry_angle, block_indices, start_offsets, active_count, measured_sinogram = input_arrays
        table_row = footprint[(view_number // V_DEV) * A_DEV + gantry_angle].reshape(YW * VX, DC)
        blocks = vol_bf[block_indices].reshape(KMAX * BZ, YW * VX)
        part = jnp.dot(blocks, table_row, preferred_element_type=jnp.float32)
        forward_projection = jnp.zeros((DR, DC), jnp.float32)
        for slot in range(KMAX):
            alive = (slot < active_count).astype(jnp.float32)
            placed = lax.dynamic_update_slice(jnp.zeros((DR, DC), jnp.float32), part[slot * BZ:(slot + 1) * BZ], (start_offsets[slot].astype(jnp.int32), zero_index))
            forward_projection = forward_projection + alive * placed
        measured_float = measured_sinogram.astype(jnp.float32)
        weighted_residual = (jnp.exp(-measured_float) * (forward_projection - measured_float)).astype(jnp.bfloat16)
        for slot in range(KMAX):
            alive = (slot < active_count).astype(jnp.float32)
            picked = lax.dynamic_slice(weighted_residual, (start_offsets[slot].astype(jnp.int32), zero_index), (BZ, DC))
            back = lax.dot_general(picked, table_row, (((1,), (1,)), ((), ())), preferred_element_type=jnp.float32)
            grad = grad.at[block_indices[slot]].add(alive * back.reshape(BZ, YW, VX))
        return grad, None

    views_iota = jnp.arange(nviews, dtype=jnp.int32)
    data_grad, _ = lax.scan(view_step, jnp.zeros(volume.shape, jnp.float32), (views_iota, angle_index, cover, offset, count, measured))

    flat = volume.reshape(NBLOCKS * BZ, YW, VX)
    zdiff = jnp.clip(flat[1:] - flat[:-1], -DELTA, DELTA)
    prior = jnp.zeros(flat.shape, jnp.float32)
    prior = prior.at[1:].add(zdiff).at[:-1].add(-zdiff)
    ydiff = jnp.clip(flat[:, 1:] - flat[:, :-1], -DELTA, DELTA)
    prior = prior.at[:, 1:].add(ydiff).at[:, :-1].add(-ydiff)
    xdiff = jnp.clip(flat[:, :, 1:] - flat[:, :, :-1], -DELTA, DELTA)
    prior = prior.at[:, :, 1:].add(xdiff).at[:, :, :-1].add(-xdiff)
    return data_grad + PRIOR_WEIGHT * prior.reshape(volume.shape)
```

```python
import functools

import jax
import jax.numpy as jnp
from jax import lax
from jax.experimental import pallas as pl
from jax.experimental.pallas import tpu as pltpu
from jax.sharding import PartitionSpec as P

AXES = ("grp", "view")
DELTA = 0.5
PRIOR_WEIGHT = 2.0
CHUNK_PAIRS = 16


def both_ways(pairs):
    return pairs + [(b, a) for a, b in pairs]


def exchange_pairs(devices):
    chips = devices // 2
    swap = [(i, i ^ 1) for i in range(devices)]
    edge_y = [(i, i + 1) for i in range(0, chips, 2)]
    edge_d = [(i, i + 1) for i in range(1, chips - 1, 2)]
    edge_a = [(i + j, i + j + 2) for i in range(0, chips, 4) for j in (0, 1)]
    edge_b = [(i + j, i + j + 2) for i in range(2, chips - 2, 4) for j in (0, 1)]
    on_core = lambda edges, core: [(2 * a + core, 2 * b + core) for a, b in edges]
    last = devices - 1
    ends = [(0, 1), (1, 2), (2, 0), (last, last - 1), (last - 1, last - 3), (last - 3, last)]
    first = both_ways(on_core(edge_b, 0) + on_core(edge_d, 1)) + ends
    second = both_ways(on_core(edge_y, 0) + on_core(edge_a, 1))
    return swap, first, second


def pack_kernel(vol_ref, out_ref):
    slices = vol_ref.shape[0]
    row = vol_ref.shape[2]
    for y in range(vol_ref.shape[1]):
        cols = slice(y * row, (y + 1) * row)
        plane = vol_ref[:, y, :]
        high = plane.astype(jnp.bfloat16)
        rest = plane - high.astype(jnp.float32)
        mid = rest.astype(jnp.bfloat16)
        low = (rest - mid.astype(jnp.float32)).astype(jnp.bfloat16)
        out_ref[0:slices, cols] = high
        mid = mid.astype(jnp.float32)
        low = low.astype(jnp.float32)
        spare = jnp.concatenate(
            [
                mid[0:1],
                low[0:1],
                mid[slices - 1 : slices],
                low[slices - 1 : slices],
                jnp.zeros((4, row), jnp.float32),
            ],
            axis=0,
        )
        out_ref[slices : slices + 8, cols] = spare.astype(jnp.bfloat16)


def project_kernel(
    rows_ref,
    offset_ref,
    count_ref,
    angle_ref,
    own_ref,
    other_ref,
    near_ref,
    far_ref,
    table_ref,
    measured_ref,
    keep_ref,
    give_ref,
    window,
    table_proj,
    sino,
    picked,
    spread,
    grad,
    pos_ref,
):
    views, det_rows, channels = measured_ref.shape
    tables = table_ref.shape[0]
    slots = offset_ref.shape[1]
    slab = 16
    win_rows = window.shape[0]
    part = own_ref.shape[0] - 8
    piece = 2 * part
    window[0:piece, :] = near_ref[0:piece, :]
    window[piece : 2 * piece, :] = near_ref[piece + 8 : 2 * piece + 8, :]
    window[2 * piece : 3 * piece, :] = far_ref[0:piece, :]
    window[3 * piece : 4 * piece, :] = far_ref[piece + 8 : 2 * piece + 8, :]
    window[4 * piece : 4 * piece + part, :] = own_ref[0:part, :]
    window[4 * piece + part : 5 * piece, :] = other_ref[0:part, :]

    sino[...] = jnp.zeros_like(sino)
    grad[...] = jnp.zeros_like(grad)

    def count_table(view, total):
        return total + jnp.where(angle_ref[view] == 0, count_ref[view], 0)

    first_pairs = lax.fori_loop(0, views, count_table, 0)
    first_chunks = (first_pairs + CHUNK_PAIRS - 1) // CHUNK_PAIRS

    def forward(table, carry):
        table_proj[pl.ds(pl.multiple_of(table * win_rows, 16), win_rows), :] = jnp.dot(
            window[...], table_ref[table], preferred_element_type=jnp.float32
        )
        return carry

    lax.fori_loop(0, tables, forward, 0)

    def place(view, carry):
        base = angle_ref[view] * win_rows
        for slot in range(slots):

            @pl.when(slot < count_ref[view])
            def _():
                source = pl.multiple_of(base + rows_ref[view, slot], slab)
                target = view * det_rows + offset_ref[view, slot]
                for lane in range(0, channels, 128):
                    sino[lane // 128, pl.ds(target, slab), :] += table_proj[
                        pl.ds(source, slab), lane : lane + 128
                    ]

        return carry

    lax.fori_loop(0, views, place, 0)

    def weigh(view, carry):
        here = pl.ds(pl.multiple_of(view * det_rows, det_rows), det_rows)
        for lane in range(0, channels, 128):
            seen = measured_ref[view, :, lane : lane + 128].astype(jnp.float32)
            value = jnp.exp(-seen) * (sino[lane // 128, here, :] - seen)
            sino[lane // 128, here, :] = value.astype(jnp.bfloat16).astype(jnp.float32)
        return carry

    lax.fori_loop(0, views, weigh, 0)

    def pick(view, carry):
        zero_next, one_next = carry
        is_one = angle_ref[view] != 0
        start = jnp.where(is_one, one_next, zero_next)
        for slot in range(slots):

            @pl.when(slot < count_ref[view])
            def _():
                place_at = start + slot
                pos_ref[view * slots + slot] = place_at
                source = view * det_rows + offset_ref[view, slot]
                target = pl.multiple_of(place_at * slab, slab)
                for lane in range(0, channels, 128):
                    picked[pl.ds(target, slab), lane : lane + 128] = sino[
                        lane // 128, pl.ds(source, slab), :
                    ].astype(jnp.bfloat16)

        taken = count_ref[view]
        return (
            zero_next + jnp.where(is_one, 0, taken),
            one_next + jnp.where(is_one, taken, 0),
        )

    _, end = lax.fori_loop(0, views, pick, (jnp.int32(0), first_chunks * CHUNK_PAIRS))
    chunks = (end + CHUNK_PAIRS - 1) // CHUNK_PAIRS
    chunk_rows = CHUNK_PAIRS * slab

    def backward(chunk, carry):
        here = pl.ds(pl.multiple_of(chunk * chunk_rows, chunk_rows), chunk_rows)
        table = jnp.where(chunk < first_chunks, 0, 1)
        spread[here, :] = lax.dot_general(
            picked[here, :],
            table_ref[table],
            (((1,), (1,)), ((), ())),
            preferred_element_type=jnp.float32,
        )
        return carry

    lax.fori_loop(0, chunks, backward, 0)

    def collect(view, carry):
        for slot in range(slots):

            @pl.when(slot < count_ref[view])
            def _():
                source = pl.multiple_of(pos_ref[view * slots + slot] * slab, slab)
                target = pl.multiple_of(rows_ref[view, slot], slab)
                grad[pl.ds(target, slab), :] += spread[pl.ds(source, slab), :]

        return carry

    lax.fori_loop(0, views, collect, 0)
    keep_ref[0 : 2 * piece, :] = grad[0 : 2 * piece, :]
    keep_ref[2 * piece : 2 * piece + part, :] = grad[4 * piece : 4 * piece + part, :]
    give_ref[0 : 2 * piece, :] = grad[2 * piece : 4 * piece, :]
    give_ref[2 * piece : 2 * piece + part, :] = grad[4 * piece + part : 5 * piece, :]


def prior_kernel(scal_ref, vol_ref, own_ref, other_ref, near_ref, far_ref, out_ref):
    slices, strip, row = vol_ref.shape
    part = slices
    piece = 2 * part

    def halo(which, at):
        edge = 0 if which == 0 else part - 1

        def read(ref, base, tail):
            whole = ref[base + edge : base + edge + 1, :].astype(jnp.float32)
            more = ref[tail + 2 * which : tail + 2 * which + 2, :].astype(jnp.float32)
            return whole + more[0:1] + more[1:2]

        return read, at

    core = scal_ref[0]
    odd = scal_ref[1]
    has_low = scal_ref[2]
    has_high = scal_ref[3]
    step = piece + 8

    def piece_slice(which, exchange, via_me, via):
        qcore = 1 if which == 1 else 0
        sub = qcore ^ via
        ref = near_ref if via_me else far_ref
        base = exchange * step + sub * part
        tail = exchange * step + piece + 4 * sub
        read, _ = halo(which, None)
        return read(ref, base, tail)

    def other_slice(which):
        read, _ = halo(which, None)
        return read(other_ref, 0, part)

    def emit(low, high):
        for y in range(strip):
            cols = slice(y * row, (y + 1) * row)
            here = vol_ref[:, y, :]
            below = jnp.concatenate([low[:, cols], here[:-1]], axis=0)
            above = jnp.concatenate([here[1:], high[:, cols]], axis=0)
            iota = lax.broadcasted_iota(jnp.int32, here.shape, 0)
            down = jnp.clip(here - below, -DELTA, DELTA)
            down = jnp.where((iota > 0) | (has_low > 0), down, 0.0)
            up = jnp.clip(here - above, -DELTA, DELTA)
            up = jnp.where((iota < slices - 1) | (has_high > 0), up, 0.0)
            total = down + up
            if y > 0:
                total = total + jnp.clip(here - vol_ref[:, y - 1, :], -DELTA, DELTA)
            if y + 1 < strip:
                total = total + jnp.clip(here - vol_ref[:, y + 1, :], -DELTA, DELTA)
            lane = lax.broadcasted_iota(jnp.int32, here.shape, 1)
            left = jnp.clip(here - pltpu.roll(here, 1, 1), -DELTA, DELTA)
            total = total + jnp.where(lane > 0, left, 0.0)
            right = jnp.clip(here - pltpu.roll(here, row - 1, 1), -DELTA, DELTA)
            total = total + jnp.where(lane < row - 1, right, 0.0)
            out_ref[:, cols] = PRIOR_WEIGHT * total

    @pl.when((core == 0) & (odd == 0))
    def _():
        emit(piece_slice(1, 0, False, 1), other_slice(0))

    @pl.when((core == 0) & (odd == 1))
    def _():
        emit(piece_slice(1, 1, True, 0), other_slice(0))

    @pl.when((core == 1) & (odd == 0))
    def _():
        emit(other_slice(1), piece_slice(0, 1, False, 0))

    @pl.when((core == 1) & (odd == 1))
    def _():
        emit(other_slice(1), piece_slice(0, 0, True, 1))


def window_rows(cover, position, local_blocks, slab):
    core = position % 2
    chip = position // 2
    owner = cover // local_blocks
    owner_core = owner % 2
    delta = owner // 2 - chip
    nearer = jnp.abs(delta) == 1
    up = delta > 0
    is_y = up == (chip % 2 == 0)
    is_a = up == (chip % 4 < 2)
    second = jnp.where(nearer, is_y, is_a).astype(jnp.int32)
    via = jnp.where(nearer, jnp.where(is_y, 0, 1), jnp.where(is_a, 1, 0))
    part = local_blocks * slab
    away = ((via ^ core) * 2 + second) * 2 * part + (owner_core ^ via) * part
    here = 8 * part + (owner_core ^ core) * part
    return jnp.where(delta == 0, here, away) + (cover % local_blocks) * slab


def shards(volume, footprint, measured, angle_index, cover, offset, count):
    local_blocks, slab, strip, row = volume.shape
    views, det_rows, channels = measured.shape
    tables = footprint.shape[0]
    slots = cover.shape[1]
    plane = strip * row
    devices = lax.axis_size(AXES)
    position = lax.axis_index(AXES)
    core = position % 2
    swap, first, second = exchange_pairs(devices)
    send = lambda value, pairs: lax.ppermute(value, AXES, pairs)
    part = local_blocks * slab
    piece = 2 * part
    flat = volume.reshape(part, strip, row)
    vmem = pl.BlockSpec(memory_space=pltpu.VMEM)
    smem = pl.BlockSpec(memory_space=pltpu.SMEM)

    own = pl.pallas_call(
        pack_kernel,
        out_shape=jax.ShapeDtypeStruct((part + 8, plane), jnp.bfloat16),
        in_specs=[vmem],
        out_specs=vmem,
        name="pack",
    )(flat)
    other = send(own, swap)
    both = jnp.concatenate(
        [own[:part], other[:part], own[part : part + 4], other[part : part + 4]], axis=0
    )
    got_first = send(both, first)
    got_second = send(both, second)
    near = jnp.concatenate([got_first, got_second], axis=0)
    far = send(near, swap)

    rows = window_rows(cover, position, local_blocks, slab)
    keep, give = pl.pallas_call(
        project_kernel,
        out_shape=(
            jax.ShapeDtypeStruct((2 * piece + part, plane), jnp.float32),
            jax.ShapeDtypeStruct((2 * piece + part, plane), jnp.float32),
        ),
        in_specs=[smem] * 4 + [vmem] * 6,
        out_specs=(vmem, vmem),
        scratch_shapes=[
            pltpu.VMEM((5 * piece, plane), jnp.bfloat16),
            pltpu.VMEM((tables * 5 * piece, channels), jnp.float32),
            pltpu.VMEM((channels // 128, views * det_rows, 128), jnp.float32),
            pltpu.VMEM((views * slots * slab + CHUNK_PAIRS * slab, channels), jnp.bfloat16),
            pltpu.VMEM((views * slots * slab + CHUNK_PAIRS * slab, plane), jnp.float32),
            pltpu.VMEM((5 * piece, plane), jnp.float32),
            pltpu.SMEM((views * slots,), jnp.int32),
        ],
        compiler_params=pltpu.CompilerParams(vmem_limit_bytes=40 * 1024 * 1024),
        cost_estimate=pl.CostEstimate(flops=4_000_000_000, bytes_accessed=8_000_000, transcendentals=500_000),
        name="project",
    )(
        rows,
        offset,
        count,
        angle_index,
        own,
        other,
        near,
        far,
        footprint.reshape(tables, plane, channels),
        measured,
    )
    taken = send(give, swap)
    total = keep + taken
    wire = total[: 2 * piece].astype(jnp.bfloat16)
    back_first = send(wire[:piece], first)
    back_second = send(wire[piece:], second)

    scalars = jnp.stack(
        [
            core,
            (position // 2) % 2,
            (position > 0).astype(jnp.int32),
            (position < devices - 1).astype(jnp.int32),
        ]
    ).astype(jnp.int32)
    prior = pl.pallas_call(
        prior_kernel,
        out_shape=jax.ShapeDtypeStruct((part, plane), jnp.float32),
        in_specs=[smem] + [vmem] * 5,
        out_specs=vmem,
        name="prior",
        cost_estimate=pl.CostEstimate(flops=2_000_000, bytes_accessed=1_000_000, transcendentals=0),
    )(scalars, flat, own, other, near, far)

    arrived = back_first.astype(jnp.float32) + back_second.astype(jnp.float32)
    passed = send(arrived[part:], swap)
    data = total[2 * piece :] + arrived[:part] + passed
    return (data + prior).reshape(volume.shape)


def solution(mesh):
    in_specs = (
        P(AXES, None, None, None),
        P(AXES, None, None, None),
        P(AXES, None, None),
        P(AXES),
        P(AXES, None),
        P(AXES, None),
        P(AXES),
    )
    out_specs = P(AXES, None, None, None)
    return jax.shard_map(shards, mesh=mesh, in_specs=in_specs, out_specs=out_specs, check_vma=False)
```

```python
import functools

import jax
import jax.numpy as jnp
from jax import lax
from jax.experimental import pallas as pl
from jax.experimental.pallas import tpu as pltpu
from jax.sharding import PartitionSpec as P

AXES = ("grp", "view")
DELTA = 0.5
PRIOR_WEIGHT = 2.0
CHUNK_PAIRS = 16


def both_ways(pairs):
    return pairs + [(b, a) for a, b in pairs]


def exchange_pairs(devices):
    chips = devices // 2
    swap = [(i, i ^ 1) for i in range(devices)]
    edge_y = [(i, i + 1) for i in range(0, chips, 2)]
    edge_d = [(i, i + 1) for i in range(1, chips - 1, 2)]
    edge_a = [(i + j, i + j + 2) for i in range(0, chips, 4) for j in (0, 1)]
    edge_b = [(i + j, i + j + 2) for i in range(2, chips - 2, 4) for j in (0, 1)]
    on_core = lambda edges, core: [(2 * a + core, 2 * b + core) for a, b in edges]
    last = devices - 1
    ends = [(0, 1), (1, 2), (2, 0), (last, last - 1), (last - 1, last - 3), (last - 3, last)]
    first = both_ways(on_core(edge_b, 0) + on_core(edge_d, 1)) + ends
    second = both_ways(on_core(edge_y, 0) + on_core(edge_a, 1))
    return swap, first, second


def pack_kernel(vol_ref, out_ref):
    slices, strip, row = vol_ref.shape
    for y in range(strip):
        cols = slice(y * row, (y + 1) * row)
        plane = vol_ref[:, y, :]
        high = plane.astype(jnp.bfloat16)
        rest = plane - high.astype(jnp.float32)
        mid = rest.astype(jnp.bfloat16).astype(jnp.float32)
        low = rest - mid
        out_ref[0:slices, cols] = high
        spare = jnp.concatenate(
            [
                mid[0:1],
                low[0:1],
                mid[slices - 1 : slices],
                low[slices - 1 : slices],
                jnp.zeros((4, row), jnp.float32),
            ],
            axis=0,
        )
        out_ref[slices : slices + 8, cols] = spare.astype(jnp.bfloat16)


def join_kernel(own_ref, other_ref, out_ref):
    part = own_ref.shape[0] - 8
    out_ref[0:part, :] = own_ref[0:part, :]
    out_ref[part : 2 * part, :] = other_ref[0:part, :]
    mine = own_ref[part : part + 8, :].astype(jnp.float32)
    theirs = other_ref[part : part + 8, :].astype(jnp.float32)
    spare = jnp.concatenate([mine[0:4], theirs[0:4]], axis=0)
    out_ref[2 * part : 2 * part + 8, :] = spare.astype(jnp.bfloat16)


def early_kernel(own_ref, other_ref, table_ref, measured_ref, proj_ref, decay_ref, window):
    views, det_rows, channels = measured_ref.shape
    tables = table_ref.shape[0]
    part = own_ref.shape[0] - 8
    window[0:part, :] = own_ref[0:part, :]
    window[part : 2 * part, :] = other_ref[0:part, :]

    def forward(table, carry):
        here = pl.ds(pl.multiple_of(table * 2 * part, 16), 2 * part)
        proj_ref[here, :] = jnp.dot(
            window[...], table_ref[table], preferred_element_type=jnp.float32
        )
        return carry

    lax.fori_loop(0, tables, forward, 0)

    def fade(view, carry):
        here = pl.ds(pl.multiple_of(view * det_rows, det_rows), det_rows)
        for lane in range(0, channels, 128):
            seen = measured_ref[view, :, lane : lane + 128].astype(jnp.float32)
            decay_ref[lane // 128, here, :] = jnp.exp(-seen)
        return carry

    lax.fori_loop(0, views, fade, 0)


def project_kernel(
    scal_ref,
    near_ref,
    far_ref,
    table_ref,
    measured_ref,
    own_proj_ref,
    decay_ref,
    keep_ref,
    give_ref,
    window,
    table_proj,
    sino,
    picked,
    spread,
    row_ref,
    *,
    local_blocks,
    slots,
):
    views, det_rows, channels = measured_ref.shape
    tables = table_ref.shape[0]
    slab = 16
    part = local_blocks * slab
    piece = 2 * part
    win_rows = 5 * piece
    away_rows = 4 * piece
    position = scal_ref[2 * slots + 2, 0]
    core = lax.rem(position, 2)
    chip = position // 2

    angle_of = lambda view: scal_ref[2 * slots + 1, view]
    count_of = lambda view: scal_ref[2 * slots, view]
    offset_of = lambda view, slot: scal_ref[slots + slot, view]

    def window_row(block):
        owner = block // local_blocks
        owner_core = lax.rem(owner, 2)
        delta = owner // 2 - chip
        up = delta > 0
        nearer = jnp.abs(delta) == 1
        is_y = up == (lax.rem(chip, 2) == 0)
        is_a = up == (lax.rem(chip, 4) < 2)
        second = jnp.where(nearer, is_y, is_a).astype(jnp.int32)
        via = jnp.where(nearer, 1 - is_y.astype(jnp.int32), is_a.astype(jnp.int32))
        differ = lambda one, two: jnp.where(one == two, 0, 1)
        away = (differ(via, core) * 2 + second) * piece + differ(owner_core, via) * part
        here = away_rows + differ(owner_core, core) * part
        return jnp.where(delta == 0, here, away) + lax.rem(block, local_blocks) * slab

    window[0:piece, :] = near_ref[0:piece, :]
    window[piece : 2 * piece, :] = near_ref[piece + 8 : 2 * piece + 8, :]
    window[2 * piece : 3 * piece, :] = far_ref[0:piece, :]
    window[3 * piece : 4 * piece, :] = far_ref[piece + 8 : 2 * piece + 8, :]
    sino[...] = jnp.zeros_like(sino)
    keep_ref[...] = jnp.zeros_like(keep_ref)
    give_ref[...] = jnp.zeros_like(give_ref)

    def count_table(view, total):
        return total + jnp.where(angle_of(view) == 0, count_of(view), 0)

    first_pairs = lax.fori_loop(0, views, count_table, 0)
    first_chunks = (first_pairs + CHUNK_PAIRS - 1) // CHUNK_PAIRS

    def forward(table, carry):
        start = pl.multiple_of(table * win_rows, 16)
        table_proj[pl.ds(start, away_rows), :] = jnp.dot(
            window[...], table_ref[table], preferred_element_type=jnp.float32
        )
        table_proj[pl.ds(pl.multiple_of(start + away_rows, 16), piece), :] = own_proj_ref[
            pl.ds(pl.multiple_of(table * piece, 16), piece), :
        ]
        return carry

    lax.fori_loop(0, tables, forward, 0)

    def place(view, carry):
        base = angle_of(view) * win_rows
        for slot in range(slots):

            @pl.when(slot < count_of(view))
            def _():
                row = window_row(scal_ref[slot, view])
                row_ref[view * slots + slot] = row
                source = pl.multiple_of(base + row, slab)
                target = view * det_rows + offset_of(view, slot)
                for lane in range(0, channels, 128):
                    sino[lane // 128, pl.ds(target, slab), :] += table_proj[
                        pl.ds(source, slab), lane : lane + 128
                    ]

        return carry

    lax.fori_loop(0, views, place, 0)

    def weigh(view, carry):
        here = pl.ds(pl.multiple_of(view * det_rows, det_rows), det_rows)
        for lane in range(0, channels, 128):
            seen = measured_ref[view, :, lane : lane + 128].astype(jnp.float32)
            value = decay_ref[lane // 128, here, :] * (sino[lane // 128, here, :] - seen)
            sino[lane // 128, here, :] = value.astype(jnp.bfloat16).astype(jnp.float32)
        return carry

    lax.fori_loop(0, views, weigh, 0)

    def starts(view, carry):
        zero_next, one_next = carry
        is_one = angle_of(view) != 0
        taken = count_of(view)
        after = (
            zero_next + jnp.where(is_one, 0, taken),
            one_next + jnp.where(is_one, taken, 0),
        )
        return jnp.where(is_one, one_next, zero_next), after

    def pick(view, carry):
        start, after = starts(view, carry)
        for slot in range(slots):

            @pl.when(slot < count_of(view))
            def _():
                source = view * det_rows + offset_of(view, slot)
                target = pl.multiple_of((start + slot) * slab, slab)
                for lane in range(0, channels, 128):
                    picked[pl.ds(target, slab), lane : lane + 128] = sino[
                        lane // 128, pl.ds(source, slab), :
                    ].astype(jnp.bfloat16)

        return after

    first = (jnp.int32(0), first_chunks * CHUNK_PAIRS)
    _, end = lax.fori_loop(0, views, pick, first)
    chunks = (end + CHUNK_PAIRS - 1) // CHUNK_PAIRS
    chunk_rows = CHUNK_PAIRS * slab

    def backward(chunk, carry):
        here = pl.ds(pl.multiple_of(chunk * chunk_rows, chunk_rows), chunk_rows)
        table = jnp.where(chunk < first_chunks, 0, 1)
        spread[here, :] = lax.dot_general(
            picked[here, :],
            table_ref[table],
            (((1,), (1,)), ((), ())),
            preferred_element_type=jnp.float32,
        )
        return carry

    lax.fori_loop(0, chunks, backward, 0)

    def collect(view, carry):
        start, after = starts(view, carry)
        for slot in range(slots):

            @pl.when(slot < count_of(view))
            def _():
                source = pl.multiple_of((start + slot) * slab, slab)
                row = row_ref[view * slots + slot]
                at_home = row >= away_rows
                local = row - jnp.where(at_home, 2 * piece, 0)
                own_side = jnp.where(at_home, row < away_rows + part, row < 2 * piece)
                kept = pl.multiple_of(local, slab)
                given = pl.multiple_of(local - jnp.where(at_home, part, 2 * piece), slab)

                @pl.when(own_side)
                def _():
                    keep_ref[pl.ds(kept, slab), :] += spread[pl.ds(source, slab), :]

                @pl.when(jnp.logical_not(own_side))
                def _():
                    give_ref[pl.ds(given, slab), :] += spread[pl.ds(source, slab), :]

        return after

    lax.fori_loop(0, views, collect, first)


def prior_kernel(scal_ref, vol_ref, other_ref, near_ref, far_ref, out_ref, *, devices, scal_row):
    slices, strip, row = vol_ref.shape
    part = slices
    piece = 2 * part
    step = piece + 8
    position = scal_ref[scal_row, 0]
    core = lax.rem(position, 2)
    odd = lax.rem(position // 2, 2)

    def edge_slice(ref, which, base, tail):
        at = base + (part - 1) * which
        whole = ref[at : at + 1, :].astype(jnp.float32)
        more = ref[tail + 2 * which : tail + 2 * which + 2, :].astype(jnp.float32)
        return whole + (more[0:1] + more[1:2])

    def chip_slice(ref, which, exchange, via):
        sub = which ^ via
        return edge_slice(ref, which, exchange * step + sub * part, exchange * step + piece + 4 * sub)

    def emit(low, high):
        for y in range(strip):
            cols = slice(y * row, (y + 1) * row)
            here = vol_ref[:, y, :]
            below = jnp.concatenate([low[:, cols], here[:-1]], axis=0)
            above = jnp.concatenate([here[1:], high[:, cols]], axis=0)
            level = lax.broadcasted_iota(jnp.int32, here.shape, 0)
            down = jnp.clip(here - below, -DELTA, DELTA)
            total = jnp.where((level > 0) | (position > 0), down, 0.0)
            up = jnp.clip(here - above, -DELTA, DELTA)
            total += jnp.where((level < slices - 1) | (position < devices - 1), up, 0.0)
            if y > 0:
                total += jnp.clip(here - vol_ref[:, y - 1, :], -DELTA, DELTA)
            if y + 1 < strip:
                total += jnp.clip(here - vol_ref[:, y + 1, :], -DELTA, DELTA)
            lane = lax.broadcasted_iota(jnp.int32, here.shape, 1)
            left = jnp.clip(here - pltpu.roll(here, 1, 1), -DELTA, DELTA)
            total += jnp.where(lane > 0, left, 0.0)
            right = jnp.clip(here - pltpu.roll(here, row - 1, 1), -DELTA, DELTA)
            total += jnp.where(lane < row - 1, right, 0.0)
            out_ref[:, cols] = PRIOR_WEIGHT * total

    @pl.when((core == 0) & (odd == 0))
    def _():
        emit(chip_slice(far_ref, 1, 0, 1), edge_slice(other_ref, 0, 0, part))

    @pl.when((core == 0) & (odd == 1))
    def _():
        emit(chip_slice(near_ref, 1, 1, 0), edge_slice(other_ref, 0, 0, part))

    @pl.when((core == 1) & (odd == 0))
    def _():
        emit(edge_slice(other_ref, 1, 0, part), chip_slice(far_ref, 0, 1, 0))

    @pl.when((core == 1) & (odd == 1))
    def _():
        emit(edge_slice(other_ref, 1, 0, part), chip_slice(near_ref, 0, 0, 1))


def last_kernel(total_ref, arrived_ref, passed_ref, prior_ref, out_ref):
    part, strip, row = out_ref.shape
    for y in range(strip):
        cols = slice(y * row, (y + 1) * row)
        out_ref[:, y, :] = (
            (total_ref[:, cols] + arrived_ref[:, cols]) + passed_ref[:, cols]
        ) + prior_ref[:, cols]


def shards(volume, footprint, measured, angle_index, cover, offset, count):
    local_blocks, slab, strip, row = volume.shape
    views, det_rows, channels = measured.shape
    tables = footprint.shape[0]
    slots = cover.shape[1]
    plane = strip * row
    devices = lax.axis_size(AXES)
    position = lax.axis_index(AXES)
    swap, first, second = exchange_pairs(devices)
    send = lambda value, pairs: lax.ppermute(value, AXES, pairs)
    part = local_blocks * slab
    piece = 2 * part
    flat = volume.reshape(part, strip, row)
    table = footprint.reshape(tables, plane, channels)
    vmem = pl.BlockSpec(memory_space=pltpu.VMEM)
    smem = pl.BlockSpec(memory_space=pltpu.SMEM)
    shape = jax.ShapeDtypeStruct
    room = lambda mib: pltpu.CompilerParams(vmem_limit_bytes=mib * 1024 * 1024)
    cost = lambda flops, size: pl.CostEstimate(flops=flops, bytes_accessed=size, transcendentals=0)

    own = pl.pallas_call(
        pack_kernel,
        out_shape=shape((part + 8, plane), jnp.bfloat16),
        in_specs=[vmem],
        out_specs=vmem,
        compiler_params=room(4),
        name="pack",
    )(flat)
    other = send(own, swap)
    both = pl.pallas_call(
        join_kernel,
        out_shape=shape((piece + 8, plane), jnp.bfloat16),
        in_specs=[vmem] * 2,
        out_specs=vmem,
        compiler_params=room(4),
        name="join",
    )(own, other)
    got_first = send(both, first)
    got_second = send(both, second)

    scalars = jnp.concatenate(
        [
            cover.T,
            offset.T,
            count[None],
            angle_index[None],
            jnp.broadcast_to(position.astype(jnp.int32), (1, views)),
        ],
        axis=0,
    )
    own_proj, decay = pl.pallas_call(
        early_kernel,
        out_shape=(
            shape((tables * piece, channels), jnp.float32),
            shape((channels // 128, views * det_rows, 128), jnp.float32),
        ),
        in_specs=[vmem] * 4,
        out_specs=(vmem, vmem),
        scratch_shapes=[pltpu.VMEM((piece, plane), jnp.bfloat16)],
        compiler_params=room(16),
        cost_estimate=cost(1_000_000_000, 8_000_000),
        name="early",
    )(own, other, table, measured)
    got_first, got_second, own_proj, decay, scalars = lax.optimization_barrier(
        (got_first, got_second, own_proj, decay, scalars)
    )
    near = jnp.concatenate([got_first, got_second], axis=0)
    far = send(near, swap)

    pair_rows = views * slots * slab + CHUNK_PAIRS * slab
    keep, give = pl.pallas_call(
        functools.partial(project_kernel, local_blocks=local_blocks, slots=slots),
        out_shape=(
            shape((2 * piece + part, plane), jnp.float32),
            shape((2 * piece + part, plane), jnp.float32),
        ),
        in_specs=[smem] + [vmem] * 6,
        out_specs=(vmem, vmem),
        scratch_shapes=[
            pltpu.VMEM((4 * piece, plane), jnp.bfloat16),
            pltpu.VMEM((tables * 5 * piece, channels), jnp.float32),
            pltpu.VMEM((channels // 128, views * det_rows, 128), jnp.float32),
            pltpu.VMEM((pair_rows, channels), jnp.bfloat16),
            pltpu.VMEM((pair_rows, plane), jnp.float32),
            pltpu.SMEM((views * slots,), jnp.int32),
        ],
        compiler_params=room(32),
        cost_estimate=cost(4_000_000_000, 8_000_000),
        name="project",
    )(scalars, near, far, table, measured, own_proj, decay)
    taken = send(give, swap)
    total = keep + taken
    wire = total[: 2 * piece].astype(jnp.bfloat16)
    back_first = send(wire[:piece], first)
    back_second = send(wire[piece:], second)

    prior = pl.pallas_call(
        functools.partial(prior_kernel, devices=devices, scal_row=2 * slots + 2),
        out_shape=shape((part, plane), jnp.float32),
        in_specs=[smem] + [vmem] * 4,
        out_specs=vmem,
        compiler_params=room(8),
        cost_estimate=cost(10_000_000, 1_000_000),
        name="prior",
    )(scalars, flat, other, near, far)
    back_first, back_second, prior = lax.optimization_barrier((back_first, back_second, prior))

    arrived = back_first.astype(jnp.float32) + back_second.astype(jnp.float32)
    passed = send(arrived[part:], swap)
    out = pl.pallas_call(
        last_kernel,
        out_shape=shape((part, strip, row), jnp.float32),
        in_specs=[vmem] * 4,
        out_specs=vmem,
        compiler_params=room(4),
        name="last",
    )(total[2 * piece :], arrived[:part], passed, prior)
    return out.reshape(volume.shape)


def solution(mesh):
    in_specs = (
        P(AXES, None, None, None),
        P(AXES, None, None, None),
        P(AXES, None, None),
        P(AXES),
        P(AXES, None),
        P(AXES, None),
        P(AXES),
    )
    out_specs = P(AXES, None, None, None)
    return jax.shard_map(shards, mesh=mesh, in_specs=in_specs, out_specs=out_specs, check_vma=False)
```

```python
import functools

import jax
import jax.numpy as jnp
from jax import lax
from jax.experimental import pallas as pl
from jax.experimental.pallas import tpu as pltpu
from jax.sharding import PartitionSpec as P

AXES = ("grp", "view")
DELTA = 0.5
PRIOR_WEIGHT = 2.0


def both_ways(pairs):
    return pairs + [(b, a) for a, b in pairs]


def exchange_pairs(devices):
    chips = devices // 2
    swap = [(i, i ^ 1) for i in range(devices)]
    edge_y = [(i, i + 1) for i in range(0, chips, 2)]
    edge_d = [(i, i + 1) for i in range(1, chips - 1, 2)]
    edge_a = [(i + j, i + j + 2) for i in range(0, chips, 4) for j in (0, 1)]
    edge_b = [(i + j, i + j + 2) for i in range(2, chips - 2, 4) for j in (0, 1)]
    on_core = lambda edges, core: [(2 * a + core, 2 * b + core) for a, b in edges]
    last = devices - 1
    ends = [(0, 1), (1, 2), (2, 0), (last, last - 1), (last - 1, last - 3), (last - 3, last)]
    long = both_ways(on_core(edge_b, 0) + on_core(edge_d, 1)) + ends
    short = both_ways(on_core(edge_y, 0) + on_core(edge_a, 1))
    return swap, long, short


def load_kernel(source, target, sem):
    copy = pltpu.make_async_copy(source, target, sem)
    copy.start()
    copy.wait()


def join_kernel(own_ref, other_ref, out_ref):
    slices, strip, row = own_ref.shape
    for y in range(strip):
        cols = slice(y * row, (y + 1) * row)
        spare = []
        for k, ref in enumerate((own_ref, other_ref)):
            plane = ref[:, y, :]
            high = plane.astype(jnp.bfloat16)
            out_ref[k * slices : (k + 1) * slices, cols] = high
            rest = plane - high.astype(jnp.float32)
            mid = rest.astype(jnp.bfloat16).astype(jnp.float32)
            low = rest - mid
            for at in (0, slices - 1):
                spare += [mid[at : at + 1], low[at : at + 1]]
        spare = jnp.concatenate(spare, axis=0).astype(jnp.bfloat16)
        out_ref[2 * slices : 2 * slices + 8, cols] = spare


def window_rows(block, position, local_blocks, slab):
    part = local_blocks * slab
    piece = 2 * part
    core = lax.rem(position, 2)
    chip = position // 2
    owner = block // local_blocks
    owner_core = lax.rem(owner, 2)
    delta = owner // 2 - chip
    flag = lambda what: jnp.where(what, 1, 0)
    up = flag(delta > 0)
    nearer = jnp.abs(delta) == 1
    is_y = flag(up == 1 - lax.rem(chip, 2))
    is_a = flag(up == flag(lax.rem(chip, 4) < 2))
    short = jnp.where(nearer, is_y, is_a)
    via = jnp.where(nearer, 1 - is_y, is_a)
    away = (2 * jnp.abs(via - core) + short) * piece + jnp.abs(owner_core - via) * part
    here = 4 * piece + jnp.abs(owner_core - core) * part
    return jnp.where(delta == 0, here, away) + lax.rem(block, local_blocks) * slab


class Scalars:
    def __init__(self, ref):
        self.ref = ref
        self.slots = (ref.shape[0] - 2) // 2
        self.views = ref.shape[1]

    def each_pair(self, first_row, rows, do):
        def body(view, carry):
            count = self.ref[2 * self.slots, view]
            angle = self.ref[2 * self.slots + 1, view]
            for slot in range(self.slots):
                row = self.ref[slot, view]

                @pl.when((slot < count) & (row >= first_row) & (row < first_row + rows))
                def _():
                    do(view, angle, self.ref[self.slots + slot, view], row - first_row)

            return carry

        lax.fori_loop(0, self.views, body, 0)


def place(scal, sino, proj, first_row, rows, slab):
    det_rows = sino.shape[1] // scal.views

    def add(view, angle, offset, local):
        source = pl.multiple_of(angle * rows + local, slab)
        target = pl.ds(view * det_rows + offset, slab)
        for tile in range(sino.shape[0]):
            cols = slice(tile * 128, (tile + 1) * 128)
            sino[tile, target, :] += proj[pl.ds(source, slab), cols]

    scal.each_pair(first_row, rows, add)


def gather(scal, sino, decay, sums, first_row, rows, slab):
    det_rows = sino.shape[1] // scal.views

    def add(view, angle, offset, local):
        source = pl.ds(view * det_rows + offset, slab)
        target = pl.ds(pl.multiple_of(angle * rows + local, slab), slab)
        for tile in range(sino.shape[0]):
            cols = slice(tile * 128, (tile + 1) * 128)
            value = (decay[tile, source, :] * sino[tile, source, :]).astype(jnp.bfloat16)
            sums[target, cols] += value.astype(jnp.float32)

    scal.each_pair(first_row, rows, add)


def back_project(sums, turned_ref, group):
    total = None
    for table in range(turned_ref.shape[0]):
        value = sums[table * group : (table + 1) * group, :]
        high = value.astype(jnp.bfloat16)
        low = (value - high.astype(jnp.float32)).astype(jnp.bfloat16)
        both = jnp.concatenate([high, low], axis=0)
        got = jnp.dot(both, turned_ref[table], preferred_element_type=jnp.float32)
        got = got[:group] + got[group:]
        total = got if total is None else total + got
    return total


def early_kernel(
    both_ref,
    table_hbm,
    measured_hbm,
    cover_hbm,
    offset_hbm,
    count_hbm,
    angle_hbm,
    table_ref,
    turned_ref,
    scal_ref,
    sino_ref,
    decay_ref,
    measured,
    cover,
    offset,
    count,
    angle,
    scal,
    proj,
    sems,
    *,
    local_blocks,
    slab,
    here,
):
    views, det_rows, channels = measured.shape
    slots = cover.shape[0]
    piece = both_ref.shape[0] - 8
    small = [(cover_hbm, cover), (offset_hbm, offset), (count_hbm, count), (angle_hbm, angle)]
    copies = [pltpu.make_async_copy(a, b, sems.at[i]) for i, (a, b) in enumerate(small)]
    copies.append(pltpu.make_async_copy(measured_hbm, measured, sems.at[4]))
    for table in range(table_ref.shape[0]):
        copies.append(
            pltpu.make_async_copy(table_hbm.at[table], table_ref.at[table], sems.at[5 + table])
        )
    for copy in copies:
        copy.start()
    for copy in copies[:4]:
        copy.wait()
    scal_ref[0:slots, :] = window_rows(cover[...], here(), local_blocks, slab)
    scal_ref[slots : 2 * slots, :] = offset[...]
    scal_ref[2 * slots : 2 * slots + 1, :] = count[...]
    scal_ref[2 * slots + 1 : 2 * slots + 2, :] = angle[...]
    load = fetch(scal_ref, scal, sems.at[0])
    copies[4].wait()

    def fade(view, carry):
        rows = pl.ds(pl.multiple_of(view * det_rows, det_rows), det_rows)
        for tile in range(sino_ref.shape[0]):
            seen = measured[view, :, tile * 128 : (tile + 1) * 128].astype(jnp.float32)
            decay_ref[tile, rows, :] = jnp.exp(-seen)
            sino_ref[tile, rows, :] = -seen
        return carry

    lax.fori_loop(0, views, fade, 0)
    for table in range(table_ref.shape[0]):
        copies[5 + table].wait()
        turned_ref[table] = table_ref[table].T
        proj[table * piece : (table + 1) * piece, :] = jnp.dot(
            both_ref[0:piece, :], table_ref[table], preferred_element_type=jnp.float32
        )
    load.wait()
    place(Scalars(scal), sino_ref, proj, 4 * piece, piece, slab)


def project_into(sino_ref, begun_ref, scal, load, proj, pieces, table_ref, first_row, slab):
    rows = sum(piece.shape[0] for piece in pieces)
    sino_ref[...] = begun_ref[...]
    window = pieces[0] if len(pieces) == 1 else jnp.concatenate(pieces, axis=0)
    for table in range(table_ref.shape[0]):
        proj[table * rows : (table + 1) * rows, :] = jnp.dot(
            window, table_ref[table], preferred_element_type=jnp.float32
        )
    load.wait()
    place(scal, sino_ref, proj, first_row, rows, slab)


def fetch(scal_ref, scal, sem):
    load = pltpu.make_async_copy(scal_ref, scal, sem)
    load.start()
    return load


def middle_kernel(
    scal_ref, long_ref, short_ref, table_ref, begun_ref, sino_ref, scal, proj, sem, *, slab
):
    load = fetch(scal_ref, scal, sem)
    piece = long_ref.shape[0] - 8
    pieces = [long_ref[0:piece, :], short_ref[0:piece, :]]
    project_into(sino_ref, begun_ref, Scalars(scal), load, proj, pieces, table_ref, 0, slab)


def main_kernel(
    scal_ref,
    long_ref,
    short_ref,
    table_ref,
    turned_ref,
    begun_ref,
    decay_ref,
    sino_ref,
    give_ref,
    scal,
    proj,
    sums,
    sem,
    *,
    slab,
):
    load = fetch(scal_ref, scal, sem)
    piece = long_ref.shape[0] - 8
    sums[...] = jnp.zeros_like(sums)
    index = Scalars(scal)
    pieces = [long_ref[0:piece, :], short_ref[0:piece, :]]
    project_into(sino_ref, begun_ref, index, load, proj, pieces, table_ref, 2 * piece, slab)
    gather(index, sino_ref, decay_ref, sums, 2 * piece, 2 * piece, slab)
    give_ref[...] = back_project(sums, turned_ref, 2 * piece)


def rest_kernel(
    scal_ref, turned_ref, sino_ref, decay_ref, out_ref, scal, sums, sem, *, first_row, slab
):
    load = fetch(scal_ref, scal, sem)
    sums[...] = jnp.zeros_like(sums)
    rows = out_ref.shape[0]
    load.wait()
    gather(Scalars(scal), sino_ref, decay_ref, sums, first_row, rows, slab)
    out_ref[...] = back_project(sums, turned_ref, rows)


def prior_kernel(
    vol_ref, other_ref, long_ref, far_long_ref, short_ref, far_short_ref, out_ref, *, devices, here
):
    slices, strip, row = vol_ref.shape
    part = slices
    piece = 2 * part
    position = here()
    core = lax.rem(position, 2)
    odd = lax.rem(position // 2, 2)

    def chip_slice(ref, which, via):
        sub = which ^ via
        at = sub * part + (part - 1) * which
        tail = piece + 4 * sub + 2 * which
        whole = ref[at : at + 1, :].astype(jnp.float32)
        more = ref[tail : tail + 2, :].astype(jnp.float32)
        whole = whole + (more[0:1] + more[1:2])
        return lambda y: whole[:, y * row : (y + 1) * row]

    def core_slice(which):
        at = (part - 1) * which
        return lambda y: other_ref[at : at + 1, y, :]

    def emit(low, high):
        for y in range(strip):
            cols = slice(y * row, (y + 1) * row)
            here = vol_ref[:, y, :]
            below = jnp.concatenate([low(y), here[:-1]], axis=0)
            above = jnp.concatenate([here[1:], high(y)], axis=0)
            level = lax.broadcasted_iota(jnp.int32, here.shape, 0)
            down = jnp.clip(here - below, -DELTA, DELTA)
            total = jnp.where((level > 0) | (position > 0), down, 0.0)
            up = jnp.clip(here - above, -DELTA, DELTA)
            total += jnp.where((level < slices - 1) | (position < devices - 1), up, 0.0)
            if y > 0:
                total += jnp.clip(here - vol_ref[:, y - 1, :], -DELTA, DELTA)
            if y + 1 < strip:
                total += jnp.clip(here - vol_ref[:, y + 1, :], -DELTA, DELTA)
            lane = lax.broadcasted_iota(jnp.int32, here.shape, 1)
            left = jnp.clip(here - pltpu.roll(here, 1, 1), -DELTA, DELTA)
            total += jnp.where(lane > 0, left, 0.0)
            right = jnp.clip(here - pltpu.roll(here, row - 1, 1), -DELTA, DELTA)
            total += jnp.where(lane < row - 1, right, 0.0)
            out_ref[:, cols] = PRIOR_WEIGHT * total

    @pl.when((core == 0) & (odd == 0))
    def _():
        emit(chip_slice(far_long_ref, 1, 1), core_slice(0))

    @pl.when((core == 0) & (odd == 1))
    def _():
        emit(chip_slice(short_ref, 1, 0), core_slice(0))

    @pl.when((core == 1) & (odd == 0))
    def _():
        emit(core_slice(1), chip_slice(far_short_ref, 0, 0))

    @pl.when((core == 1) & (odd == 1))
    def _():
        emit(core_slice(1), chip_slice(long_ref, 0, 1))


def last_kernel(arrived_ref, passed_ref, prior_ref, out_ref):
    part, strip, row = out_ref.shape
    for y in range(strip):
        cols = slice(y * row, (y + 1) * row)
        out_ref[:, y, :] = (arrived_ref[:, cols] + passed_ref[:, cols]) + prior_ref[:, cols]


def shards(volume, footprint, measured, angle_index, cover, offset, count):
    local_blocks, slab, strip, row = volume.shape
    views, det_rows, channels = measured.shape
    tables = footprint.shape[0]
    slots = cover.shape[1]
    plane = strip * row
    devices = lax.axis_size(AXES)
    position = lax.axis_index(AXES)
    swap, long, short = exchange_pairs(devices)
    send = lambda value, pairs: lax.ppermute(value, AXES, pairs)
    part = local_blocks * slab
    piece = 2 * part
    flat = volume.reshape(part, strip, row)
    table = footprint.reshape(tables, plane, channels)
    vmem = pl.BlockSpec(memory_space=pltpu.VMEM)
    smem = pl.BlockSpec(memory_space=pltpu.SMEM)
    shape = jax.ShapeDtypeStruct
    room = lambda mib: pltpu.CompilerParams(vmem_limit_bytes=mib * 1024 * 1024)
    cost = lambda flops, size: pl.CostEstimate(flops=flops, bytes_accessed=size, transcendentals=0)

    here = lambda: lax.axis_index("grp") * lax.axis_size("view") + lax.axis_index("view")
    hbm = pl.BlockSpec(memory_space=pltpu.HBM)
    stay = lambda value: pltpu.with_memory_space_constraint(value, pltpu.HBM)

    other = send(flat, swap)
    mine = pl.pallas_call(
        load_kernel,
        out_shape=shape(flat.shape, flat.dtype),
        in_specs=[hbm],
        out_specs=vmem,
        scratch_shapes=[pltpu.SemaphoreType.DMA],
        compiler_params=room(4),
        cost_estimate=cost(1, 1),
        name="load",
    )(stay(flat))
    other, mine = lax.optimization_barrier((other, mine))
    both = pl.pallas_call(
        join_kernel,
        out_shape=shape((piece + 8, plane), jnp.bfloat16),
        in_specs=[vmem] * 2,
        out_specs=vmem,
        compiler_params=room(4),
        name="join",
    )(mine, other)
    got_short = send(both, short)
    got_long = send(both, long)

    sino_shape = shape((channels // 128, views * det_rows, 128), jnp.float32)
    scal_shape = (2 * slots + 2, views)
    table_vmem, turned, scalars, sino, decay = pl.pallas_call(
        functools.partial(early_kernel, local_blocks=local_blocks, slab=slab, here=here),
        out_shape=(
            shape(table.shape, table.dtype),
            shape((tables, channels, plane), table.dtype),
            shape(scal_shape, jnp.int32),
            sino_shape,
            sino_shape,
        ),
        in_specs=[vmem] + [hbm] * 6,
        out_specs=(vmem,) * 5,
        scratch_shapes=[
            pltpu.VMEM(measured.shape, measured.dtype),
            pltpu.VMEM((slots, views), jnp.int32),
            pltpu.VMEM((slots, views), jnp.int32),
            pltpu.VMEM((1, views), jnp.int32),
            pltpu.VMEM((1, views), jnp.int32),
            pltpu.SMEM(scal_shape, jnp.int32),
            pltpu.VMEM((tables * piece, channels), jnp.float32),
            pltpu.SemaphoreType.DMA((5 + tables,)),
        ],
        compiler_params=room(16),
        cost_estimate=cost(1, 1),
        name="early",
    )(
        both,
        stay(table),
        stay(measured),
        stay(cover.T),
        stay(offset.T),
        stay(count.reshape(1, views)),
        stay(angle_index.reshape(1, views)),
    )
    got_short, got_long, table_vmem, turned, scalars, sino, decay = lax.optimization_barrier(
        (got_short, got_long, table_vmem, turned, scalars, sino, decay)
    )
    index = [pltpu.SMEM(scal_shape, jnp.int32)]
    waits = [pltpu.SemaphoreType.DMA]
    proj = lambda rows: [pltpu.VMEM((tables * rows, channels), jnp.float32)]
    sums = lambda rows: [pltpu.VMEM((tables * rows, channels), jnp.float32)]

    far_short = send(got_short, swap)
    far_long = send(got_long, swap)
    sino = pl.pallas_call(
        functools.partial(middle_kernel, slab=slab),
        out_shape=sino_shape,
        in_specs=[vmem] * 5,
        out_specs=vmem,
        scratch_shapes=index + proj(2 * piece) + waits,
        compiler_params=room(16),
        cost_estimate=cost(1, 1),
        name="middle",
    )(scalars, got_long, got_short, table_vmem, sino)
    far_short, far_long, sino = lax.optimization_barrier((far_short, far_long, sino))
    sino, give = pl.pallas_call(
        functools.partial(main_kernel, slab=slab),
        out_shape=(sino_shape, shape((2 * piece, plane), jnp.float32)),
        in_specs=[vmem] * 7,
        out_specs=(vmem, vmem),
        scratch_shapes=index + proj(2 * piece) + sums(2 * piece) + waits,
        compiler_params=room(16),
        cost_estimate=cost(1, 1),
        name="main",
    )(scalars, far_long, far_short, table_vmem, turned, sino, decay)
    taken = send(give, swap)
    keep = pl.pallas_call(
        functools.partial(rest_kernel, first_row=0, slab=slab),
        out_shape=shape((2 * piece, plane), jnp.float32),
        in_specs=[vmem] * 4,
        out_specs=vmem,
        scratch_shapes=index + sums(2 * piece) + waits,
        compiler_params=room(16),
        cost_estimate=cost(1, 1),
        name="rest",
    )(scalars, turned, sino, decay)
    taken, keep = lax.optimization_barrier((taken, keep))
    wire = (keep + taken).astype(jnp.bfloat16)
    back_short = send(wire[piece:], short)
    back_long = send(wire[:piece], long)

    home = pl.pallas_call(
        functools.partial(rest_kernel, first_row=4 * piece, slab=slab),
        out_shape=shape((piece, plane), jnp.float32),
        in_specs=[vmem] * 4,
        out_specs=vmem,
        scratch_shapes=index + sums(piece) + waits,
        compiler_params=room(16),
        cost_estimate=cost(1, 1),
        name="home",
    )(scalars, turned, sino, decay)
    prior = pl.pallas_call(
        functools.partial(prior_kernel, devices=devices, here=here),
        out_shape=shape((part, plane), jnp.float32),
        in_specs=[vmem] * 6,
        out_specs=vmem,
        compiler_params=room(8),
        cost_estimate=cost(1, 1),
        name="prior",
    )(mine, other, got_long, far_long, got_short, far_short)
    back_short, back_long, home, prior = lax.optimization_barrier(
        (back_short, back_long, home, prior)
    )

    arrived = (back_short.astype(jnp.float32) + back_long.astype(jnp.float32)) + home
    passed = send(arrived[part:], swap)
    out = pl.pallas_call(
        last_kernel,
        out_shape=shape((part, strip, row), jnp.float32),
        in_specs=[vmem] * 3,
        out_specs=vmem,
        compiler_params=room(4),
        name="last",
    )(arrived[:part], passed, prior)
    return out.reshape(volume.shape)


def solution(mesh):
    in_specs = (
        P(AXES, None, None, None),
        P(AXES, None, None, None),
        P(AXES, None, None),
        P(AXES),
        P(AXES, None),
        P(AXES, None),
        P(AXES),
    )
    out_specs = P(AXES, None, None, None)
    return jax.shard_map(shards, mesh=mesh, in_specs=in_specs, out_specs=out_specs, check_vma=False)
```

```python
import functools

import jax
import jax.numpy as jnp
from jax import lax
from jax.experimental import pallas as pl
from jax.experimental.pallas import tpu as pltpu
from jax.sharding import PartitionSpec as P

AXES = ("grp", "view")
DELTA = 0.5
PRIOR_WEIGHT = 2.0


def both_ways(pairs):
    return pairs + [(b, a) for a, b in pairs]


def exchange_pairs(devices):
    chips = devices // 2
    swap = [(i, i ^ 1) for i in range(devices)]
    edge_y = [(i, i + 1) for i in range(0, chips, 2)]
    edge_d = [(i, i + 1) for i in range(1, chips - 1, 2)]
    edge_a = [(i + j, i + j + 2) for i in range(0, chips, 4) for j in (0, 1)]
    edge_b = [(i + j, i + j + 2) for i in range(2, chips - 2, 4) for j in (0, 1)]
    on_core = lambda edges, core: [(2 * a + core, 2 * b + core) for a, b in edges]
    last = devices - 1
    ends = [(0, 1), (1, 2), (2, 0), (last, last - 1), (last - 1, last - 3), (last - 3, last)]
    long = both_ways(on_core(edge_b, 0) + on_core(edge_d, 1)) + ends
    short = both_ways(on_core(edge_y, 0) + on_core(edge_a, 1))
    return swap, long, short


def load_kernel(source, target, sem):
    copy = pltpu.make_async_copy(source, target, sem)
    copy.start()
    copy.wait()


def join_kernel(own_ref, other_ref, out_ref):
    slices, strip, row = own_ref.shape
    for y in range(strip):
        cols = slice(y * row, (y + 1) * row)
        spare = []
        for k, ref in enumerate((own_ref, other_ref)):
            plane = ref[:, y, :]
            high = plane.astype(jnp.bfloat16)
            out_ref[k * slices : (k + 1) * slices, cols] = high
            rest = plane - high.astype(jnp.float32)
            mid = rest.astype(jnp.bfloat16).astype(jnp.float32)
            low = rest - mid
            for at in (0, slices - 1):
                spare += [mid[at : at + 1], low[at : at + 1]]
        spare = jnp.concatenate(spare, axis=0).astype(jnp.bfloat16)
        out_ref[2 * slices : 2 * slices + 8, cols] = spare


def window_rows(block, position, local_blocks, slab):
    part = local_blocks * slab
    piece = 2 * part
    core = lax.rem(position, 2)
    chip = position // 2
    owner = block // local_blocks
    owner_core = lax.rem(owner, 2)
    delta = owner // 2 - chip
    flag = lambda what: jnp.where(what, 1, 0)
    up = flag(delta > 0)
    nearer = jnp.abs(delta) == 1
    is_y = flag(up == 1 - lax.rem(chip, 2))
    is_a = flag(up == flag(lax.rem(chip, 4) < 2))
    short = jnp.where(nearer, is_y, is_a)
    via = jnp.where(nearer, 1 - is_y, is_a)
    away = (2 * jnp.abs(via - core) + short) * piece + jnp.abs(owner_core - via) * part
    here = 4 * piece + jnp.abs(owner_core - core) * part
    return jnp.where(delta == 0, here, away) + lax.rem(block, local_blocks) * slab


class Pairs:
    def __init__(self, ref):
        self.ref = ref

    def each(self, group, do):
        def body(i, carry):
            do(*(self.ref[3 * group + k, i] for k in range(3)))
            return carry

        lax.fori_loop(0, self.ref[9, group], body, 0)


def list_pairs(scal, lists, near_rows, det_rows):
    slots = (scal.shape[0] - 2) // 2

    def body(view, used):
        count = scal[2 * slots, view]
        table = scal[2 * slots + 1, view]
        for slot in range(slots):
            row = scal[slot, view]
            group = jnp.minimum(row // near_rows, 2)
            at = jnp.where(group == 0, used[0], jnp.where(group == 1, used[1], used[2]))

            @pl.when(slot < count)
            def _():
                lists[3 * group, at] = view * det_rows + scal[slots + slot, view]
                lists[3 * group + 1, at] = table
                lists[3 * group + 2, at] = row

            used = tuple(
                n + jnp.where((group == k) & (slot < count), 1, 0) for k, n in enumerate(used)
            )
        return used

    zero = jnp.int32(0)
    used = lax.fori_loop(0, scal.shape[1], body, (zero, zero, zero))
    for k, n in enumerate(used):
        lists[9, k] = n


def place(pairs, group, sino, proj, first_row, slab):
    width = sino.shape[0] * 128

    def add(target, table, row):
        source = pl.ds(pl.multiple_of(row - first_row, slab), slab)
        for tile in range(sino.shape[0]):
            cols = pl.ds(pl.multiple_of(table * width + tile * 128, 128), 128)
            sino[tile, pl.ds(target, slab), :] += proj[source, cols]

    pairs.each(group, add)


def gather(pairs, group, sino, decay, sums, first_row, slab):
    width = sino.shape[0] * 128

    def add(source, table, row):
        target = pl.ds(pl.multiple_of(row - first_row, slab), slab)
        here = pl.ds(source, slab)
        for tile in range(sino.shape[0]):
            cols = pl.ds(pl.multiple_of(table * width + tile * 128, 128), 128)
            value = (decay[tile, here, :] * sino[tile, here, :]).astype(jnp.bfloat16)
            sums[target, cols] += value.astype(jnp.float32)

    pairs.each(group, add)


def back_project(sums, turned_ref):
    rows = sums.shape[0]
    value = sums[...]
    high = value.astype(jnp.bfloat16)
    low = (value - high.astype(jnp.float32)).astype(jnp.bfloat16)
    both = jnp.concatenate([high, low], axis=0)
    got = jnp.dot(both, turned_ref[...], preferred_element_type=jnp.float32)
    return got[:rows] + got[rows:]


def early_kernel(
    both_ref,
    table_hbm,
    measured_hbm,
    cover_hbm,
    offset_hbm,
    count_hbm,
    angle_hbm,
    table_ref,
    turned_ref,
    lists_ref,
    sino_ref,
    decay_ref,
    measured,
    cover,
    offset,
    count,
    angle,
    index,
    scal,
    lists,
    proj,
    sems,
    *,
    local_blocks,
    slab,
    here,
):
    views, det_rows, channels = measured.shape
    slots = cover.shape[0]
    tables = table_hbm.shape[0]
    piece = both_ref.shape[0] - 8
    small = [(cover_hbm, cover), (offset_hbm, offset), (count_hbm, count), (angle_hbm, angle)]
    copies = [pltpu.make_async_copy(a, b, sems.at[i]) for i, (a, b) in enumerate(small)]
    copies.append(pltpu.make_async_copy(measured_hbm, measured, sems.at[4]))
    for table in range(tables):
        to = table_ref.at[:, table * channels : (table + 1) * channels]
        copies.append(pltpu.make_async_copy(table_hbm.at[table], to, sems.at[5 + table]))
    for copy in copies:
        copy.start()
    for copy in copies[:4]:
        copy.wait()
    index[0:slots, :] = window_rows(cover[...], here(), local_blocks, slab)
    index[slots : 2 * slots, :] = offset[...]
    index[2 * slots : 2 * slots + 1, :] = count[...]
    index[2 * slots + 1 : 2 * slots + 2, :] = angle[...]
    load = fetch(index, scal, sems.at[0])
    copies[4].wait()

    def fade(view, carry):
        rows = pl.ds(pl.multiple_of(view * det_rows, det_rows), det_rows)
        for tile in range(sino_ref.shape[0]):
            seen = measured[view, :, tile * 128 : (tile + 1) * 128].astype(jnp.float32)
            decay_ref[tile, rows, :] = jnp.exp(-seen)
            sino_ref[tile, rows, :] = -seen
        return carry

    lax.fori_loop(0, views, fade, 0)
    load.wait()
    list_pairs(scal, lists, 2 * piece, det_rows)
    save = fetch(lists, lists_ref, sems.at[0])
    for table in range(tables):
        copies[5 + table].wait()
        cols = slice(table * channels, (table + 1) * channels)
        turned_ref[cols, :] = table_ref[:, cols].T
    proj[...] = jnp.dot(both_ref[0:piece, :], table_ref[...], preferred_element_type=jnp.float32)
    place(Pairs(lists), 2, sino_ref, proj, 4 * piece, slab)
    save.wait()


def fetch(source, target, sem):
    load = pltpu.make_async_copy(source, target, sem)
    load.start()
    return load


def project(load, lists, group, long_ref, short_ref, table_ref, begun_ref, sino_ref, proj, slab):
    piece = long_ref.shape[0] - 8
    sino_ref[...] = begun_ref[...]
    window = jnp.concatenate([long_ref[0:piece, :], short_ref[0:piece, :]], axis=0)
    proj[...] = jnp.dot(window, table_ref[...], preferred_element_type=jnp.float32)
    load.wait()
    place(Pairs(lists), group, sino_ref, proj, group * 2 * piece, slab)


def middle_kernel(
    lists_ref, long_ref, short_ref, table_ref, begun_ref, sino_ref, lists, proj, sem, *, slab
):
    load = fetch(lists_ref, lists, sem)
    project(load, lists, 0, long_ref, short_ref, table_ref, begun_ref, sino_ref, proj, slab)


def main_kernel(
    lists_ref,
    long_ref,
    short_ref,
    table_ref,
    turned_ref,
    begun_ref,
    decay_ref,
    sino_ref,
    give_ref,
    lists,
    proj,
    sums,
    sem,
    *,
    slab,
):
    load = fetch(lists_ref, lists, sem)
    sums[...] = jnp.zeros_like(sums)
    project(load, lists, 1, long_ref, short_ref, table_ref, begun_ref, sino_ref, proj, slab)
    gather(Pairs(lists), 1, sino_ref, decay_ref, sums, sums.shape[0], slab)
    give_ref[...] = back_project(sums, turned_ref)


def rest_kernel(
    lists_ref, turned_ref, sino_ref, decay_ref, out_ref, lists, sums, sem, *, group, first_row, slab
):
    load = fetch(lists_ref, lists, sem)
    sums[...] = jnp.zeros_like(sums)
    load.wait()
    gather(Pairs(lists), group, sino_ref, decay_ref, sums, first_row, slab)
    out_ref[...] = back_project(sums, turned_ref)


def prior_kernel(
    vol_ref, other_ref, long_ref, far_long_ref, short_ref, far_short_ref, out_ref, *, devices, here
):
    slices, strip, row = vol_ref.shape
    part = slices
    piece = 2 * part
    position = here()
    core = lax.rem(position, 2)
    odd = lax.rem(position // 2, 2)

    def chip_slice(ref, which, via):
        sub = which ^ via
        at = sub * part + (part - 1) * which
        tail = piece + 4 * sub + 2 * which
        whole = ref[at : at + 1, :].astype(jnp.float32)
        more = ref[tail : tail + 2, :].astype(jnp.float32)
        whole = whole + (more[0:1] + more[1:2])
        return lambda y: whole[:, y * row : (y + 1) * row]

    def core_slice(which):
        at = (part - 1) * which
        return lambda y: other_ref[at : at + 1, y, :]

    def emit(low, high):
        for y in range(strip):
            cols = slice(y * row, (y + 1) * row)
            here = vol_ref[:, y, :]
            below = jnp.concatenate([low(y), here[:-1]], axis=0)
            above = jnp.concatenate([here[1:], high(y)], axis=0)
            level = lax.broadcasted_iota(jnp.int32, here.shape, 0)
            down = jnp.clip(here - below, -DELTA, DELTA)
            total = jnp.where((level > 0) | (position > 0), down, 0.0)
            up = jnp.clip(here - above, -DELTA, DELTA)
            total += jnp.where((level < slices - 1) | (position < devices - 1), up, 0.0)
            if y > 0:
                total += jnp.clip(here - vol_ref[:, y - 1, :], -DELTA, DELTA)
            if y + 1 < strip:
                total += jnp.clip(here - vol_ref[:, y + 1, :], -DELTA, DELTA)
            lane = lax.broadcasted_iota(jnp.int32, here.shape, 1)
            left = jnp.clip(here - pltpu.roll(here, 1, 1), -DELTA, DELTA)
            total += jnp.where(lane > 0, left, 0.0)
            right = jnp.clip(here - pltpu.roll(here, row - 1, 1), -DELTA, DELTA)
            total += jnp.where(lane < row - 1, right, 0.0)
            out_ref[:, cols] = PRIOR_WEIGHT * total

    @pl.when((core == 0) & (odd == 0))
    def _():
        emit(chip_slice(far_long_ref, 1, 1), core_slice(0))

    @pl.when((core == 0) & (odd == 1))
    def _():
        emit(chip_slice(short_ref, 1, 0), core_slice(0))

    @pl.when((core == 1) & (odd == 0))
    def _():
        emit(core_slice(1), chip_slice(far_short_ref, 0, 0))

    @pl.when((core == 1) & (odd == 1))
    def _():
        emit(core_slice(1), chip_slice(long_ref, 0, 1))


def last_kernel(arrived_ref, passed_ref, prior_ref, out_ref):
    part, strip, row = out_ref.shape
    for y in range(strip):
        cols = slice(y * row, (y + 1) * row)
        out_ref[:, y, :] = (arrived_ref[:, cols] + passed_ref[:, cols]) + prior_ref[:, cols]


def shards(volume, footprint, measured, angle_index, cover, offset, count):
    local_blocks, slab, strip, row = volume.shape
    views, det_rows, channels = measured.shape
    tables = footprint.shape[0]
    slots = cover.shape[1]
    plane = strip * row
    devices = lax.axis_size(AXES)
    position = lax.axis_index(AXES)
    swap, long, short = exchange_pairs(devices)
    send = lambda value, pairs: lax.ppermute(value, AXES, pairs)
    part = local_blocks * slab
    piece = 2 * part
    flat = volume.reshape(part, strip, row)
    table = footprint.reshape(tables, plane, channels)
    vmem = pl.BlockSpec(memory_space=pltpu.VMEM)
    smem = pl.BlockSpec(memory_space=pltpu.SMEM)
    shape = jax.ShapeDtypeStruct
    room = lambda mib: pltpu.CompilerParams(vmem_limit_bytes=mib * 1024 * 1024)
    cost = lambda flops, size: pl.CostEstimate(flops=flops, bytes_accessed=size, transcendentals=0)

    here = lambda: lax.axis_index("grp") * lax.axis_size("view") + lax.axis_index("view")
    hbm = pl.BlockSpec(memory_space=pltpu.HBM)
    stay = lambda value: pltpu.with_memory_space_constraint(value, pltpu.HBM)

    other = send(flat, swap)
    mine = pl.pallas_call(
        load_kernel,
        out_shape=shape(flat.shape, flat.dtype),
        in_specs=[hbm],
        out_specs=vmem,
        scratch_shapes=[pltpu.SemaphoreType.DMA],
        compiler_params=room(4),
        cost_estimate=cost(1, 1),
        name="load",
    )(stay(flat))
    other, mine = lax.optimization_barrier((other, mine))
    both = pl.pallas_call(
        join_kernel,
        out_shape=shape((piece + 8, plane), jnp.bfloat16),
        in_specs=[vmem] * 2,
        out_specs=vmem,
        compiler_params=room(4),
        name="join",
    )(mine, other)
    got_short = send(both, short)
    got_long = send(both, long)

    sino_shape = shape((channels // 128, views * det_rows, 128), jnp.float32)
    lists_shape = (10, views * slots)
    table_vmem, turned, lists, sino, decay = pl.pallas_call(
        functools.partial(early_kernel, local_blocks=local_blocks, slab=slab, here=here),
        out_shape=(
            shape((plane, tables * channels), table.dtype),
            shape((tables * channels, plane), table.dtype),
            shape(lists_shape, jnp.int32),
            sino_shape,
            sino_shape,
        ),
        in_specs=[vmem] + [hbm] * 6,
        out_specs=(vmem,) * 5,
        scratch_shapes=[
            pltpu.VMEM(measured.shape, measured.dtype),
            pltpu.VMEM((slots, views), jnp.int32),
            pltpu.VMEM((slots, views), jnp.int32),
            pltpu.VMEM((1, views), jnp.int32),
            pltpu.VMEM((1, views), jnp.int32),
            pltpu.VMEM((2 * slots + 2, views), jnp.int32),
            pltpu.SMEM((2 * slots + 2, views), jnp.int32),
            pltpu.SMEM(lists_shape, jnp.int32),
            pltpu.VMEM((piece, tables * channels), jnp.float32),
            pltpu.SemaphoreType.DMA((5 + tables,)),
        ],
        compiler_params=room(16),
        cost_estimate=cost(1, 1),
        name="early",
    )(
        both,
        stay(table),
        stay(measured),
        stay(cover.T),
        stay(offset.T),
        stay(count.reshape(1, views)),
        stay(angle_index.reshape(1, views)),
    )
    got_short, got_long, table_vmem, turned, lists, sino, decay = lax.optimization_barrier(
        (got_short, got_long, table_vmem, turned, lists, sino, decay)
    )
    index = [pltpu.SMEM(lists_shape, jnp.int32)]
    waits = [pltpu.SemaphoreType.DMA]
    rows_of = lambda rows: [pltpu.VMEM((rows, tables * channels), jnp.float32)]

    far = send(jnp.concatenate([got_long, got_short], axis=0), swap)
    far_long, far_short = far[: piece + 8], far[piece + 8 :]
    sino = pl.pallas_call(
        functools.partial(middle_kernel, slab=slab),
        out_shape=sino_shape,
        in_specs=[vmem] * 5,
        out_specs=vmem,
        scratch_shapes=index + rows_of(2 * piece) + waits,
        compiler_params=room(16),
        cost_estimate=cost(1, 1),
        name="middle",
    )(lists, got_long, got_short, table_vmem, sino)
    far_short, far_long, sino = lax.optimization_barrier((far_short, far_long, sino))
    sino, give = pl.pallas_call(
        functools.partial(main_kernel, slab=slab),
        out_shape=(sino_shape, shape((2 * piece, plane), jnp.float32)),
        in_specs=[vmem] * 7,
        out_specs=(vmem, vmem),
        scratch_shapes=index + rows_of(2 * piece) + rows_of(2 * piece) + waits,
        compiler_params=room(16),
        cost_estimate=cost(1, 1),
        name="main",
    )(lists, far_long, far_short, table_vmem, turned, sino, decay)
    taken = send(give, swap)
    keep = pl.pallas_call(
        functools.partial(rest_kernel, group=0, first_row=0, slab=slab),
        out_shape=shape((2 * piece, plane), jnp.float32),
        in_specs=[vmem] * 4,
        out_specs=vmem,
        scratch_shapes=index + rows_of(2 * piece) + waits,
        compiler_params=room(16),
        cost_estimate=cost(1, 1),
        name="rest",
    )(lists, turned, sino, decay)
    taken, keep = lax.optimization_barrier((taken, keep))
    wire = (keep + taken).astype(jnp.bfloat16)
    back_short = send(wire[piece:], short)
    back_long = send(wire[:piece], long)

    home = pl.pallas_call(
        functools.partial(rest_kernel, group=2, first_row=4 * piece, slab=slab),
        out_shape=shape((piece, plane), jnp.float32),
        in_specs=[vmem] * 4,
        out_specs=vmem,
        scratch_shapes=index + rows_of(piece) + waits,
        compiler_params=room(16),
        cost_estimate=cost(1, 1),
        name="home",
    )(lists, turned, sino, decay)
    prior = pl.pallas_call(
        functools.partial(prior_kernel, devices=devices, here=here),
        out_shape=shape((part, plane), jnp.float32),
        in_specs=[vmem] * 6,
        out_specs=vmem,
        compiler_params=room(8),
        cost_estimate=cost(1, 1),
        name="prior",
    )(mine, other, got_long, far_long, got_short, far_short)
    back_short, back_long, home, prior = lax.optimization_barrier(
        (back_short, back_long, home, prior)
    )

    arrived = (back_short.astype(jnp.float32) + back_long.astype(jnp.float32)) + home
    passed = send(arrived[part:], swap)
    out = pl.pallas_call(
        last_kernel,
        out_shape=shape((part, strip, row), jnp.float32),
        in_specs=[vmem] * 3,
        out_specs=vmem,
        compiler_params=room(4),
        name="last",
    )(arrived[:part], passed, prior)
    return out.reshape(volume.shape)


def solution(mesh):
    in_specs = (
        P(AXES, None, None, None),
        P(AXES, None, None, None),
        P(AXES, None, None),
        P(AXES),
        P(AXES, None),
        P(AXES, None),
        P(AXES),
    )
    out_specs = P(AXES, None, None, None)
    return jax.shard_map(shards, mesh=mesh, in_specs=in_specs, out_specs=out_specs, check_vma=False)
```

```python
import functools

import jax
import jax.numpy as jnp
from jax import lax
from jax.experimental import pallas as pl
from jax.experimental.pallas import tpu as pltpu
from jax.sharding import PartitionSpec as P

AXES = ("grp", "view")
APART = 4
DELTA = 0.5
PRIOR_WEIGHT = 2.0


def both_ways(pairs):
    return pairs + [(b, a) for a, b in pairs]


def exchange_pairs(devices):
    chips = devices // 2
    swap = [(i, i ^ 1) for i in range(devices)]
    edge_y = [(i, i + 1) for i in range(0, chips, 2)]
    edge_d = [(i, i + 1) for i in range(1, chips - 1, 2)]
    edge_a = [(i + j, i + j + 2) for i in range(0, chips, 4) for j in (0, 1)]
    edge_b = [(i + j, i + j + 2) for i in range(2, chips - 2, 4) for j in (0, 1)]
    idle = [(0, 1), (chips - 2, chips - 1)]
    on_core = lambda edges, core: [(2 * a + core, 2 * b + core) for a, b in edges]
    last = devices - 1
    ends = [(0, 4), (4, 1), (1, 0), (last - 1, last - 5), (last - 5, last), (last, last - 1)]
    first = both_ways(on_core(edge_a[1:-1], 0) + on_core(edge_d, 1)) + ends
    second = both_ways(on_core(edge_b + idle, 0) + on_core(edge_y, 1))
    return swap, first, second


def load_kernel(source, target, sem):
    copy = pltpu.make_async_copy(source, target, sem)
    copy.start()
    copy.wait()


def join_kernel(own_ref, other_ref, out_ref):
    slices, strip, row = own_ref.shape
    for y in range(strip):
        cols = slice(y * row, (y + 1) * row)
        spare = []
        for k, ref in enumerate((own_ref, other_ref)):
            plane = ref[:, y, :]
            high = plane.astype(jnp.bfloat16)
            out_ref[k * slices : (k + 1) * slices, cols] = high
            rest = plane - high.astype(jnp.float32)
            mid = rest.astype(jnp.bfloat16).astype(jnp.float32)
            low = rest - mid
            for at in (0, slices - 1):
                spare += [mid[at : at + 1], low[at : at + 1]]
        spare = jnp.concatenate(spare, axis=0).astype(jnp.bfloat16)
        out_ref[2 * slices : 2 * slices + 8, cols] = spare


def window_rows(block, position, chips, local_blocks, slab):
    part = local_blocks * slab
    piece = 2 * part
    core = lax.rem(position, 2)
    chip = position // 2
    owner = block // local_blocks
    owner_core = lax.rem(owner, 2)
    delta = owner // 2 - chip
    flag = lambda what: jnp.where(what, 1, 0)
    up = flag(delta > 0)
    nearer = jnp.abs(delta) == 1
    is_y = flag(up == 1 - lax.rem(chip, 2))
    is_a = flag(up == flag(lax.rem(chip, 4) < 2))
    second = jnp.where(nearer, is_y, 1 - is_a)
    via = flag(nearer)
    end = flag((chip == 0) | (chip == chips - 1))
    held = jnp.where(nearer, 1, is_a * end)
    away = (2 * jnp.abs(held - core) + second) * piece + jnp.abs(owner_core - via) * part
    here = 4 * piece + jnp.abs(owner_core - core) * part
    return jnp.where(delta == 0, here, away) + lax.rem(block, local_blocks) * slab


class Pairs:
    FIELDS = 5
    GROUPS = 3

    def __init__(self, ref):
        self.ref = ref

    def each(self, group, do):
        def body(i, carry):
            do(*(self.ref[self.FIELDS * group + k, i] for k in range(4)))
            return carry

        lax.fori_loop(0, self.ref[self.FIELDS * self.GROUPS, group], body, 0)

    def apart(self, group):
        return self.ref[self.FIELDS * self.GROUPS + 1, group]

    def target(self, group, i):
        return self.ref[self.FIELDS * group + 4, i]


def list_pairs(scal, lists, seen, near_rows, det_rows, tables, slab):
    slots = (scal.shape[0] - 2) // 2
    fields, groups = Pairs.FIELDS, Pairs.GROUPS

    def clear(i, carry):
        seen[i] = jnp.int32(0)
        return carry

    lax.fori_loop(0, seen.shape[0], clear, 0)
    for k in range(groups):
        lists[fields * groups, k] = jnp.int32(0)
        lists[fields * groups + 1, k] = jnp.int32(0)

    def body(view, carry):
        count = scal[2 * slots, view]
        table = scal[2 * slots + 1, view]
        for slot in range(slots):

            @pl.when(slot < count)
            def _():
                row = scal[slot, view]
                group = jnp.minimum(row // near_rows, groups - 1)
                local = row - group * near_rows
                at = lists[fields * groups, group]
                spare = lists[fields * groups + 1, group]
                first = fields * group
                bucket = (row // slab) * tables + table
                taken = seen[bucket]
                rows = jnp.where(group == groups - 1, near_rows // 2, near_rows)
                lists[first, at] = view * det_rows + scal[slots + slot, view]
                lists[first + 1, at] = table
                lists[first + 2, at] = local
                lists[first + 3, at] = jnp.where(taken == 0, local, rows + spare * slab)
                lists[first + 4, spare] = local
                lists[fields * groups, group] = at + 1
                lists[fields * groups + 1, group] = spare + taken
                seen[bucket] = jnp.int32(1)

        return carry

    lax.fori_loop(0, scal.shape[1], body, 0)


def place(pairs, group, sino, proj, slab):
    width = sino.shape[0] * 128

    def add(target, table, local, dest):
        source = pl.ds(pl.multiple_of(local, slab), slab)
        for tile in range(sino.shape[0]):
            cols = pl.ds(pl.multiple_of(table * width + tile * 128, 128), 128)
            sino[tile, pl.ds(target, slab), :] += proj[source, cols]

    pairs.each(group, add)


def clear_rows(picked, rows):
    picked[0:rows, :] = jnp.zeros((rows, picked.shape[1]), picked.dtype)


def gather(pairs, group, sino, decay, picked, static_rows, slab):
    width = sino.shape[0] * 128
    chunk = APART * slab

    def clear(i, carry):
        here = pl.ds(pl.multiple_of(static_rows + i * chunk, chunk), chunk)
        picked[here, :] = jnp.zeros((chunk, picked.shape[1]), picked.dtype)
        return carry

    lax.fori_loop(0, (pairs.apart(group) - 1) // APART, clear, 0)

    def take(source, table, local, dest):
        target = pl.ds(pl.multiple_of(dest, slab), slab)
        here = pl.ds(source, slab)
        for tile in range(sino.shape[0]):
            cols = pl.ds(pl.multiple_of(table * width + tile * 128, 128), 128)
            value = decay[tile, here, :] * sino[tile, here, :]
            picked[target, cols] = value.astype(jnp.bfloat16)

    pairs.each(group, take)


def back_project(pairs, group, picked, turned_ref, extra, out_ref, slab):
    rows = out_ref.shape[0]
    chunk = APART * slab
    apart = pairs.apart(group)

    def add(i, carry):
        target = pl.ds(pl.multiple_of(pairs.target(group, i), slab), slab)
        source = pl.ds(pl.multiple_of(lax.rem(i, APART) * slab, slab), slab)
        out_ref[target, :] += extra[source, :]
        return carry

    got = jnp.dot(picked[0 : rows + chunk, :], turned_ref[...], preferred_element_type=jnp.float32)
    out_ref[...] = got[0:rows]
    extra[...] = got[rows:]
    lax.fori_loop(0, jnp.minimum(apart, APART), add, 0)

    def further(c, carry):
        here = pl.ds(pl.multiple_of(rows + c * chunk, chunk), chunk)
        extra[...] = jnp.dot(picked[here, :], turned_ref[...], preferred_element_type=jnp.float32)
        lax.fori_loop(c * APART, jnp.minimum(apart, (c + 1) * APART), add, 0)
        return carry

    lax.fori_loop(1, (apart + APART - 1) // APART, further, 0)


def early_kernel(
    both_ref,
    table_hbm,
    measured_hbm,
    cover_hbm,
    offset_hbm,
    count_hbm,
    angle_hbm,
    table_ref,
    turned_ref,
    lists_ref,
    sino_ref,
    decay_ref,
    measured,
    cover,
    offset,
    count,
    angle,
    index,
    scal,
    lists,
    seen,
    proj,
    sems,
    *,
    chips,
    local_blocks,
    slab,
    here,
):
    views, det_rows, channels = measured.shape
    slots = cover.shape[0]
    tables = table_hbm.shape[0]
    piece = both_ref.shape[0] - 8
    small = [(cover_hbm, cover), (offset_hbm, offset), (count_hbm, count), (angle_hbm, angle)]
    copies = [pltpu.make_async_copy(a, b, sems.at[i]) for i, (a, b) in enumerate(small)]
    copies.append(pltpu.make_async_copy(measured_hbm, measured, sems.at[4]))
    for table in range(tables):
        to = table_ref.at[:, table * channels : (table + 1) * channels]
        copies.append(pltpu.make_async_copy(table_hbm.at[table], to, sems.at[5 + table]))
    for copy in copies:
        copy.start()
    for copy in copies[:4]:
        copy.wait()
    index[0:slots, :] = window_rows(cover[...], here(), chips, local_blocks, slab)
    index[slots : 2 * slots, :] = offset[...]
    index[2 * slots : 2 * slots + 1, :] = count[...]
    index[2 * slots + 1 : 2 * slots + 2, :] = angle[...]
    load = fetch(index, scal, sems.at[0])
    copies[4].wait()

    def fade(view, carry):
        rows = pl.ds(pl.multiple_of(view * det_rows, det_rows), det_rows)
        for tile in range(sino_ref.shape[0]):
            value = measured[view, :, tile * 128 : (tile + 1) * 128].astype(jnp.float32)
            decay_ref[tile, rows, :] = jnp.exp(-value)
            sino_ref[tile, rows, :] = -value
        return carry

    lax.fori_loop(0, views, fade, 0)
    load.wait()
    list_pairs(scal, lists, seen, 2 * piece, det_rows, tables, slab)
    save = fetch(lists, lists_ref, sems.at[0])
    for table in range(tables):
        copies[5 + table].wait()
        cols = slice(table * channels, (table + 1) * channels)
        turned_ref[cols, :] = table_ref[:, cols].T
    proj[...] = jnp.dot(both_ref[0:piece, :], table_ref[...], preferred_element_type=jnp.float32)
    place(Pairs(lists), 2, sino_ref, proj, slab)
    save.wait()


def fetch(source, target, sem):
    load = pltpu.make_async_copy(source, target, sem)
    load.start()
    return load


def project(load, lists, group, window, table_ref, begun_ref, sino_ref, proj, slab):
    sino_ref[...] = begun_ref[...]
    proj[...] = jnp.dot(window, table_ref[...], preferred_element_type=jnp.float32)
    load.wait()
    place(Pairs(lists), group, sino_ref, proj, slab)


def middle_kernel(
    lists_ref, first_ref, second_ref, table_ref, begun_ref, sino_ref, lists, proj, sem, *, slab
):
    load = fetch(lists_ref, lists, sem)
    piece = first_ref.shape[0] - 8
    window = jnp.concatenate([first_ref[0:piece, :], second_ref[0:piece, :]], axis=0)
    project(load, lists, 0, window, table_ref, begun_ref, sino_ref, proj, slab)


def main_kernel(
    lists_ref,
    far_ref,
    table_ref,
    turned_ref,
    begun_ref,
    decay_ref,
    sino_ref,
    give_ref,
    lists,
    proj,
    picked,
    extra,
    sem,
    *,
    slab,
):
    load = fetch(lists_ref, lists, sem)
    static_rows = give_ref.shape[0] + extra.shape[0]
    clear_rows(picked, static_rows)
    step = far_ref.shape[0] // 2
    window = jnp.concatenate([far_ref[0 : step - 8, :], far_ref[step : 2 * step - 8, :]], axis=0)
    project(load, lists, 1, window, table_ref, begun_ref, sino_ref, proj, slab)
    pairs = Pairs(lists)
    gather(pairs, 1, sino_ref, decay_ref, picked, static_rows, slab)
    back_project(pairs, 1, picked, turned_ref, extra, give_ref, slab)


def rest_kernel(
    lists_ref, turned_ref, sino_ref, decay_ref, out_ref, lists, picked, extra, sem, *, group, slab
):
    load = fetch(lists_ref, lists, sem)
    static_rows = out_ref.shape[0] + extra.shape[0]
    clear_rows(picked, static_rows)
    load.wait()
    pairs = Pairs(lists)
    gather(pairs, group, sino_ref, decay_ref, picked, static_rows, slab)
    back_project(pairs, group, picked, turned_ref, extra, out_ref, slab)


def prior_kernel(
    vol_ref, other_ref, first_ref, second_ref, far_ref, out_ref, *, devices, here
):
    slices, strip, row = vol_ref.shape
    part = slices
    piece = 2 * part
    position = here()
    core = lax.rem(position, 2)
    odd = lax.rem(position // 2, 2)

    def chip_slice(ref, which, via, base=0):
        sub = which ^ via
        at = base + sub * part + (part - 1) * which
        tail = base + piece + 4 * sub + 2 * which
        whole = ref[at : at + 1, :].astype(jnp.float32)
        more = ref[tail : tail + 2, :].astype(jnp.float32)
        whole = whole + (more[0:1] + more[1:2])
        return lambda y: whole[:, y * row : (y + 1) * row]

    def core_slice(which):
        at = (part - 1) * which
        return lambda y: other_ref[at : at + 1, y, :]

    def emit(low, high):
        for y in range(strip):
            cols = slice(y * row, (y + 1) * row)
            here = vol_ref[:, y, :]
            below = jnp.concatenate([low(y), here[:-1]], axis=0)
            above = jnp.concatenate([here[1:], high(y)], axis=0)
            level = lax.broadcasted_iota(jnp.int32, here.shape, 0)
            down = jnp.clip(here - below, -DELTA, DELTA)
            total = jnp.where((level > 0) | (position > 0), down, 0.0)
            up = jnp.clip(here - above, -DELTA, DELTA)
            total += jnp.where((level < slices - 1) | (position < devices - 1), up, 0.0)
            if y > 0:
                total += jnp.clip(here - vol_ref[:, y - 1, :], -DELTA, DELTA)
            if y + 1 < strip:
                total += jnp.clip(here - vol_ref[:, y + 1, :], -DELTA, DELTA)
            lane = lax.broadcasted_iota(jnp.int32, here.shape, 1)
            left = jnp.clip(here - pltpu.roll(here, 1, 1), -DELTA, DELTA)
            total += jnp.where(lane > 0, left, 0.0)
            right = jnp.clip(here - pltpu.roll(here, row - 1, 1), -DELTA, DELTA)
            total += jnp.where(lane < row - 1, right, 0.0)
            out_ref[:, cols] = PRIOR_WEIGHT * total

    @pl.when((core == 0) & (odd == 0))
    def _():
        emit(chip_slice(far_ref, 1, 1), core_slice(0))

    @pl.when((core == 0) & (odd == 1))
    def _():
        emit(chip_slice(far_ref, 1, 1, piece + 8), core_slice(0))

    @pl.when((core == 1) & (odd == 0))
    def _():
        emit(core_slice(1), chip_slice(second_ref, 0, 1))

    @pl.when((core == 1) & (odd == 1))
    def _():
        emit(core_slice(1), chip_slice(first_ref, 0, 1))


def last_kernel(arrived_ref, passed_ref, prior_ref, out_ref):
    part, strip, row = out_ref.shape
    for y in range(strip):
        cols = slice(y * row, (y + 1) * row)
        out_ref[:, y, :] = (arrived_ref[:, cols] + passed_ref[:, cols]) + prior_ref[:, cols]


def shards(volume, footprint, measured, angle_index, cover, offset, count):
    local_blocks, slab, strip, row = volume.shape
    views, det_rows, channels = measured.shape
    tables = footprint.shape[0]
    slots = cover.shape[1]
    plane = strip * row
    devices = lax.axis_size(AXES)
    position = lax.axis_index(AXES)
    swap, first, second = exchange_pairs(devices)
    back = lambda pairs: [(b, a) for a, b in pairs]
    send = lambda value, pairs: lax.ppermute(value, AXES, pairs)
    part = local_blocks * slab
    piece = 2 * part
    flat = volume.reshape(part, strip, row)
    table = footprint.reshape(tables, plane, channels)
    vmem = pl.BlockSpec(memory_space=pltpu.VMEM)
    smem = pl.BlockSpec(memory_space=pltpu.SMEM)
    shape = jax.ShapeDtypeStruct
    room = lambda mib: pltpu.CompilerParams(vmem_limit_bytes=mib * 1024 * 1024)
    cost = lambda flops, size: pl.CostEstimate(flops=flops, bytes_accessed=size, transcendentals=0)

    here = lambda: lax.axis_index("grp") * lax.axis_size("view") + lax.axis_index("view")
    hbm = pl.BlockSpec(memory_space=pltpu.HBM)
    stay = lambda value: pltpu.with_memory_space_constraint(value, pltpu.HBM)

    other = send(flat, swap)
    mine = pl.pallas_call(
        load_kernel,
        out_shape=shape(flat.shape, flat.dtype),
        in_specs=[hbm],
        out_specs=vmem,
        scratch_shapes=[pltpu.SemaphoreType.DMA],
        compiler_params=room(4),
        cost_estimate=cost(1, 1),
        name="load",
    )(stay(flat))
    other, mine = lax.optimization_barrier((other, mine))
    both = pl.pallas_call(
        join_kernel,
        out_shape=shape((piece + 8, plane), jnp.bfloat16),
        in_specs=[vmem] * 2,
        out_specs=vmem,
        compiler_params=room(4),
        name="join",
    )(mine, other)
    got_second = send(both, second)
    got_first = send(both, first)

    sino_shape = shape((channels // 128, views * det_rows, 128), jnp.float32)
    lists_shape = (Pairs.FIELDS * Pairs.GROUPS + 2, views * slots)
    table_vmem, turned, lists, sino, decay = pl.pallas_call(
        functools.partial(
            early_kernel, chips=devices // 2, local_blocks=local_blocks, slab=slab, here=here
        ),
        out_shape=(
            shape((plane, tables * channels), table.dtype),
            shape((tables * channels, plane), table.dtype),
            shape(lists_shape, jnp.int32),
            sino_shape,
            sino_shape,
        ),
        in_specs=[vmem] + [hbm] * 6,
        out_specs=(vmem,) * 5,
        scratch_shapes=[
            pltpu.VMEM(measured.shape, measured.dtype),
            pltpu.VMEM((slots, views), jnp.int32),
            pltpu.VMEM((slots, views), jnp.int32),
            pltpu.VMEM((1, views), jnp.int32),
            pltpu.VMEM((1, views), jnp.int32),
            pltpu.VMEM((2 * slots + 2, views), jnp.int32),
            pltpu.SMEM((2 * slots + 2, views), jnp.int32),
            pltpu.SMEM(lists_shape, jnp.int32),
            pltpu.SMEM((5 * piece // slab * tables,), jnp.int32),
            pltpu.VMEM((piece, tables * channels), jnp.float32),
            pltpu.SemaphoreType.DMA((5 + tables,)),
        ],
        compiler_params=room(16),
        cost_estimate=cost(1, 1),
        name="early",
    )(
        both,
        stay(table),
        stay(measured),
        stay(cover.T),
        stay(offset.T),
        stay(count.reshape(1, views)),
        stay(angle_index.reshape(1, views)),
    )
    got_second, got_first, table_vmem, turned, lists, sino, decay = lax.optimization_barrier(
        (got_second, got_first, table_vmem, turned, lists, sino, decay)
    )
    index = [pltpu.SMEM(lists_shape, jnp.int32)]
    waits = [pltpu.SemaphoreType.DMA]
    rows_of = lambda rows: [pltpu.VMEM((rows, tables * channels), jnp.float32)]
    picks_of = lambda rows: [
        pltpu.VMEM((rows + (views * slots + APART) * slab, tables * channels), jnp.bfloat16),
        pltpu.VMEM((APART * slab, plane), jnp.float32),
    ]

    far = send(jnp.concatenate([got_first, got_second], axis=0), swap)
    sino = pl.pallas_call(
        functools.partial(middle_kernel, slab=slab),
        out_shape=sino_shape,
        in_specs=[vmem] * 5,
        out_specs=vmem,
        scratch_shapes=index + rows_of(2 * piece) + waits,
        compiler_params=room(16),
        cost_estimate=cost(1, 1),
        name="middle",
    )(lists, got_first, got_second, table_vmem, sino)
    far, sino = lax.optimization_barrier((far, sino))
    sino, give = pl.pallas_call(
        functools.partial(main_kernel, slab=slab),
        out_shape=(sino_shape, shape((2 * piece, plane), jnp.float32)),
        in_specs=[vmem] * 6,
        out_specs=(vmem, vmem),
        scratch_shapes=index + rows_of(2 * piece) + picks_of(2 * piece) + waits,
        compiler_params=room(16),
        cost_estimate=cost(1, 1),
        name="main",
    )(lists, far, table_vmem, turned, sino, decay)
    taken = send(give, swap)
    keep = pl.pallas_call(
        functools.partial(rest_kernel, group=0, slab=slab),
        out_shape=shape((2 * piece, plane), jnp.float32),
        in_specs=[vmem] * 4,
        out_specs=vmem,
        scratch_shapes=index + picks_of(2 * piece) + waits,
        compiler_params=room(16),
        cost_estimate=cost(1, 1),
        name="rest",
    )(lists, turned, sino, decay)
    taken, keep = lax.optimization_barrier((taken, keep))
    wire = (keep + taken).astype(jnp.bfloat16)
    back_second = send(wire[piece:], back(second))
    back_first = send(wire[:piece], back(first))

    home = pl.pallas_call(
        functools.partial(rest_kernel, group=2, slab=slab),
        out_shape=shape((piece, plane), jnp.float32),
        in_specs=[vmem] * 4,
        out_specs=vmem,
        scratch_shapes=index + picks_of(piece) + waits,
        compiler_params=room(16),
        cost_estimate=cost(1, 1),
        name="home",
    )(lists, turned, sino, decay)
    prior = pl.pallas_call(
        functools.partial(prior_kernel, devices=devices, here=here),
        out_shape=shape((part, plane), jnp.float32),
        in_specs=[vmem] * 5,
        out_specs=vmem,
        compiler_params=room(8),
        cost_estimate=cost(1, 1),
        name="prior",
    )(mine, other, got_first, got_second, far)
    back_second, back_first, home, prior = lax.optimization_barrier(
        (back_second, back_first, home, prior)
    )

    arrived = (back_second.astype(jnp.float32) + back_first.astype(jnp.float32)) + home
    passed = send(arrived[part:], swap)
    out = pl.pallas_call(
        last_kernel,
        out_shape=shape((part, strip, row), jnp.float32),
        in_specs=[vmem] * 3,
        out_specs=vmem,
        compiler_params=room(4),
        name="last",
    )(arrived[:part], passed, prior)
    return out.reshape(volume.shape)


def solution(mesh):
    in_specs = (
        P(AXES, None, None, None),
        P(AXES, None, None, None),
        P(AXES, None, None),
        P(AXES),
        P(AXES, None),
        P(AXES, None),
        P(AXES),
    )
    out_specs = P(AXES, None, None, None)
    return jax.shard_map(shards, mesh=mesh, in_specs=in_specs, out_specs=out_specs, check_vma=False)
```

```python
import functools

import jax
import jax.numpy as jnp
from jax import lax
from jax.experimental import pallas as pl
from jax.experimental.pallas import tpu as pltpu
from jax.sharding import PartitionSpec as P

AXES = ("grp", "view")
STATIC = 12
MORE = 4
DELTA = 0.5
PRIOR_WEIGHT = 2.0


def both_ways(pairs):
    return pairs + [(b, a) for a, b in pairs]


def exchange_pairs(devices):
    chips = devices // 2
    swap = [(i, i ^ 1) for i in range(devices)]
    edge_y = [(i, i + 1) for i in range(0, chips, 2)]
    edge_d = [(i, i + 1) for i in range(1, chips - 1, 2)]
    edge_a = [(i + j, i + j + 2) for i in range(0, chips, 4) for j in (0, 1)]
    edge_b = [(i + j, i + j + 2) for i in range(2, chips - 2, 4) for j in (0, 1)]
    idle = [(0, 1), (chips - 2, chips - 1)]
    on_core = lambda edges, core: [(2 * a + core, 2 * b + core) for a, b in edges]
    last = devices - 1
    ends = [(0, 4), (4, 1), (1, 0), (last - 1, last - 5), (last - 5, last), (last, last - 1)]
    first = both_ways(on_core(edge_a[1:-1], 0) + on_core(edge_d, 1)) + ends
    second = both_ways(on_core(edge_b + idle, 0) + on_core(edge_y, 1))
    return swap, first, second


def pack(plane, out_ref, first_row, cols):
    high = plane.astype(jnp.bfloat16)
    out_ref[first_row : first_row + plane.shape[0], cols] = high
    ends = []
    for at in (0, plane.shape[0] - 1):
        rest = plane[at : at + 1] - high[at : at + 1].astype(jnp.float32)
        mid = rest.astype(jnp.bfloat16).astype(jnp.float32)
        ends += [mid, rest - mid]
    return ends


def load_kernel(source, target, own_ref, sem):
    copy = pltpu.make_async_copy(source, target, sem)
    copy.start()
    copy.wait()
    slices, strip, row = target.shape
    for y in range(strip):
        cols = slice(y * row, (y + 1) * row)
        ends = pack(target[:, y, :], own_ref, 0, cols)
        own_ref[slices : slices + 8, cols] = jnp.concatenate(ends + ends, axis=0).astype(
            jnp.bfloat16
        )


def join_kernel(own_ref, other_ref, out_ref):
    slices, strip, row = other_ref.shape
    out_ref[0:slices, :] = own_ref[0:slices, :]
    mine = own_ref[slices : slices + 8, :].astype(jnp.float32)
    for y in range(strip):
        cols = slice(y * row, (y + 1) * row)
        ends = pack(other_ref[:, y, :], out_ref, slices, cols)
        spare = jnp.concatenate([mine[0:4, cols]] + ends, axis=0)
        out_ref[2 * slices : 2 * slices + 8, cols] = spare.astype(jnp.bfloat16)


def window_rows(block, position, chips, local_blocks, slab):
    part = local_blocks * slab
    piece = 2 * part
    core = lax.rem(position, 2)
    chip = position // 2
    owner = block // local_blocks
    owner_core = lax.rem(owner, 2)
    delta = owner // 2 - chip
    flag = lambda what: jnp.where(what, 1, 0)
    up = flag(delta > 0)
    nearer = jnp.abs(delta) == 1
    is_y = flag(up == 1 - lax.rem(chip, 2))
    is_a = flag(up == flag(lax.rem(chip, 4) < 2))
    second = jnp.where(nearer, is_y, 1 - is_a)
    via = flag(nearer)
    end = flag((chip == 0) | (chip == chips - 1))
    held = jnp.where(nearer, 1, is_a * end)
    away = (2 * jnp.abs(held - core) + second) * piece + jnp.abs(owner_core - via) * part
    here = 4 * piece + jnp.abs(owner_core - core) * part
    return jnp.where(delta == 0, here, away) + lax.rem(block, local_blocks) * slab


class Pairs:
    FIELDS = 5
    GROUPS = 3

    def __init__(self, ref):
        self.ref = ref

    def each(self, group, do):
        def body(i, carry):
            do(*(self.ref[self.FIELDS * group + k, i] for k in range(4)))
            return carry

        lax.fori_loop(0, self.ref[self.FIELDS * self.GROUPS, group], body, 0)

    def gathered(self, group):
        return self.ref[self.FIELDS * self.GROUPS + 1, group]

    def target(self, group, i):
        return self.ref[self.FIELDS * group + 4, i]


def list_pairs(scal, lists, seen, height, held, near_rows, det_rows, tables, slab):
    slots = (scal.shape[0] - 2) // 2
    most = held.shape[1]
    fields, groups = Pairs.FIELDS, Pairs.GROUPS

    def clear(i, carry):
        height[i] = jnp.int32(0)
        for table in range(tables):
            seen[i, table] = jnp.int32(0)
        return carry

    lax.fori_loop(0, height.shape[0], clear, 0)
    for k in range(groups):
        lists[fields * groups, k] = jnp.int32(0)
        lists[fields * groups + 1, k] = jnp.int32(0)

    def body(view, carry):
        count = scal[2 * slots, view]
        table = scal[2 * slots + 1, view]
        for slot in range(slots):

            @pl.when(slot < count)
            def _():
                row = scal[slot, view]
                block = row // slab
                group = jnp.minimum(row // near_rows, groups - 1)
                local = row - group * near_rows
                first = fields * group
                at = lists[fields * groups, group]
                used = lists[fields * groups + 1, group]
                rank = seen[block, table]
                top = height[block]
                fresh = rank >= top
                mine = jnp.where(fresh, used, held[block, rank])
                held[block, rank] = mine
                seen[block, table] = rank + 1
                height[block] = jnp.where(fresh, rank + 1, top)
                lists[first, at] = view * det_rows + scal[slots + slot, view]
                lists[first + 1, at] = table
                lists[first + 2, at] = local
                lists[first + 3, at] = mine * slab
                lists[first + 4, mine] = local
                lists[fields * groups, group] = at + 1
                lists[fields * groups + 1, group] = used + jnp.where(fresh, 1, 0)

        return carry

    lax.fori_loop(0, scal.shape[1], body, 0)


def place(pairs, group, sino, proj, slab):
    width = sino.shape[0] * 128

    def add(target, table, local, dest):
        source = pl.ds(pl.multiple_of(local, slab), slab)
        for tile in range(sino.shape[0]):
            cols = pl.ds(pl.multiple_of(table * width + tile * 128, 128), 128)
            sino[tile, pl.ds(target, slab), :] += proj[source, cols]

    pairs.each(group, add)


def clear_rows(picked, static_rows):
    picked[0:static_rows, :] = jnp.zeros((static_rows, picked.shape[1]), picked.dtype)


def gather(pairs, group, sino, decay, picked, static_rows, slab):
    width = sino.shape[0] * 128
    chunk = MORE * slab

    def clear(i, carry):
        here = pl.ds(pl.multiple_of(static_rows + i * chunk, chunk), chunk)
        picked[here, :] = jnp.zeros((chunk, picked.shape[1]), picked.dtype)
        return carry

    more = pairs.gathered(group) * slab - static_rows
    lax.fori_loop(0, (more + chunk - 1) // chunk, clear, 0)

    def take(source, table, local, dest):
        target = pl.ds(pl.multiple_of(dest, slab), slab)
        here = pl.ds(source, slab)
        for tile in range(sino.shape[0]):
            cols = pl.ds(pl.multiple_of(table * width + tile * 128, 128), 128)
            value = decay[tile, here, :] * sino[tile, here, :]
            picked[target, cols] = value.astype(jnp.bfloat16)

    pairs.each(group, take)


def back_project(pairs, group, picked, turned_ref, spread, out_ref, slab):
    static_rows = spread.shape[0]
    static = static_rows // slab
    blocks = pairs.gathered(group)
    out_ref[...] = jnp.zeros_like(out_ref)

    def add_from(begin):
        def add(i, carry):
            target = pl.ds(pl.multiple_of(pairs.target(group, i), slab), slab)
            source = pl.ds(pl.multiple_of((i - begin) * slab, slab), slab)
            out_ref[target, :] += spread[source, :]
            return carry

        return add

    spread[...] = jnp.dot(
        picked[0:static_rows, :], turned_ref[...], preferred_element_type=jnp.float32
    )
    lax.fori_loop(0, jnp.minimum(blocks, static), add_from(0), 0)

    def further(c, carry):
        begin = static + c * MORE
        here = pl.ds(pl.multiple_of(begin * slab, MORE * slab), MORE * slab)
        spread[0 : MORE * slab, :] = jnp.dot(
            picked[here, :], turned_ref[...], preferred_element_type=jnp.float32
        )
        lax.fori_loop(begin, jnp.minimum(blocks, begin + MORE), add_from(begin), 0)
        return carry

    lax.fori_loop(0, (blocks - static + MORE - 1) // MORE, further, 0)


def early_kernel(
    both_ref,
    table_hbm,
    measured_hbm,
    cover_hbm,
    offset_hbm,
    count_hbm,
    angle_hbm,
    table_ref,
    turned_ref,
    lists_ref,
    sino_ref,
    decay_ref,
    measured,
    cover,
    offset,
    count,
    angle,
    index,
    scal,
    lists,
    seen,
    height,
    held,
    proj,
    sems,
    *,
    chips,
    local_blocks,
    slab,
    here,
):
    views, det_rows, channels = measured.shape
    slots = cover.shape[0]
    tables = table_hbm.shape[0]
    piece = both_ref.shape[0] - 8
    small = [(cover_hbm, cover), (offset_hbm, offset), (count_hbm, count), (angle_hbm, angle)]
    copies = [pltpu.make_async_copy(a, b, sems.at[i]) for i, (a, b) in enumerate(small)]
    copies.append(pltpu.make_async_copy(measured_hbm, measured, sems.at[4]))
    for table in range(tables):
        to = table_ref.at[:, table * channels : (table + 1) * channels]
        copies.append(pltpu.make_async_copy(table_hbm.at[table], to, sems.at[5 + table]))
    for copy in copies:
        copy.start()
    for copy in copies[:4]:
        copy.wait()
    index[0:slots, :] = window_rows(cover[...], here(), chips, local_blocks, slab)
    index[slots : 2 * slots, :] = offset[...]
    index[2 * slots : 2 * slots + 1, :] = count[...]
    index[2 * slots + 1 : 2 * slots + 2, :] = angle[...]
    load = fetch(index, scal, sems.at[0])
    copies[4].wait()

    def fade(view, carry):
        rows = pl.ds(pl.multiple_of(view * det_rows, det_rows), det_rows)
        for tile in range(sino_ref.shape[0]):
            value = measured[view, :, tile * 128 : (tile + 1) * 128].astype(jnp.float32)
            decay_ref[tile, rows, :] = jnp.exp(-value)
            sino_ref[tile, rows, :] = -value
        return carry

    lax.fori_loop(0, views, fade, 0)
    load.wait()
    list_pairs(scal, lists, seen, height, held, 2 * piece, det_rows, tables, slab)
    save = fetch(lists, lists_ref, sems.at[0])
    for table in range(tables):
        copies[5 + table].wait()
        cols = slice(table * channels, (table + 1) * channels)
        turned_ref[cols, :] = table_ref[:, cols].T
    proj[...] = jnp.dot(both_ref[0:piece, :], table_ref[...], preferred_element_type=jnp.float32)
    place(Pairs(lists), 2, sino_ref, proj, slab)
    save.wait()


def fetch(source, target, sem):
    load = pltpu.make_async_copy(source, target, sem)
    load.start()
    return load


def project(load, lists, group, window, table_ref, begun_ref, sino_ref, proj, slab):
    sino_ref[...] = begun_ref[...]
    proj[...] = jnp.dot(window, table_ref[...], preferred_element_type=jnp.float32)
    load.wait()
    place(Pairs(lists), group, sino_ref, proj, slab)


def middle_kernel(
    lists_ref, first_ref, second_ref, table_ref, begun_ref, sino_ref, lists, proj, sem, *, slab
):
    load = fetch(lists_ref, lists, sem)
    piece = first_ref.shape[0] - 8
    window = jnp.concatenate([first_ref[0:piece, :], second_ref[0:piece, :]], axis=0)
    project(load, lists, 0, window, table_ref, begun_ref, sino_ref, proj, slab)


def main_kernel(
    lists_ref,
    far_ref,
    table_ref,
    turned_ref,
    begun_ref,
    decay_ref,
    sino_ref,
    give_ref,
    lists,
    proj,
    picked,
    spread,
    sem,
    *,
    slab,
):
    load = fetch(lists_ref, lists, sem)
    clear_rows(picked, spread.shape[0])
    step = far_ref.shape[0] // 2
    window = jnp.concatenate([far_ref[0 : step - 8, :], far_ref[step : 2 * step - 8, :]], axis=0)
    project(load, lists, 1, window, table_ref, begun_ref, sino_ref, proj, slab)
    pairs = Pairs(lists)
    gather(pairs, 1, sino_ref, decay_ref, picked, spread.shape[0], slab)
    back_project(pairs, 1, picked, turned_ref, spread, give_ref, slab)


def rest_kernel(
    lists_ref, turned_ref, sino_ref, decay_ref, out_ref, lists, picked, spread, sem, *, group, slab
):
    load = fetch(lists_ref, lists, sem)
    clear_rows(picked, spread.shape[0])
    load.wait()
    pairs = Pairs(lists)
    gather(pairs, group, sino_ref, decay_ref, picked, spread.shape[0], slab)
    back_project(pairs, group, picked, turned_ref, spread, out_ref, slab)


def prior_kernel(
    vol_ref, other_ref, first_ref, second_ref, far_ref, out_ref, *, devices, here
):
    slices, strip, row = vol_ref.shape
    part = slices
    piece = 2 * part
    position = here()
    core = lax.rem(position, 2)
    odd = lax.rem(position // 2, 2)

    def chip_slice(ref, which, via, base=0):
        sub = which ^ via
        at = base + sub * part + (part - 1) * which
        tail = base + piece + 4 * sub + 2 * which
        whole = ref[at : at + 1, :].astype(jnp.float32)
        more = ref[tail : tail + 2, :].astype(jnp.float32)
        whole = whole + (more[0:1] + more[1:2])
        return lambda y: whole[:, y * row : (y + 1) * row]

    def core_slice(which):
        at = (part - 1) * which
        return lambda y: other_ref[at : at + 1, y, :]

    def emit(low, high):
        for y in range(strip):
            cols = slice(y * row, (y + 1) * row)
            here = vol_ref[:, y, :]
            below = jnp.concatenate([low(y), here[:-1]], axis=0)
            above = jnp.concatenate([here[1:], high(y)], axis=0)
            level = lax.broadcasted_iota(jnp.int32, here.shape, 0)
            down = jnp.clip(here - below, -DELTA, DELTA)
            total = jnp.where((level > 0) | (position > 0), down, 0.0)
            up = jnp.clip(here - above, -DELTA, DELTA)
            total += jnp.where((level < slices - 1) | (position < devices - 1), up, 0.0)
            if y > 0:
                total += jnp.clip(here - vol_ref[:, y - 1, :], -DELTA, DELTA)
            if y + 1 < strip:
                total += jnp.clip(here - vol_ref[:, y + 1, :], -DELTA, DELTA)
            lane = lax.broadcasted_iota(jnp.int32, here.shape, 1)
            left = jnp.clip(here - pltpu.roll(here, 1, 1), -DELTA, DELTA)
            total += jnp.where(lane > 0, left, 0.0)
            right = jnp.clip(here - pltpu.roll(here, row - 1, 1), -DELTA, DELTA)
            total += jnp.where(lane < row - 1, right, 0.0)
            out_ref[:, cols] = PRIOR_WEIGHT * total

    @pl.when((core == 0) & (odd == 0))
    def _():
        emit(chip_slice(far_ref, 1, 1), core_slice(0))

    @pl.when((core == 0) & (odd == 1))
    def _():
        emit(chip_slice(far_ref, 1, 1, piece + 8), core_slice(0))

    @pl.when((core == 1) & (odd == 0))
    def _():
        emit(core_slice(1), chip_slice(second_ref, 0, 1))

    @pl.when((core == 1) & (odd == 1))
    def _():
        emit(core_slice(1), chip_slice(first_ref, 0, 1))


def last_kernel(arrived_ref, passed_ref, prior_ref, out_ref):
    part, strip, row = out_ref.shape
    for y in range(strip):
        cols = slice(y * row, (y + 1) * row)
        out_ref[:, y, :] = (arrived_ref[:, cols] + passed_ref[:, cols]) + prior_ref[:, cols]


def shards(volume, footprint, measured, angle_index, cover, offset, count):
    local_blocks, slab, strip, row = volume.shape
    views, det_rows, channels = measured.shape
    tables = footprint.shape[0]
    slots = cover.shape[1]
    plane = strip * row
    devices = lax.axis_size(AXES)
    position = lax.axis_index(AXES)
    swap, first, second = exchange_pairs(devices)
    back = lambda pairs: [(b, a) for a, b in pairs]
    send = lambda value, pairs: lax.ppermute(value, AXES, pairs)
    part = local_blocks * slab
    piece = 2 * part
    flat = volume.reshape(part, strip, row)
    table = footprint.reshape(tables, plane, channels)
    vmem = pl.BlockSpec(memory_space=pltpu.VMEM)
    smem = pl.BlockSpec(memory_space=pltpu.SMEM)
    shape = jax.ShapeDtypeStruct
    room = lambda mib: pltpu.CompilerParams(vmem_limit_bytes=mib * 1024 * 1024)
    cost = lambda flops, size: pl.CostEstimate(flops=flops, bytes_accessed=size, transcendentals=0)

    here = lambda: lax.axis_index("grp") * lax.axis_size("view") + lax.axis_index("view")
    hbm = pl.BlockSpec(memory_space=pltpu.HBM)
    stay = lambda value: pltpu.with_memory_space_constraint(value, pltpu.HBM)

    other = send(flat, swap)
    mine, packed = pl.pallas_call(
        load_kernel,
        out_shape=(shape(flat.shape, flat.dtype), shape((part + 8, plane), jnp.bfloat16)),
        in_specs=[hbm],
        out_specs=(vmem, vmem),
        scratch_shapes=[pltpu.SemaphoreType.DMA],
        compiler_params=room(4),
        cost_estimate=cost(1, 1),
        name="load",
    )(stay(flat))
    other, mine, packed = lax.optimization_barrier((other, mine, packed))
    both = pl.pallas_call(
        join_kernel,
        out_shape=shape((piece + 8, plane), jnp.bfloat16),
        in_specs=[vmem] * 2,
        out_specs=vmem,
        compiler_params=room(4),
        name="join",
    )(packed, other)
    got_second = send(both, second)
    got_first = send(both, first)

    sino_shape = shape((channels // 128, views * det_rows, 128), jnp.float32)
    lists_shape = (Pairs.FIELDS * Pairs.GROUPS + 2, views * slots)
    table_vmem, turned, lists, sino, decay = pl.pallas_call(
        functools.partial(
            early_kernel, chips=devices // 2, local_blocks=local_blocks, slab=slab, here=here
        ),
        out_shape=(
            shape((plane, tables * channels), table.dtype),
            shape((tables * channels, plane), table.dtype),
            shape(lists_shape, jnp.int32),
            sino_shape,
            sino_shape,
        ),
        in_specs=[vmem] + [hbm] * 6,
        out_specs=(vmem,) * 5,
        scratch_shapes=[
            pltpu.VMEM(measured.shape, measured.dtype),
            pltpu.VMEM((slots, views), jnp.int32),
            pltpu.VMEM((slots, views), jnp.int32),
            pltpu.VMEM((1, views), jnp.int32),
            pltpu.VMEM((1, views), jnp.int32),
            pltpu.VMEM((2 * slots + 2, views), jnp.int32),
            pltpu.SMEM((2 * slots + 2, views), jnp.int32),
            pltpu.SMEM(lists_shape, jnp.int32),
            pltpu.SMEM((5 * piece // slab, tables), jnp.int32),
            pltpu.SMEM((5 * piece // slab,), jnp.int32),
            pltpu.SMEM((5 * piece // slab, views * slots), jnp.int32),
            pltpu.VMEM((piece, tables * channels), jnp.float32),
            pltpu.SemaphoreType.DMA((5 + tables,)),
        ],
        compiler_params=room(16),
        cost_estimate=cost(1, 1),
        name="early",
    )(
        both,
        stay(table),
        stay(measured),
        stay(cover.T),
        stay(offset.T),
        stay(count.reshape(1, views)),
        stay(angle_index.reshape(1, views)),
    )
    got_second, got_first, table_vmem, turned, lists, sino, decay = lax.optimization_barrier(
        (got_second, got_first, table_vmem, turned, lists, sino, decay)
    )
    index = [pltpu.SMEM(lists_shape, jnp.int32)]
    waits = [pltpu.SemaphoreType.DMA]
    rows_of = lambda rows: [pltpu.VMEM((rows, tables * channels), jnp.float32)]
    picks_of = lambda blocks: [
        pltpu.VMEM(((max(views * slots, blocks) + MORE) * slab, tables * channels), jnp.bfloat16),
        pltpu.VMEM((blocks * slab, plane), jnp.float32),
    ]

    far = send(jnp.concatenate([got_first, got_second], axis=0), swap)
    sino = pl.pallas_call(
        functools.partial(middle_kernel, slab=slab),
        out_shape=sino_shape,
        in_specs=[vmem] * 5,
        out_specs=vmem,
        scratch_shapes=index + rows_of(2 * piece) + waits,
        compiler_params=room(16),
        cost_estimate=cost(1, 1),
        name="middle",
    )(lists, got_first, got_second, table_vmem, sino)
    far, sino = lax.optimization_barrier((far, sino))
    sino, give = pl.pallas_call(
        functools.partial(main_kernel, slab=slab),
        out_shape=(sino_shape, shape((2 * piece, plane), jnp.float32)),
        in_specs=[vmem] * 6,
        out_specs=(vmem, vmem),
        scratch_shapes=index + rows_of(2 * piece) + picks_of(STATIC) + waits,
        compiler_params=room(16),
        cost_estimate=cost(1, 1),
        name="main",
    )(lists, far, table_vmem, turned, sino, decay)
    taken = send(give, swap)
    keep = pl.pallas_call(
        functools.partial(rest_kernel, group=0, slab=slab),
        out_shape=shape((2 * piece, plane), jnp.float32),
        in_specs=[vmem] * 4,
        out_specs=vmem,
        scratch_shapes=index + picks_of(STATIC) + waits,
        compiler_params=room(16),
        cost_estimate=cost(1, 1),
        name="rest",
    )(lists, turned, sino, decay)
    taken, keep = lax.optimization_barrier((taken, keep))
    wire = (keep + taken).astype(jnp.bfloat16)
    back_second = send(wire[piece:], back(second))
    back_first = send(wire[:piece], back(first))

    home = pl.pallas_call(
        functools.partial(rest_kernel, group=2, slab=slab),
        out_shape=shape((piece, plane), jnp.float32),
        in_specs=[vmem] * 4,
        out_specs=vmem,
        scratch_shapes=index + picks_of(8) + waits,
        compiler_params=room(16),
        cost_estimate=cost(1, 1),
        name="home",
    )(lists, turned, sino, decay)
    prior = pl.pallas_call(
        functools.partial(prior_kernel, devices=devices, here=here),
        out_shape=shape((part, plane), jnp.float32),
        in_specs=[vmem] * 5,
        out_specs=vmem,
        compiler_params=room(8),
        cost_estimate=cost(1, 1),
        name="prior",
    )(mine, other, got_first, got_second, far)
    back_second, back_first, home, prior = lax.optimization_barrier(
        (back_second, back_first, home, prior)
    )

    arrived = (back_second.astype(jnp.float32) + back_first.astype(jnp.float32)) + home
    passed = send(arrived[part:], swap)
    out = pl.pallas_call(
        last_kernel,
        out_shape=shape((part, strip, row), jnp.float32),
        in_specs=[vmem] * 3,
        out_specs=vmem,
        compiler_params=room(4),
        name="last",
    )(arrived[:part], passed, prior)
    return out.reshape(volume.shape)


def solution(mesh):
    in_specs = (
        P(AXES, None, None, None),
        P(AXES, None, None, None),
        P(AXES, None, None),
        P(AXES),
        P(AXES, None),
        P(AXES, None),
        P(AXES),
    )
    out_specs = P(AXES, None, None, None)
    return jax.shard_map(shards, mesh=mesh, in_specs=in_specs, out_specs=out_specs, check_vma=False)
```

```python
import functools

import jax
import jax.numpy as jnp
from jax import lax
from jax.experimental import pallas as pl
from jax.experimental.pallas import tpu as pltpu
from jax.sharding import PartitionSpec as P

AXES = ("grp", "view")
STATIC = 12
MORE = 4
DELTA = 0.5
PRIOR_WEIGHT = 2.0


def both_ways(pairs):
    return pairs + [(b, a) for a, b in pairs]


def exchange_pairs(devices):
    chips = devices // 2
    swap = [(i, i ^ 1) for i in range(devices)]
    edge_y = [(i, i + 1) for i in range(0, chips, 2)]
    edge_d = [(i, i + 1) for i in range(1, chips - 1, 2)]
    edge_a = [(i + j, i + j + 2) for i in range(0, chips, 4) for j in (0, 1)]
    edge_b = [(i + j, i + j + 2) for i in range(2, chips - 2, 4) for j in (0, 1)]
    idle = [(0, 1), (chips - 2, chips - 1)]
    on_core = lambda edges, core: [(2 * a + core, 2 * b + core) for a, b in edges]
    last = devices - 1
    ends = [(0, 4), (4, 1), (1, 0), (last - 1, last - 5), (last - 5, last), (last, last - 1)]
    first = both_ways(on_core(edge_a[1:-1], 0) + on_core(edge_d, 1)) + ends
    second = both_ways(on_core(edge_b + idle, 0) + on_core(edge_y, 1))
    return swap, first, second


def load_kernel(source, target, own_ref, sem):
    copy = pltpu.make_async_copy(source, target, sem)
    copy.start()
    copy.wait()
    strip, row = target.shape[1:]
    for y in range(strip):
        own_ref[:, y * row : (y + 1) * row] = target[:, y, :].astype(jnp.bfloat16)


def join_kernel(mine_ref, own_ref, other_ref, first_ref, second_ref, *, here):
    slices, strip, row = other_ref.shape
    tiles = strip * row // 128
    part = slices
    rest = {}
    for name, ref in (("mine", mine_ref), ("other", other_ref)):
        for at in (0, slices - 1):
            for y in range(strip):
                whole = ref[at : at + 1, y, :]
                left = whole - whole.astype(jnp.bfloat16).astype(jnp.float32)
                mid = left.astype(jnp.bfloat16).astype(jnp.float32)
                rest[name, at, y] = (mid, left - mid)
    position = here()
    core = lax.rem(position, 2)
    odd = lax.rem(position // 2, 2)
    for y in range(strip):
        packed = other_ref[:, y, :].astype(jnp.bfloat16)
        for k in range(row // 128):
            tile = y * (row // 128) + k
            cols = slice(k * 128, (k + 1) * 128)
            for ref in (first_ref, second_ref):
                ref[tile * 2 * part : tile * 2 * part + part, :] = own_ref[
                    :, tile * 128 : (tile + 1) * 128
                ]
                ref[tile * 2 * part + part : (tile + 1) * 2 * part, :] = packed[:, cols]
    top, bottom = [], []
    for y in range(strip):
        for k in range(row // 128):
            cols = slice(k * 128, (k + 1) * 128)
            for which in range(2):
                a = rest["mine", 0, y][which][:, cols]
                b = rest["other", 0, y][which][:, cols]
                top.append(jnp.where(core == 0, a, b))
                a = rest["mine", slices - 1, y][which][:, cols]
                b = rest["other", slices - 1, y][which][:, cols]
                bottom.append(jnp.where(core == 1, a, b))
    top = jnp.concatenate(top, axis=0)
    bottom = jnp.concatenate(bottom, axis=0)
    tail = slice(tiles * 2 * part, tiles * 2 * part + 2 * tiles)
    first_ref[tail, :] = jnp.where(odd == 1, bottom, top).astype(jnp.bfloat16)
    second_ref[tail, :] = jnp.where(odd == 1, top, bottom).astype(jnp.bfloat16)


def unfold(ref, begin, window, first_row, piece):
    for j in range(window.shape[1] // 128):
        window[first_row : first_row + piece, j * 128 : (j + 1) * 128] = ref[
            begin + j * piece : begin + (j + 1) * piece, :
        ]


def window_rows(block, position, chips, local_blocks, slab):
    part = local_blocks * slab
    piece = 2 * part
    core = lax.rem(position, 2)
    chip = position // 2
    owner = block // local_blocks
    owner_core = lax.rem(owner, 2)
    delta = owner // 2 - chip
    flag = lambda what: jnp.where(what, 1, 0)
    up = flag(delta > 0)
    nearer = jnp.abs(delta) == 1
    is_y = flag(up == 1 - lax.rem(chip, 2))
    is_a = flag(up == flag(lax.rem(chip, 4) < 2))
    second = jnp.where(nearer, is_y, 1 - is_a)
    via = flag(nearer)
    end = flag((chip == 0) | (chip == chips - 1))
    held = jnp.where(nearer, 1, is_a * end)
    away = (2 * jnp.abs(held - core) + second) * piece + jnp.abs(owner_core - via) * part
    here = 4 * piece + jnp.abs(owner_core - core) * part
    return jnp.where(delta == 0, here, away) + lax.rem(block, local_blocks) * slab


class Pairs:
    FIELDS = 5
    GROUPS = 3

    def __init__(self, ref):
        self.ref = ref

    def each(self, group, do):
        def body(i, carry):
            do(*(self.ref[self.FIELDS * group + k, i] for k in range(4)))
            return carry

        lax.fori_loop(0, self.ref[self.FIELDS * self.GROUPS, group], body, 0)

    def gathered(self, group):
        return self.ref[self.FIELDS * self.GROUPS + 1, group]

    def target(self, group, i):
        return self.ref[self.FIELDS * group + 4, i]


def list_pairs(scal, lists, seen, height, held, near_rows, det_rows, tables, slab):
    slots = (scal.shape[0] - 2) // 2
    most = held.shape[1]
    fields, groups = Pairs.FIELDS, Pairs.GROUPS

    def clear(i, carry):
        height[i] = jnp.int32(0)
        for table in range(tables):
            seen[i, table] = jnp.int32(0)
        return carry

    lax.fori_loop(0, height.shape[0], clear, 0)
    for k in range(groups):
        lists[fields * groups, k] = jnp.int32(0)
        lists[fields * groups + 1, k] = jnp.int32(0)

    def body(view, carry):
        count = scal[2 * slots, view]
        table = scal[2 * slots + 1, view]
        for slot in range(slots):

            @pl.when(slot < count)
            def _():
                row = scal[slot, view]
                block = row // slab
                group = jnp.minimum(row // near_rows, groups - 1)
                local = row - group * near_rows
                first = fields * group
                at = lists[fields * groups, group]
                used = lists[fields * groups + 1, group]
                rank = seen[block, table]
                top = height[block]
                fresh = rank >= top
                mine = jnp.where(fresh, used, held[block, rank])
                held[block, rank] = mine
                seen[block, table] = rank + 1
                height[block] = jnp.where(fresh, rank + 1, top)
                lists[first, at] = view * det_rows + scal[slots + slot, view]
                lists[first + 1, at] = table
                lists[first + 2, at] = local
                lists[first + 3, at] = mine * slab
                lists[first + 4, mine] = local
                lists[fields * groups, group] = at + 1
                lists[fields * groups + 1, group] = used + jnp.where(fresh, 1, 0)

        return carry

    lax.fori_loop(0, scal.shape[1], body, 0)


def place(pairs, group, sino, proj, slab):
    width = sino.shape[0] * 128

    def add(target, table, local, dest):
        source = pl.ds(pl.multiple_of(local, slab), slab)
        for tile in range(sino.shape[0]):
            cols = pl.ds(pl.multiple_of(table * width + tile * 128, 128), 128)
            sino[tile, pl.ds(target, slab), :] += proj[source, cols]

    pairs.each(group, add)


def clear_rows(picked, static_rows):
    picked[0:static_rows, :] = jnp.zeros((static_rows, picked.shape[1]), picked.dtype)


def gather(pairs, group, sino, decay, picked, static_rows, slab):
    width = sino.shape[0] * 128
    chunk = MORE * slab

    def clear(i, carry):
        here = pl.ds(pl.multiple_of(static_rows + i * chunk, chunk), chunk)
        picked[here, :] = jnp.zeros((chunk, picked.shape[1]), picked.dtype)
        return carry

    more = pairs.gathered(group) * slab - static_rows
    lax.fori_loop(0, (more + chunk - 1) // chunk, clear, 0)

    def take(source, table, local, dest):
        target = pl.ds(pl.multiple_of(dest, slab), slab)
        here = pl.ds(source, slab)
        for tile in range(sino.shape[0]):
            cols = pl.ds(pl.multiple_of(table * width + tile * 128, 128), 128)
            value = decay[tile, here, :] * sino[tile, here, :]
            picked[target, cols] = value.astype(jnp.bfloat16)

    pairs.each(group, take)


def back_project(pairs, group, picked, turned_ref, spread, out_ref, slab):
    static_rows = spread.shape[0]
    static = static_rows // slab
    blocks = pairs.gathered(group)
    out_ref[...] = jnp.zeros_like(out_ref)

    def add_from(begin):
        def add(i, carry):
            target = pl.ds(pl.multiple_of(pairs.target(group, i), slab), slab)
            source = pl.ds(pl.multiple_of((i - begin) * slab, slab), slab)
            out_ref[target, :] += spread[source, :]
            return carry

        return add

    spread[...] = jnp.dot(
        picked[0:static_rows, :], turned_ref[...], preferred_element_type=jnp.float32
    )
    lax.fori_loop(0, jnp.minimum(blocks, static), add_from(0), 0)

    def further(c, carry):
        begin = static + c * MORE
        here = pl.ds(pl.multiple_of(begin * slab, MORE * slab), MORE * slab)
        spread[0 : MORE * slab, :] = jnp.dot(
            picked[here, :], turned_ref[...], preferred_element_type=jnp.float32
        )
        lax.fori_loop(begin, jnp.minimum(blocks, begin + MORE), add_from(begin), 0)
        return carry

    lax.fori_loop(0, (blocks - static + MORE - 1) // MORE, further, 0)


def early_kernel(
    both_ref,
    table_hbm,
    measured_hbm,
    cover_hbm,
    offset_hbm,
    count_hbm,
    angle_hbm,
    table_ref,
    turned_ref,
    lists_ref,
    sino_ref,
    decay_ref,
    measured,
    cover,
    offset,
    count,
    angle,
    index,
    scal,
    lists,
    seen,
    height,
    held,
    window,
    proj,
    sems,
    *,
    piece,
    chips,
    local_blocks,
    slab,
    here,
):
    views, det_rows, channels = measured.shape
    slots = cover.shape[0]
    tables = table_hbm.shape[0]
    small = [(cover_hbm, cover), (offset_hbm, offset), (count_hbm, count), (angle_hbm, angle)]
    unfold(both_ref, 0, window, 0, piece)
    copies = [pltpu.make_async_copy(a, b, sems.at[i]) for i, (a, b) in enumerate(small)]
    copies.append(pltpu.make_async_copy(measured_hbm, measured, sems.at[4]))
    for table in range(tables):
        to = table_ref.at[:, table * channels : (table + 1) * channels]
        copies.append(pltpu.make_async_copy(table_hbm.at[table], to, sems.at[5 + table]))
    for copy in copies:
        copy.start()
    for copy in copies[:4]:
        copy.wait()
    index[0:slots, :] = window_rows(cover[...], here(), chips, local_blocks, slab)
    index[slots : 2 * slots, :] = offset[...]
    index[2 * slots : 2 * slots + 1, :] = count[...]
    index[2 * slots + 1 : 2 * slots + 2, :] = angle[...]
    load = fetch(index, scal, sems.at[0])
    copies[4].wait()

    def fade(view, carry):
        rows = pl.ds(pl.multiple_of(view * det_rows, det_rows), det_rows)
        for tile in range(sino_ref.shape[0]):
            value = measured[view, :, tile * 128 : (tile + 1) * 128].astype(jnp.float32)
            decay_ref[tile, rows, :] = jnp.exp(-value)
            sino_ref[tile, rows, :] = -value
        return carry

    lax.fori_loop(0, views, fade, 0)
    load.wait()
    list_pairs(scal, lists, seen, height, held, 2 * piece, det_rows, tables, slab)
    save = fetch(lists, lists_ref, sems.at[0])
    for table in range(tables):
        copies[5 + table].wait()
        cols = slice(table * channels, (table + 1) * channels)
        turned_ref[cols, :] = table_ref[:, cols].T
    proj[...] = jnp.dot(window[...], table_ref[...], preferred_element_type=jnp.float32)
    place(Pairs(lists), 2, sino_ref, proj, slab)
    save.wait()


def fetch(source, target, sem):
    load = pltpu.make_async_copy(source, target, sem)
    load.start()
    return load


def project(load, lists, group, window, table_ref, begun_ref, sino_ref, proj, slab):
    sino_ref[...] = begun_ref[...]
    proj[...] = jnp.dot(window[...], table_ref[...], preferred_element_type=jnp.float32)
    load.wait()
    place(Pairs(lists), group, sino_ref, proj, slab)


def middle_kernel(
    lists_ref, first_ref, second_ref, table_ref, begun_ref, sino_ref, lists, window, proj, sem, *, slab
):
    load = fetch(lists_ref, lists, sem)
    piece = proj.shape[0] // 2
    for k, ref in enumerate((first_ref, second_ref)):
        unfold(ref, 0, window, k * piece, piece)
    project(load, lists, 0, window, table_ref, begun_ref, sino_ref, proj, slab)


def main_kernel(
    lists_ref,
    far_ref,
    table_ref,
    turned_ref,
    begun_ref,
    decay_ref,
    sino_ref,
    give_ref,
    lists,
    window,
    proj,
    picked,
    spread,
    sem,
    *,
    slab,
):
    load = fetch(lists_ref, lists, sem)
    clear_rows(picked, spread.shape[0])
    piece = proj.shape[0] // 2
    for k in range(2):
        unfold(far_ref, k * far_ref.shape[0] // 2, window, k * piece, piece)
    project(load, lists, 1, window, table_ref, begun_ref, sino_ref, proj, slab)
    pairs = Pairs(lists)
    gather(pairs, 1, sino_ref, decay_ref, picked, spread.shape[0], slab)
    back_project(pairs, 1, picked, turned_ref, spread, give_ref, slab)


def rest_kernel(
    lists_ref, turned_ref, sino_ref, decay_ref, out_ref, lists, picked, spread, sem, *, group, slab
):
    load = fetch(lists_ref, lists, sem)
    clear_rows(picked, spread.shape[0])
    load.wait()
    pairs = Pairs(lists)
    gather(pairs, group, sino_ref, decay_ref, picked, spread.shape[0], slab)
    back_project(pairs, group, picked, turned_ref, spread, out_ref, slab)


def prior_kernel(
    vol_ref, other_ref, first_ref, second_ref, far_ref, out_ref, *, devices, here
):
    slices, strip, row = vol_ref.shape
    part = slices
    piece = 2 * part
    position = here()
    core = lax.rem(position, 2)
    odd = lax.rem(position // 2, 2)

    def chip_slice(ref, which, base=0):
        at = part if which == 0 else part - 1
        tiles = strip * row // 128

        def column(tile):
            whole = ref[base + tile * piece + at : base + tile * piece + at + 1, :]
            tail = base + tiles * piece + 2 * tile
            mid, low = ref[tail : tail + 1, :], ref[tail + 1 : tail + 2, :]
            return whole.astype(jnp.float32) + (mid.astype(jnp.float32) + low.astype(jnp.float32))

        here = row // 128
        return lambda y: jnp.concatenate([column(y * here + k) for k in range(here)], axis=1)

    def core_slice(which):
        at = (part - 1) * which
        return lambda y: other_ref[at : at + 1, y, :]

    def emit(low, high):
        for y in range(strip):
            cols = slice(y * row, (y + 1) * row)
            here = vol_ref[:, y, :]
            below = jnp.concatenate([low(y), here[:-1]], axis=0)
            above = jnp.concatenate([here[1:], high(y)], axis=0)
            level = lax.broadcasted_iota(jnp.int32, here.shape, 0)
            down = jnp.clip(here - below, -DELTA, DELTA)
            total = jnp.where((level > 0) | (position > 0), down, 0.0)
            up = jnp.clip(here - above, -DELTA, DELTA)
            total += jnp.where((level < slices - 1) | (position < devices - 1), up, 0.0)
            if y > 0:
                total += jnp.clip(here - vol_ref[:, y - 1, :], -DELTA, DELTA)
            if y + 1 < strip:
                total += jnp.clip(here - vol_ref[:, y + 1, :], -DELTA, DELTA)
            lane = lax.broadcasted_iota(jnp.int32, here.shape, 1)
            left = jnp.clip(here - pltpu.roll(here, 1, 1), -DELTA, DELTA)
            total += jnp.where(lane > 0, left, 0.0)
            right = jnp.clip(here - pltpu.roll(here, row - 1, 1), -DELTA, DELTA)
            total += jnp.where(lane < row - 1, right, 0.0)
            out_ref[:, cols] = PRIOR_WEIGHT * total

    @pl.when((core == 0) & (odd == 0))
    def _():
        emit(chip_slice(far_ref, 1), core_slice(0))

    @pl.when((core == 0) & (odd == 1))
    def _():
        emit(chip_slice(far_ref, 1, far_ref.shape[0] // 2), core_slice(0))

    @pl.when((core == 1) & (odd == 0))
    def _():
        emit(core_slice(1), chip_slice(second_ref, 0))

    @pl.when((core == 1) & (odd == 1))
    def _():
        emit(core_slice(1), chip_slice(first_ref, 0))


def last_kernel(arrived_ref, passed_ref, prior_ref, out_ref):
    part, strip, row = out_ref.shape
    for y in range(strip):
        cols = slice(y * row, (y + 1) * row)
        out_ref[:, y, :] = (arrived_ref[:, cols] + passed_ref[:, cols]) + prior_ref[:, cols]


def shards(volume, footprint, measured, angle_index, cover, offset, count):
    local_blocks, slab, strip, row = volume.shape
    views, det_rows, channels = measured.shape
    tables = footprint.shape[0]
    slots = cover.shape[1]
    plane = strip * row
    devices = lax.axis_size(AXES)
    position = lax.axis_index(AXES)
    swap, first, second = exchange_pairs(devices)
    back = lambda pairs: [(b, a) for a, b in pairs]
    send = lambda value, pairs: lax.ppermute(value, AXES, pairs)
    part = local_blocks * slab
    piece = 2 * part
    flat = volume.reshape(part, strip, row)
    table = footprint.reshape(tables, plane, channels)
    vmem = pl.BlockSpec(memory_space=pltpu.VMEM)
    smem = pl.BlockSpec(memory_space=pltpu.SMEM)
    shape = jax.ShapeDtypeStruct
    room = lambda mib: pltpu.CompilerParams(vmem_limit_bytes=mib * 1024 * 1024)
    cost = lambda flops, size: pl.CostEstimate(flops=flops, bytes_accessed=size, transcendentals=0)

    here = lambda: lax.axis_index("grp") * lax.axis_size("view") + lax.axis_index("view")
    hbm = pl.BlockSpec(memory_space=pltpu.HBM)
    stay = lambda value: pltpu.with_memory_space_constraint(value, pltpu.HBM)

    other = send(flat, swap)
    mine, packed = pl.pallas_call(
        load_kernel,
        out_shape=(shape(flat.shape, flat.dtype), shape((part, plane), jnp.bfloat16)),
        in_specs=[hbm],
        out_specs=(vmem, vmem),
        scratch_shapes=[pltpu.SemaphoreType.DMA],
        compiler_params=room(4),
        cost_estimate=cost(1, 1),
        name="load",
    )(stay(flat))
    other, mine, packed = lax.optimization_barrier((other, mine, packed))
    sent = shape((plane // 128 * (piece + 2), 128), jnp.bfloat16)
    for_first, for_second = pl.pallas_call(
        functools.partial(join_kernel, here=here),
        out_shape=(sent, sent),
        in_specs=[vmem] * 3,
        out_specs=(vmem, vmem),
        compiler_params=room(4),
        name="join",
    )(mine, packed, other)
    got_second = send(for_second, second)
    got_first = send(for_first, first)

    sino_shape = shape((channels // 128, views * det_rows, 128), jnp.float32)
    lists_shape = (Pairs.FIELDS * Pairs.GROUPS + 2, views * slots)
    table_vmem, turned, lists, sino, decay = pl.pallas_call(
        functools.partial(
            early_kernel,
            piece=piece,
            chips=devices // 2,
            local_blocks=local_blocks,
            slab=slab,
            here=here,
        ),
        out_shape=(
            shape((plane, tables * channels), table.dtype),
            shape((tables * channels, plane), table.dtype),
            shape(lists_shape, jnp.int32),
            sino_shape,
            sino_shape,
        ),
        in_specs=[vmem] + [hbm] * 6,
        out_specs=(vmem,) * 5,
        scratch_shapes=[
            pltpu.VMEM(measured.shape, measured.dtype),
            pltpu.VMEM((slots, views), jnp.int32),
            pltpu.VMEM((slots, views), jnp.int32),
            pltpu.VMEM((1, views), jnp.int32),
            pltpu.VMEM((1, views), jnp.int32),
            pltpu.VMEM((2 * slots + 2, views), jnp.int32),
            pltpu.SMEM((2 * slots + 2, views), jnp.int32),
            pltpu.SMEM(lists_shape, jnp.int32),
            pltpu.SMEM((5 * piece // slab, tables), jnp.int32),
            pltpu.SMEM((5 * piece // slab,), jnp.int32),
            pltpu.SMEM((5 * piece // slab, views * slots), jnp.int32),
            pltpu.VMEM((piece, plane), jnp.bfloat16),
            pltpu.VMEM((piece, tables * channels), jnp.float32),
            pltpu.SemaphoreType.DMA((5 + tables,)),
        ],
        compiler_params=room(16),
        cost_estimate=cost(1, 1),
        name="early",
    )(
        for_second,
        stay(table),
        stay(measured),
        stay(cover.T),
        stay(offset.T),
        stay(count.reshape(1, views)),
        stay(angle_index.reshape(1, views)),
    )
    got_second, got_first, table_vmem, turned, lists, sino, decay = lax.optimization_barrier(
        (got_second, got_first, table_vmem, turned, lists, sino, decay)
    )
    index = [pltpu.SMEM(lists_shape, jnp.int32)]
    waits = [pltpu.SemaphoreType.DMA]
    rows_of = lambda rows: [pltpu.VMEM((rows, tables * channels), jnp.float32)]
    window = [pltpu.VMEM((2 * piece, plane), jnp.bfloat16)]
    picks_of = lambda blocks: [
        pltpu.VMEM(((max(views * slots, blocks) + MORE) * slab, tables * channels), jnp.bfloat16),
        pltpu.VMEM((blocks * slab, plane), jnp.float32),
    ]

    far = send(jnp.concatenate([got_first, got_second], axis=0), swap)
    sino = pl.pallas_call(
        functools.partial(middle_kernel, slab=slab),
        out_shape=sino_shape,
        in_specs=[vmem] * 5,
        out_specs=vmem,
        scratch_shapes=index + window + rows_of(2 * piece) + waits,
        compiler_params=room(16),
        cost_estimate=cost(1, 1),
        name="middle",
    )(lists, got_first, got_second, table_vmem, sino)
    far, sino = lax.optimization_barrier((far, sino))
    sino, give = pl.pallas_call(
        functools.partial(main_kernel, slab=slab),
        out_shape=(sino_shape, shape((2 * piece, plane), jnp.float32)),
        in_specs=[vmem] * 6,
        out_specs=(vmem, vmem),
        scratch_shapes=index + window + rows_of(2 * piece) + picks_of(STATIC) + waits,
        compiler_params=room(16),
        cost_estimate=cost(1, 1),
        name="main",
    )(lists, far, table_vmem, turned, sino, decay)
    taken = send(give, swap)
    keep = pl.pallas_call(
        functools.partial(rest_kernel, group=0, slab=slab),
        out_shape=shape((2 * piece, plane), jnp.float32),
        in_specs=[vmem] * 4,
        out_specs=vmem,
        scratch_shapes=index + picks_of(STATIC) + waits,
        compiler_params=room(16),
        cost_estimate=cost(1, 1),
        name="rest",
    )(lists, turned, sino, decay)
    taken, keep = lax.optimization_barrier((taken, keep))
    wire = (keep + taken).astype(jnp.bfloat16)
    back_second = send(wire[piece:], back(second))
    back_first = send(wire[:piece], back(first))

    home = pl.pallas_call(
        functools.partial(rest_kernel, group=2, slab=slab),
        out_shape=shape((piece, plane), jnp.float32),
        in_specs=[vmem] * 4,
        out_specs=vmem,
        scratch_shapes=index + picks_of(8) + waits,
        compiler_params=room(16),
        cost_estimate=cost(1, 1),
        name="home",
    )(lists, turned, sino, decay)
    prior = pl.pallas_call(
        functools.partial(prior_kernel, devices=devices, here=here),
        out_shape=shape((part, plane), jnp.float32),
        in_specs=[vmem] * 5,
        out_specs=vmem,
        compiler_params=room(8),
        cost_estimate=cost(1, 1),
        name="prior",
    )(mine, other, got_first, got_second, far)
    back_second, back_first, home, prior = lax.optimization_barrier(
        (back_second, back_first, home, prior)
    )

    arrived = (back_second.astype(jnp.float32) + back_first.astype(jnp.float32)) + home
    passed = send(arrived[part:], swap)
    out = pl.pallas_call(
        last_kernel,
        out_shape=shape((part, strip, row), jnp.float32),
        in_specs=[vmem] * 3,
        out_specs=vmem,
        compiler_params=room(4),
        name="last",
    )(arrived[:part], passed, prior)
    return out.reshape(volume.shape)


def solution(mesh):
    in_specs = (
        P(AXES, None, None, None),
        P(AXES, None, None, None),
        P(AXES, None, None),
        P(AXES),
        P(AXES, None),
        P(AXES, None),
        P(AXES),
    )
    out_specs = P(AXES, None, None, None)
    return jax.shard_map(shards, mesh=mesh, in_specs=in_specs, out_specs=out_specs, check_vma=False)
```

```python
import functools

import jax
import jax.numpy as jnp
from jax import lax
from jax.experimental import pallas as pl
from jax.experimental.pallas import tpu as pltpu
from jax.sharding import PartitionSpec as P

AXES = ("grp", "view")
STATIC = 12
MORE = 4
DELTA = 0.5
PRIOR_WEIGHT = 2.0


def both_ways(pairs):
    return pairs + [(b, a) for a, b in pairs]


def exchange_pairs(devices):
    chips = devices // 2
    swap = [(i, i ^ 1) for i in range(devices)]
    edge_y = [(i, i + 1) for i in range(0, chips, 2)]
    edge_d = [(i, i + 1) for i in range(1, chips - 1, 2)]
    edge_a = [(i + j, i + j + 2) for i in range(0, chips, 4) for j in (0, 1)]
    edge_b = [(i + j, i + j + 2) for i in range(2, chips - 2, 4) for j in (0, 1)]
    idle = [(0, 1), (chips - 2, chips - 1)]
    on_core = lambda edges, core: [(2 * a + core, 2 * b + core) for a, b in edges]
    last = devices - 1
    ends = [(0, 4), (4, 1), (1, 0), (last - 1, last - 5), (last - 5, last), (last, last - 1)]
    first = both_ways(on_core(edge_a[1:-1], 0) + on_core(edge_d, 1)) + ends
    second = both_ways(on_core(edge_b + idle, 0) + on_core(edge_y, 1))
    return swap, first, second


def load_kernel(source, target, own_ref, sem):
    copy = pltpu.make_async_copy(source, target, sem)
    copy.start()
    copy.wait()
    strip, row = target.shape[1:]
    for y in range(strip):
        own_ref[:, y * row : (y + 1) * row] = target[:, y, :].astype(jnp.bfloat16)


def join_kernel(mine_ref, own_ref, other_ref, first_ref, second_ref, *, here):
    slices, strip, row = other_ref.shape
    tiles = strip * row // 128
    part = slices
    rest = {}
    for name, ref in (("mine", mine_ref), ("other", other_ref)):
        for at in (0, slices - 1):
            for y in range(strip):
                whole = ref[at : at + 1, y, :]
                left = whole - whole.astype(jnp.bfloat16).astype(jnp.float32)
                mid = left.astype(jnp.bfloat16).astype(jnp.float32)
                rest[name, at, y] = (mid, left - mid)
    position = here()
    core = lax.rem(position, 2)
    odd = lax.rem(position // 2, 2)
    for y in range(strip):
        packed = other_ref[:, y, :].astype(jnp.bfloat16)
        for k in range(row // 128):
            tile = y * (row // 128) + k
            cols = slice(k * 128, (k + 1) * 128)
            for ref in (first_ref, second_ref):
                ref[tile * 2 * part : tile * 2 * part + part, :] = own_ref[
                    :, tile * 128 : (tile + 1) * 128
                ]
                ref[tile * 2 * part + part : (tile + 1) * 2 * part, :] = packed[:, cols]
    top, bottom = [], []
    for y in range(strip):
        for k in range(row // 128):
            cols = slice(k * 128, (k + 1) * 128)
            for which in range(2):
                a = rest["mine", 0, y][which][:, cols]
                b = rest["other", 0, y][which][:, cols]
                top.append(jnp.where(core == 0, a, b))
                a = rest["mine", slices - 1, y][which][:, cols]
                b = rest["other", slices - 1, y][which][:, cols]
                bottom.append(jnp.where(core == 1, a, b))
    top = jnp.concatenate(top, axis=0)
    bottom = jnp.concatenate(bottom, axis=0)
    tail = slice(tiles * 2 * part, tiles * 2 * part + 2 * tiles)
    first_ref[tail, :] = jnp.where(odd == 1, bottom, top).astype(jnp.bfloat16)
    second_ref[tail, :] = jnp.where(odd == 1, top, bottom).astype(jnp.bfloat16)


def unfold(ref, begin, window, first_row, piece):
    for j in range(window.shape[1] // 128):
        window[first_row : first_row + piece, j * 128 : (j + 1) * 128] = ref[
            begin + j * piece : begin + (j + 1) * piece, :
        ]


def window_rows(block, position, chips, local_blocks, slab):
    part = local_blocks * slab
    piece = 2 * part
    core = lax.rem(position, 2)
    chip = position // 2
    owner = block // local_blocks
    owner_core = lax.rem(owner, 2)
    delta = owner // 2 - chip
    flag = lambda what: jnp.where(what, 1, 0)
    up = flag(delta > 0)
    nearer = jnp.abs(delta) == 1
    is_y = flag(up == 1 - lax.rem(chip, 2))
    is_a = flag(up == flag(lax.rem(chip, 4) < 2))
    second = jnp.where(nearer, is_y, 1 - is_a)
    via = flag(nearer)
    end = flag((chip == 0) | (chip == chips - 1))
    held = jnp.where(nearer, 1, is_a * end)
    away = (2 * jnp.abs(held - core) + second) * piece + jnp.abs(owner_core - via) * part
    here = 4 * piece + jnp.abs(owner_core - core) * part
    return jnp.where(delta == 0, here, away) + lax.rem(block, local_blocks) * slab


class Pairs:
    ROWS = 8
    GROUPS = 3

    def __init__(self, ref, first=0):
        self.ref = ref
        self.first = first

    def each(self, do):
        def body(i, carry):
            do(*(self.ref[self.first + k, i] for k in range(4)))
            return carry

        lax.fori_loop(0, self.ref[self.first + 5, 0], body, 0)

    def gathered(self):
        return self.ref[self.first + 5, 1]

    def target(self, i):
        return self.ref[self.first + 4, i]


def list_pairs(scal, lists, seen, height, held, near_rows, det_rows, tables, slab):
    slots = (scal.shape[0] - 2) // 2
    most = held.shape[1]
    fields, groups = Pairs.ROWS, Pairs.GROUPS

    def clear(i, carry):
        height[i] = jnp.int32(0)
        for table in range(tables):
            seen[i, table] = jnp.int32(0)
        return carry

    lax.fori_loop(0, height.shape[0], clear, 0)
    for k in range(groups):
        lists[fields * k + 5, 0] = jnp.int32(0)
        lists[fields * k + 5, 1] = jnp.int32(0)

    def body(view, carry):
        count = scal[2 * slots, view]
        table = scal[2 * slots + 1, view]
        for slot in range(slots):

            @pl.when(slot < count)
            def _():
                row = scal[slot, view]
                block = row // slab
                group = jnp.minimum(row // near_rows, groups - 1)
                local = row - group * near_rows
                first = fields * group
                at = lists[first + 5, 0]
                used = lists[first + 5, 1]
                rank = seen[block, table]
                top = height[block]
                fresh = rank >= top
                mine = jnp.where(fresh, used, held[block, rank])
                held[block, rank] = mine
                seen[block, table] = rank + 1
                height[block] = jnp.where(fresh, rank + 1, top)
                lists[first, at] = view * det_rows + scal[slots + slot, view]
                lists[first + 1, at] = table
                lists[first + 2, at] = local
                lists[first + 3, at] = mine * slab
                lists[first + 4, mine] = local
                lists[first + 5, 0] = at + 1
                lists[first + 5, 1] = used + jnp.where(fresh, 1, 0)

        return carry

    lax.fori_loop(0, scal.shape[1], body, 0)


def place(pairs, sino, proj, slab):
    width = sino.shape[0] * 128

    def add(target, table, local, dest):
        source = pl.ds(pl.multiple_of(local, slab), slab)
        for tile in range(sino.shape[0]):
            cols = pl.ds(pl.multiple_of(table * width + tile * 128, 128), 128)
            sino[tile, pl.ds(target, slab), :] += proj[source, cols]

    pairs.each(add)


def clear_rows(picked, static_rows):
    picked[0:static_rows, :] = jnp.zeros((static_rows, picked.shape[1]), picked.dtype)


def gather(pairs, sino, decay, picked, static_rows, slab):
    width = sino.shape[0] * 128
    chunk = MORE * slab

    def clear(i, carry):
        here = pl.ds(pl.multiple_of(static_rows + i * chunk, chunk), chunk)
        picked[here, :] = jnp.zeros((chunk, picked.shape[1]), picked.dtype)
        return carry

    more = pairs.gathered() * slab - static_rows
    lax.fori_loop(0, (more + chunk - 1) // chunk, clear, 0)

    def take(source, table, local, dest):
        target = pl.ds(pl.multiple_of(dest, slab), slab)
        here = pl.ds(source, slab)
        for tile in range(sino.shape[0]):
            cols = pl.ds(pl.multiple_of(table * width + tile * 128, 128), 128)
            value = decay[tile, here, :] * sino[tile, here, :]
            picked[target, cols] = value.astype(jnp.bfloat16)

    pairs.each(take)


def back_project(pairs, picked, turned_ref, spread, out_ref, slab):
    static_rows = spread.shape[0]
    static = static_rows // slab
    blocks = pairs.gathered()
    out_ref[...] = jnp.zeros_like(out_ref)

    def add_from(begin):
        def add(i, carry):
            target = pl.ds(pl.multiple_of(pairs.target(i), slab), slab)
            source = pl.ds(pl.multiple_of((i - begin) * slab, slab), slab)
            out_ref[target, :] += spread[source, :]
            return carry

        return add

    spread[...] = jnp.dot(
        picked[0:static_rows, :], turned_ref[...], preferred_element_type=jnp.float32
    )
    lax.fori_loop(0, jnp.minimum(blocks, static), add_from(0), 0)

    def further(c, carry):
        begin = static + c * MORE
        here = pl.ds(pl.multiple_of(begin * slab, MORE * slab), MORE * slab)
        spread[0 : MORE * slab, :] = jnp.dot(
            picked[here, :], turned_ref[...], preferred_element_type=jnp.float32
        )
        lax.fori_loop(begin, jnp.minimum(blocks, begin + MORE), add_from(begin), 0)
        return carry

    lax.fori_loop(0, (blocks - static + MORE - 1) // MORE, further, 0)


def early_kernel(
    both_ref,
    table_hbm,
    measured_hbm,
    cover_hbm,
    offset_hbm,
    count_hbm,
    angle_hbm,
    table_ref,
    turned_ref,
    lists_ref,
    sino_ref,
    decay_ref,
    measured,
    cover,
    offset,
    count,
    angle,
    index,
    scal,
    lists,
    seen,
    height,
    held,
    window,
    proj,
    sems,
    *,
    piece,
    chips,
    local_blocks,
    slab,
    here,
):
    views, det_rows, channels = measured.shape
    slots = cover.shape[0]
    tables = table_hbm.shape[0]
    small = [(cover_hbm, cover), (offset_hbm, offset), (count_hbm, count), (angle_hbm, angle)]
    unfold(both_ref, 0, window, 0, piece)
    copies = [pltpu.make_async_copy(a, b, sems.at[i]) for i, (a, b) in enumerate(small)]
    copies.append(pltpu.make_async_copy(measured_hbm, measured, sems.at[4]))
    for table in range(tables):
        to = table_ref.at[:, table * channels : (table + 1) * channels]
        copies.append(pltpu.make_async_copy(table_hbm.at[table], to, sems.at[5 + table]))
    for copy in copies:
        copy.start()
    for copy in copies[:4]:
        copy.wait()
    index[0:slots, :] = window_rows(cover[...], here(), chips, local_blocks, slab)
    index[slots : 2 * slots, :] = offset[...]
    index[2 * slots : 2 * slots + 1, :] = count[...]
    index[2 * slots + 1 : 2 * slots + 2, :] = angle[...]
    load = fetch(index, scal, sems.at[0])
    copies[4].wait()

    def fade(view, carry):
        rows = pl.ds(pl.multiple_of(view * det_rows, det_rows), det_rows)
        for tile in range(sino_ref.shape[0]):
            value = measured[view, :, tile * 128 : (tile + 1) * 128].astype(jnp.float32)
            decay_ref[tile, rows, :] = jnp.exp(-value)
            sino_ref[tile, rows, :] = -value
        return carry

    lax.fori_loop(0, views, fade, 0)
    load.wait()
    list_pairs(scal, lists, seen, height, held, 2 * piece, det_rows, tables, slab)
    save = fetch(lists, lists_ref, sems.at[0])
    for table in range(tables):
        copies[5 + table].wait()
        cols = slice(table * channels, (table + 1) * channels)
        turned_ref[cols, :] = table_ref[:, cols].T
    proj[...] = jnp.dot(window[...], table_ref[...], preferred_element_type=jnp.float32)
    place(Pairs(lists, 2 * Pairs.ROWS), sino_ref, proj, slab)
    save.wait()


def fetch_group(lists_ref, group, lists, sem):
    return fetch(lists_ref.at[pl.ds(group * Pairs.ROWS, Pairs.ROWS)], lists, sem)


def fetch(source, target, sem):
    load = pltpu.make_async_copy(source, target, sem)
    load.start()
    return load


def project(load, lists, window, table_ref, begun_ref, sino_ref, proj, slab):
    sino_ref[...] = begun_ref[...]
    proj[...] = jnp.dot(window[...], table_ref[...], preferred_element_type=jnp.float32)
    load.wait()
    place(Pairs(lists), sino_ref, proj, slab)


def middle_kernel(
    lists_ref, first_ref, second_ref, table_ref, begun_ref, sino_ref, lists, window, proj, sem, *, slab
):
    load = fetch_group(lists_ref, 0, lists, sem)
    piece = proj.shape[0] // 2
    for k, ref in enumerate((first_ref, second_ref)):
        unfold(ref, 0, window, k * piece, piece)
    project(load, lists, window, table_ref, begun_ref, sino_ref, proj, slab)


def main_kernel(
    lists_ref,
    far_ref,
    table_ref,
    turned_ref,
    begun_ref,
    decay_ref,
    sino_ref,
    give_ref,
    lists,
    window,
    proj,
    picked,
    spread,
    sem,
    *,
    slab,
):
    load = fetch_group(lists_ref, 1, lists, sem)
    clear_rows(picked, spread.shape[0])
    piece = proj.shape[0] // 2
    for k in range(2):
        unfold(far_ref, k * far_ref.shape[0] // 2, window, k * piece, piece)
    project(load, lists, window, table_ref, begun_ref, sino_ref, proj, slab)
    pairs = Pairs(lists)
    gather(pairs, sino_ref, decay_ref, picked, spread.shape[0], slab)
    back_project(pairs, picked, turned_ref, spread, give_ref, slab)


def rest_kernel(
    lists_ref, turned_ref, sino_ref, decay_ref, out_ref, lists, picked, spread, sem, *, group, slab
):
    load = fetch_group(lists_ref, group, lists, sem)
    clear_rows(picked, spread.shape[0])
    load.wait()
    pairs = Pairs(lists)
    gather(pairs, sino_ref, decay_ref, picked, spread.shape[0], slab)
    back_project(pairs, picked, turned_ref, spread, out_ref, slab)


def prior_kernel(
    vol_ref, other_ref, first_ref, second_ref, far_ref, out_ref, *, devices, here
):
    slices, strip, row = vol_ref.shape
    part = slices
    piece = 2 * part
    position = here()
    core = lax.rem(position, 2)
    odd = lax.rem(position // 2, 2)

    def chip_slice(ref, which, base=0):
        at = part if which == 0 else part - 1
        tiles = strip * row // 128

        def column(tile):
            whole = ref[base + tile * piece + at : base + tile * piece + at + 1, :]
            tail = base + tiles * piece + 2 * tile
            mid, low = ref[tail : tail + 1, :], ref[tail + 1 : tail + 2, :]
            return whole.astype(jnp.float32) + (mid.astype(jnp.float32) + low.astype(jnp.float32))

        here = row // 128
        return lambda y: jnp.concatenate([column(y * here + k) for k in range(here)], axis=1)

    def core_slice(which):
        at = (part - 1) * which
        return lambda y: other_ref[at : at + 1, y, :]

    def emit(low, high):
        for y in range(strip):
            cols = slice(y * row, (y + 1) * row)
            here = vol_ref[:, y, :]
            below = jnp.concatenate([low(y), here[:-1]], axis=0)
            above = jnp.concatenate([here[1:], high(y)], axis=0)
            level = lax.broadcasted_iota(jnp.int32, here.shape, 0)
            down = jnp.clip(here - below, -DELTA, DELTA)
            total = jnp.where((level > 0) | (position > 0), down, 0.0)
            up = jnp.clip(here - above, -DELTA, DELTA)
            total += jnp.where((level < slices - 1) | (position < devices - 1), up, 0.0)
            if y > 0:
                total += jnp.clip(here - vol_ref[:, y - 1, :], -DELTA, DELTA)
            if y + 1 < strip:
                total += jnp.clip(here - vol_ref[:, y + 1, :], -DELTA, DELTA)
            lane = lax.broadcasted_iota(jnp.int32, here.shape, 1)
            left = jnp.clip(here - pltpu.roll(here, 1, 1), -DELTA, DELTA)
            total += jnp.where(lane > 0, left, 0.0)
            right = jnp.clip(here - pltpu.roll(here, row - 1, 1), -DELTA, DELTA)
            total += jnp.where(lane < row - 1, right, 0.0)
            out_ref[:, cols] = PRIOR_WEIGHT * total

    @pl.when((core == 0) & (odd == 0))
    def _():
        emit(chip_slice(far_ref, 1), core_slice(0))

    @pl.when((core == 0) & (odd == 1))
    def _():
        emit(chip_slice(far_ref, 1, far_ref.shape[0] // 2), core_slice(0))

    @pl.when((core == 1) & (odd == 0))
    def _():
        emit(core_slice(1), chip_slice(second_ref, 0))

    @pl.when((core == 1) & (odd == 1))
    def _():
        emit(core_slice(1), chip_slice(first_ref, 0))


def last_kernel(arrived_ref, passed_ref, prior_ref, out_hbm, total, sems):
    part, strip, row = total.shape
    copies = []
    step = part // sems.shape[0]
    for k in range(sems.shape[0]):
        here = slice(k * step, (k + 1) * step)
        for y in range(strip):
            cols = slice(y * row, (y + 1) * row)
            total[here, y, :] = (arrived_ref[here, cols] + passed_ref[here, cols]) + prior_ref[
                here, cols
            ]
        copies.append(pltpu.make_async_copy(total.at[here], out_hbm.at[here], sems.at[k]))
        copies[-1].start()
    for copy in copies:
        copy.wait()


def shards(volume, footprint, measured, angle_index, cover, offset, count):
    local_blocks, slab, strip, row = volume.shape
    views, det_rows, channels = measured.shape
    tables = footprint.shape[0]
    slots = cover.shape[1]
    plane = strip * row
    devices = lax.axis_size(AXES)
    position = lax.axis_index(AXES)
    swap, first, second = exchange_pairs(devices)
    back = lambda pairs: [(b, a) for a, b in pairs]
    send = lambda value, pairs: lax.ppermute(value, AXES, pairs)
    part = local_blocks * slab
    piece = 2 * part
    flat = volume.reshape(part, strip, row)
    table = footprint.reshape(tables, plane, channels)
    vmem = pl.BlockSpec(memory_space=pltpu.VMEM)
    smem = pl.BlockSpec(memory_space=pltpu.SMEM)
    shape = jax.ShapeDtypeStruct
    room = lambda mib: pltpu.CompilerParams(vmem_limit_bytes=mib * 1024 * 1024)
    cost = lambda flops, size: pl.CostEstimate(flops=flops, bytes_accessed=size, transcendentals=0)

    here = lambda: lax.axis_index("grp") * lax.axis_size("view") + lax.axis_index("view")
    hbm = pl.BlockSpec(memory_space=pltpu.HBM)
    stay = lambda value: pltpu.with_memory_space_constraint(value, pltpu.HBM)

    other = send(flat, swap)
    mine, packed = pl.pallas_call(
        load_kernel,
        out_shape=(shape(flat.shape, flat.dtype), shape((part, plane), jnp.bfloat16)),
        in_specs=[hbm],
        out_specs=(vmem, vmem),
        scratch_shapes=[pltpu.SemaphoreType.DMA],
        compiler_params=room(4),
        cost_estimate=cost(1, 1),
        name="load",
    )(stay(flat))
    other, mine, packed = lax.optimization_barrier((other, mine, packed))
    sent = shape((plane // 128 * (piece + 2), 128), jnp.bfloat16)
    for_first, for_second = pl.pallas_call(
        functools.partial(join_kernel, here=here),
        out_shape=(sent, sent),
        in_specs=[vmem] * 3,
        out_specs=(vmem, vmem),
        compiler_params=room(4),
        name="join",
    )(mine, packed, other)
    got_second = send(for_second, second)
    got_first = send(for_first, first)

    sino_shape = shape((channels // 128, views * det_rows, 128), jnp.float32)
    lists_shape = (Pairs.ROWS * Pairs.GROUPS, views * slots)
    table_vmem, turned, lists, sino, decay = pl.pallas_call(
        functools.partial(
            early_kernel,
            piece=piece,
            chips=devices // 2,
            local_blocks=local_blocks,
            slab=slab,
            here=here,
        ),
        out_shape=(
            shape((plane, tables * channels), table.dtype),
            shape((tables * channels, plane), table.dtype),
            shape(lists_shape, jnp.int32),
            sino_shape,
            sino_shape,
        ),
        in_specs=[vmem] + [hbm] * 6,
        out_specs=(vmem,) * 5,
        scratch_shapes=[
            pltpu.VMEM(measured.shape, measured.dtype),
            pltpu.VMEM((slots, views), jnp.int32),
            pltpu.VMEM((slots, views), jnp.int32),
            pltpu.VMEM((1, views), jnp.int32),
            pltpu.VMEM((1, views), jnp.int32),
            pltpu.VMEM((2 * slots + 2, views), jnp.int32),
            pltpu.SMEM((2 * slots + 2, views), jnp.int32),
            pltpu.SMEM(lists_shape, jnp.int32),
            pltpu.SMEM((5 * piece // slab, tables), jnp.int32),
            pltpu.SMEM((5 * piece // slab,), jnp.int32),
            pltpu.SMEM((5 * piece // slab, views * slots), jnp.int32),
            pltpu.VMEM((piece, plane), jnp.bfloat16),
            pltpu.VMEM((piece, tables * channels), jnp.float32),
            pltpu.SemaphoreType.DMA((5 + tables,)),
        ],
        compiler_params=room(16),
        cost_estimate=cost(1, 1),
        name="early",
    )(
        for_second,
        stay(table),
        stay(measured),
        stay(cover.T),
        stay(offset.T),
        stay(count.reshape(1, views)),
        stay(angle_index.reshape(1, views)),
    )
    got_second, got_first, table_vmem, turned, lists, sino, decay = lax.optimization_barrier(
        (got_second, got_first, table_vmem, turned, lists, sino, decay)
    )
    index = [pltpu.SMEM((Pairs.ROWS, views * slots), jnp.int32)]
    waits = [pltpu.SemaphoreType.DMA]
    rows_of = lambda rows: [pltpu.VMEM((rows, tables * channels), jnp.float32)]
    window = [pltpu.VMEM((2 * piece, plane), jnp.bfloat16)]
    picks_of = lambda blocks: [
        pltpu.VMEM(((max(views * slots, blocks) + MORE) * slab, tables * channels), jnp.bfloat16),
        pltpu.VMEM((blocks * slab, plane), jnp.float32),
    ]

    far = send(jnp.concatenate([got_first, got_second], axis=0), swap)
    sino = pl.pallas_call(
        functools.partial(middle_kernel, slab=slab),
        out_shape=sino_shape,
        in_specs=[vmem] * 5,
        out_specs=vmem,
        scratch_shapes=index + window + rows_of(2 * piece) + waits,
        compiler_params=room(16),
        cost_estimate=cost(1, 1),
        name="middle",
    )(lists, got_first, got_second, table_vmem, sino)
    far, sino = lax.optimization_barrier((far, sino))
    sino, give = pl.pallas_call(
        functools.partial(main_kernel, slab=slab),
        out_shape=(sino_shape, shape((2 * piece, plane), jnp.float32)),
        in_specs=[vmem] * 6,
        out_specs=(vmem, vmem),
        scratch_shapes=index + window + rows_of(2 * piece) + picks_of(STATIC) + waits,
        compiler_params=room(16),
        cost_estimate=cost(1, 1),
        name="main",
    )(lists, far, table_vmem, turned, sino, decay)
    taken = send(give, swap)
    keep = pl.pallas_call(
        functools.partial(rest_kernel, group=0, slab=slab),
        out_shape=shape((2 * piece, plane), jnp.float32),
        in_specs=[vmem] * 4,
        out_specs=vmem,
        scratch_shapes=index + picks_of(STATIC) + waits,
        compiler_params=room(16),
        cost_estimate=cost(1, 1),
        name="rest",
    )(lists, turned, sino, decay)
    taken, keep = lax.optimization_barrier((taken, keep))
    wire = (keep + taken).astype(jnp.bfloat16)
    back_second = send(wire[piece:], back(second))
    back_first = send(wire[:piece], back(first))

    home = pl.pallas_call(
        functools.partial(rest_kernel, group=2, slab=slab),
        out_shape=shape((piece, plane), jnp.float32),
        in_specs=[vmem] * 4,
        out_specs=vmem,
        scratch_shapes=index + picks_of(8) + waits,
        compiler_params=room(16),
        cost_estimate=cost(1, 1),
        name="home",
    )(lists, turned, sino, decay)
    prior = pl.pallas_call(
        functools.partial(prior_kernel, devices=devices, here=here),
        out_shape=shape((part, plane), jnp.float32),
        in_specs=[vmem] * 5,
        out_specs=vmem,
        compiler_params=room(8),
        cost_estimate=cost(1, 1),
        name="prior",
    )(mine, other, got_first, got_second, far)
    back_second, back_first, home, prior = lax.optimization_barrier(
        (back_second, back_first, home, prior)
    )

    arrived = (back_second.astype(jnp.float32) + back_first.astype(jnp.float32)) + home
    passed = send(arrived[part:], swap)
    out = pl.pallas_call(
        last_kernel,
        out_shape=shape((part, strip, row), jnp.float32),
        in_specs=[vmem] * 3,
        out_specs=hbm,
        scratch_shapes=[
            pltpu.VMEM((part, strip, row), jnp.float32),
            pltpu.SemaphoreType.DMA((4,)),
        ],
        compiler_params=room(4),
        name="last",
    )(arrived[:part], passed, prior)
    return out.reshape(volume.shape)


def solution(mesh):
    in_specs = (
        P(AXES, None, None, None),
        P(AXES, None, None, None),
        P(AXES, None, None),
        P(AXES),
        P(AXES, None),
        P(AXES, None),
        P(AXES),
    )
    out_specs = P(AXES, None, None, None)
    return jax.shard_map(shards, mesh=mesh, in_specs=in_specs, out_specs=out_specs, check_vma=False)
```

```python
import functools

import jax
import jax.numpy as jnp
from jax import lax
from jax.experimental import pallas as pl
from jax.experimental.pallas import tpu as pltpu
from jax.sharding import PartitionSpec as P

AXES = ("grp", "view")
STATIC = 16
LEVELS = (8, 10, 12)
MORE = 4
DELTA = 0.5
PRIOR_WEIGHT = 2.0


def both_ways(pairs):
    return pairs + [(b, a) for a, b in pairs]


def exchange_pairs(devices):
    chips = devices // 2
    swap = [(i, i ^ 1) for i in range(devices)]
    edge_y = [(i, i + 1) for i in range(0, chips, 2)]
    edge_d = [(i, i + 1) for i in range(1, chips - 1, 2)]
    edge_a = [(i + j, i + j + 2) for i in range(0, chips, 4) for j in (0, 1)]
    edge_b = [(i + j, i + j + 2) for i in range(2, chips - 2, 4) for j in (0, 1)]
    idle = [(0, 1), (chips - 2, chips - 1)]
    on_core = lambda edges, core: [(2 * a + core, 2 * b + core) for a, b in edges]
    last = devices - 1
    ends = [(0, 4), (4, 1), (1, 0), (last - 1, last - 5), (last - 5, last), (last, last - 1)]
    first = both_ways(on_core(edge_a[1:-1], 0) + on_core(edge_d, 1)) + ends
    second = both_ways(on_core(edge_b + idle, 0) + on_core(edge_y, 1))
    return swap, first, second


def load_kernel(source, target, own_ref, sem):
    copy = pltpu.make_async_copy(source, target, sem)
    copy.start()
    copy.wait()
    strip, row = target.shape[1:]
    for y in range(strip):
        own_ref[:, y * row : (y + 1) * row] = target[:, y, :].astype(jnp.bfloat16)


def join_kernel(mine_ref, own_ref, other_ref, first_ref, second_ref, *, here):
    slices, strip, row = other_ref.shape
    tiles = strip * row // 128
    part = slices
    rest = {}
    for name, ref in (("mine", mine_ref), ("other", other_ref)):
        for at in (0, slices - 1):
            for y in range(strip):
                whole = ref[at : at + 1, y, :]
                left = whole - whole.astype(jnp.bfloat16).astype(jnp.float32)
                mid = left.astype(jnp.bfloat16).astype(jnp.float32)
                rest[name, at, y] = (mid, left - mid)
    position = here()
    core = lax.rem(position, 2)
    odd = lax.rem(position // 2, 2)
    for y in range(strip):
        packed = other_ref[:, y, :].astype(jnp.bfloat16)
        for k in range(row // 128):
            tile = y * (row // 128) + k
            cols = slice(k * 128, (k + 1) * 128)
            for ref in (first_ref, second_ref):
                ref[tile * 2 * part : tile * 2 * part + part, :] = own_ref[
                    :, tile * 128 : (tile + 1) * 128
                ]
                ref[tile * 2 * part + part : (tile + 1) * 2 * part, :] = packed[:, cols]
    top, bottom = [], []
    for y in range(strip):
        for k in range(row // 128):
            cols = slice(k * 128, (k + 1) * 128)
            for which in range(2):
                a = rest["mine", 0, y][which][:, cols]
                b = rest["other", 0, y][which][:, cols]
                top.append(jnp.where(core == 0, a, b))
                a = rest["mine", slices - 1, y][which][:, cols]
                b = rest["other", slices - 1, y][which][:, cols]
                bottom.append(jnp.where(core == 1, a, b))
    top = jnp.concatenate(top, axis=0)
    bottom = jnp.concatenate(bottom, axis=0)
    tail = slice(tiles * 2 * part, tiles * 2 * part + 2 * tiles)
    first_ref[tail, :] = jnp.where(odd == 1, bottom, top).astype(jnp.bfloat16)
    second_ref[tail, :] = jnp.where(odd == 1, top, bottom).astype(jnp.bfloat16)


def unfold(ref, begin, window, first_row, piece):
    for j in range(window.shape[1] // 128):
        window[first_row : first_row + piece, j * 128 : (j + 1) * 128] = ref[
            begin + j * piece : begin + (j + 1) * piece, :
        ]


def window_rows(block, position, chips, local_blocks, slab):
    part = local_blocks * slab
    piece = 2 * part
    core = lax.rem(position, 2)
    chip = position // 2
    owner = block // local_blocks
    owner_core = lax.rem(owner, 2)
    delta = owner // 2 - chip
    flag = lambda what: jnp.where(what, 1, 0)
    up = flag(delta > 0)
    nearer = jnp.abs(delta) == 1
    is_y = flag(up == 1 - lax.rem(chip, 2))
    is_a = flag(up == flag(lax.rem(chip, 4) < 2))
    second = jnp.where(nearer, is_y, 1 - is_a)
    via = flag(nearer)
    end = flag((chip == 0) | (chip == chips - 1))
    held = jnp.where(nearer, 1, is_a * end)
    away = (2 * jnp.abs(held - core) + second) * piece + jnp.abs(owner_core - via) * part
    here = 4 * piece + jnp.abs(owner_core - core) * part
    return jnp.where(delta == 0, here, away) + lax.rem(block, local_blocks) * slab


class Pairs:
    ROWS = 8
    GROUPS = 3

    def __init__(self, ref, first=0):
        self.ref = ref
        self.first = first

    def each(self, do):
        def body(i, carry):
            do(*(self.ref[self.first + k, i] for k in range(4)))
            return carry

        lax.fori_loop(0, self.ref[self.first + 5, 0], body, 0)

    def gathered(self):
        return self.ref[self.first + 5, 1]

    def target(self, i):
        return self.ref[self.first + 4, i]


def list_pairs(scal, lists, seen, height, held, near_rows, det_rows, tables, slab):
    slots = (scal.shape[0] - 2) // 2
    most = held.shape[1]
    fields, groups = Pairs.ROWS, Pairs.GROUPS

    def clear(i, carry):
        height[i] = jnp.int32(0)
        for table in range(tables):
            seen[i, table] = jnp.int32(0)
        return carry

    lax.fori_loop(0, height.shape[0], clear, 0)
    for k in range(groups):
        lists[fields * k + 5, 0] = jnp.int32(0)
        lists[fields * k + 5, 1] = jnp.int32(0)

    def body(view, carry):
        count = scal[2 * slots, view]
        table = scal[2 * slots + 1, view]
        for slot in range(slots):

            @pl.when(slot < count)
            def _():
                row = scal[slot, view]
                block = row // slab
                group = jnp.minimum(row // near_rows, groups - 1)
                local = row - group * near_rows
                first = fields * group
                at = lists[first + 5, 0]
                used = lists[first + 5, 1]
                rank = seen[block, table]
                top = height[block]
                fresh = rank >= top
                mine = jnp.where(fresh, used, held[block, rank])
                held[block, rank] = mine
                seen[block, table] = rank + 1
                height[block] = jnp.where(fresh, rank + 1, top)
                lists[first, at] = view * det_rows + scal[slots + slot, view]
                lists[first + 1, at] = table
                lists[first + 2, at] = local
                lists[first + 3, at] = mine * slab
                lists[first + 4, mine] = local
                lists[first + 5, 0] = at + 1
                lists[first + 5, 1] = used + jnp.where(fresh, 1, 0)

        return carry

    lax.fori_loop(0, scal.shape[1], body, 0)


def place(pairs, sino, proj, slab):
    width = sino.shape[0] * 128

    def add(target, table, local, dest):
        source = pl.ds(pl.multiple_of(local, slab), slab)
        for tile in range(sino.shape[0]):
            cols = pl.ds(pl.multiple_of(table * width + tile * 128, 128), 128)
            sino[tile, pl.ds(target, slab), :] += proj[source, cols]

    pairs.each(add)


def clear_rows(picked, static_rows):
    picked[0:static_rows, :] = jnp.zeros((static_rows, picked.shape[1]), picked.dtype)


def gather(pairs, sino, decay, picked, static_rows, slab):
    width = sino.shape[0] * 128
    chunk = MORE * slab

    def clear(i, carry):
        here = pl.ds(pl.multiple_of(static_rows + i * chunk, chunk), chunk)
        picked[here, :] = jnp.zeros((chunk, picked.shape[1]), picked.dtype)
        return carry

    more = pairs.gathered() * slab - static_rows
    lax.fori_loop(0, (more + chunk - 1) // chunk, clear, 0)

    def take(source, table, local, dest):
        target = pl.ds(pl.multiple_of(dest, slab), slab)
        here = pl.ds(source, slab)
        for tile in range(sino.shape[0]):
            cols = pl.ds(pl.multiple_of(table * width + tile * 128, 128), 128)
            value = decay[tile, here, :] * sino[tile, here, :]
            picked[target, cols] = value.astype(jnp.bfloat16)

    pairs.each(take)


def back_project(pairs, picked, turned_ref, spread, out_ref, slab):
    static_rows = spread.shape[0]
    static = static_rows // slab
    blocks = pairs.gathered()
    out_ref[...] = jnp.zeros_like(out_ref)

    def add_from(begin):
        def add(i, carry):
            target = pl.ds(pl.multiple_of(pairs.target(i), slab), slab)
            source = pl.ds(pl.multiple_of((i - begin) * slab, slab), slab)
            out_ref[target, :] += spread[source, :]
            return carry

        return add

    least = -1
    for most in [m for m in LEVELS if m < static] + [static]:
        rows = most * slab

        @pl.when((blocks > least) & ((blocks <= most) | (most == static)))
        def _():
            spread[0:rows, :] = jnp.dot(
                picked[0:rows, :], turned_ref[...], preferred_element_type=jnp.float32
            )

        least = most
    lax.fori_loop(0, jnp.minimum(blocks, static), add_from(0), 0)

    def further(c, carry):
        begin = static + c * MORE
        here = pl.ds(pl.multiple_of(begin * slab, MORE * slab), MORE * slab)
        spread[0 : MORE * slab, :] = jnp.dot(
            picked[here, :], turned_ref[...], preferred_element_type=jnp.float32
        )
        lax.fori_loop(begin, jnp.minimum(blocks, begin + MORE), add_from(begin), 0)
        return carry

    lax.fori_loop(0, (blocks - static + MORE - 1) // MORE, further, 0)


def early_kernel(
    both_ref,
    table_hbm,
    measured_hbm,
    cover_hbm,
    offset_hbm,
    count_hbm,
    angle_hbm,
    table_ref,
    turned_ref,
    lists_ref,
    sino_ref,
    decay_ref,
    measured,
    cover,
    offset,
    count,
    angle,
    index,
    scal,
    lists,
    seen,
    height,
    held,
    window,
    proj,
    sems,
    *,
    piece,
    chips,
    local_blocks,
    slab,
    here,
):
    views, det_rows, channels = measured.shape
    slots = cover.shape[0]
    tables = table_hbm.shape[0]
    small = [(cover_hbm, cover), (offset_hbm, offset), (count_hbm, count), (angle_hbm, angle)]
    unfold(both_ref, 0, window, 0, piece)
    copies = [pltpu.make_async_copy(a, b, sems.at[i]) for i, (a, b) in enumerate(small)]
    copies.append(pltpu.make_async_copy(measured_hbm, measured, sems.at[4]))
    for table in range(tables):
        to = table_ref.at[:, table * channels : (table + 1) * channels]
        copies.append(pltpu.make_async_copy(table_hbm.at[table], to, sems.at[5 + table]))
    for copy in copies:
        copy.start()
    for copy in copies[:4]:
        copy.wait()
    index[0:slots, :] = window_rows(cover[...], here(), chips, local_blocks, slab)
    index[slots : 2 * slots, :] = offset[...]
    index[2 * slots : 2 * slots + 1, :] = count[...]
    index[2 * slots + 1 : 2 * slots + 2, :] = angle[...]
    load = fetch(index, scal, sems.at[0])
    copies[4].wait()

    def fade(view, carry):
        rows = pl.ds(pl.multiple_of(view * det_rows, det_rows), det_rows)
        for tile in range(sino_ref.shape[0]):
            value = measured[view, :, tile * 128 : (tile + 1) * 128].astype(jnp.float32)
            decay_ref[tile, rows, :] = jnp.exp(-value)
            sino_ref[tile, rows, :] = -value
        return carry

    lax.fori_loop(0, views, fade, 0)
    load.wait()
    list_pairs(scal, lists, seen, height, held, 2 * piece, det_rows, tables, slab)
    save = fetch(lists, lists_ref, sems.at[0])
    for table in range(tables):
        copies[5 + table].wait()
        cols = slice(table * channels, (table + 1) * channels)
        turned_ref[cols, :] = table_ref[:, cols].T
    proj[...] = jnp.dot(window[...], table_ref[...], preferred_element_type=jnp.float32)
    place(Pairs(lists, 2 * Pairs.ROWS), sino_ref, proj, slab)
    save.wait()


def fetch_group(lists_ref, group, lists, sem):
    return fetch(lists_ref.at[pl.ds(group * Pairs.ROWS, Pairs.ROWS)], lists, sem)


def fetch(source, target, sem):
    load = pltpu.make_async_copy(source, target, sem)
    load.start()
    return load


def project(load, lists, window, table_ref, begun_ref, sino_ref, proj, slab):
    sino_ref[...] = begun_ref[...]
    proj[...] = jnp.dot(window[...], table_ref[...], preferred_element_type=jnp.float32)
    load.wait()
    place(Pairs(lists), sino_ref, proj, slab)


def middle_kernel(
    lists_ref, first_ref, second_ref, table_ref, begun_ref, sino_ref, lists, window, proj, sem, *, slab
):
    load = fetch_group(lists_ref, 0, lists, sem)
    piece = proj.shape[0] // 2
    for k, ref in enumerate((first_ref, second_ref)):
        unfold(ref, 0, window, k * piece, piece)
    project(load, lists, window, table_ref, begun_ref, sino_ref, proj, slab)


def main_kernel(
    lists_ref,
    far_ref,
    table_ref,
    turned_ref,
    begun_ref,
    decay_ref,
    sino_ref,
    give_ref,
    lists,
    window,
    proj,
    picked,
    spread,
    sem,
    *,
    slab,
):
    load = fetch_group(lists_ref, 1, lists, sem)
    clear_rows(picked, spread.shape[0])
    piece = proj.shape[0] // 2
    for k in range(2):
        unfold(far_ref, k * far_ref.shape[0] // 2, window, k * piece, piece)
    project(load, lists, window, table_ref, begun_ref, sino_ref, proj, slab)
    pairs = Pairs(lists)
    gather(pairs, sino_ref, decay_ref, picked, spread.shape[0], slab)
    back_project(pairs, picked, turned_ref, spread, give_ref, slab)


def rest_kernel(
    lists_ref, turned_ref, sino_ref, decay_ref, out_ref, lists, picked, spread, sem, *, group, slab
):
    load = fetch_group(lists_ref, group, lists, sem)
    clear_rows(picked, spread.shape[0])
    load.wait()
    pairs = Pairs(lists)
    gather(pairs, sino_ref, decay_ref, picked, spread.shape[0], slab)
    back_project(pairs, picked, turned_ref, spread, out_ref, slab)


def prior_kernel(
    vol_ref, other_ref, first_ref, second_ref, far_ref, out_ref, *, devices, here
):
    slices, strip, row = vol_ref.shape
    part = slices
    piece = 2 * part
    position = here()
    core = lax.rem(position, 2)
    odd = lax.rem(position // 2, 2)

    def chip_slice(ref, which, base=0):
        at = part if which == 0 else part - 1
        tiles = strip * row // 128

        def column(tile):
            whole = ref[base + tile * piece + at : base + tile * piece + at + 1, :]
            tail = base + tiles * piece + 2 * tile
            mid, low = ref[tail : tail + 1, :], ref[tail + 1 : tail + 2, :]
            return whole.astype(jnp.float32) + (mid.astype(jnp.float32) + low.astype(jnp.float32))

        here = row // 128
        return lambda y: jnp.concatenate([column(y * here + k) for k in range(here)], axis=1)

    def core_slice(which):
        at = (part - 1) * which
        return lambda y: other_ref[at : at + 1, y, :]

    def emit(low, high):
        for y in range(strip):
            cols = slice(y * row, (y + 1) * row)
            here = vol_ref[:, y, :]
            below = jnp.concatenate([low(y), here[:-1]], axis=0)
            above = jnp.concatenate([here[1:], high(y)], axis=0)
            level = lax.broadcasted_iota(jnp.int32, here.shape, 0)
            down = jnp.clip(here - below, -DELTA, DELTA)
            total = jnp.where((level > 0) | (position > 0), down, 0.0)
            up = jnp.clip(here - above, -DELTA, DELTA)
            total += jnp.where((level < slices - 1) | (position < devices - 1), up, 0.0)
            if y > 0:
                total += jnp.clip(here - vol_ref[:, y - 1, :], -DELTA, DELTA)
            if y + 1 < strip:
                total += jnp.clip(here - vol_ref[:, y + 1, :], -DELTA, DELTA)
            lane = lax.broadcasted_iota(jnp.int32, here.shape, 1)
            left = jnp.clip(here - pltpu.roll(here, 1, 1), -DELTA, DELTA)
            total += jnp.where(lane > 0, left, 0.0)
            right = jnp.clip(here - pltpu.roll(here, row - 1, 1), -DELTA, DELTA)
            total += jnp.where(lane < row - 1, right, 0.0)
            out_ref[:, cols] = PRIOR_WEIGHT * total

    @pl.when((core == 0) & (odd == 0))
    def _():
        emit(chip_slice(far_ref, 1), core_slice(0))

    @pl.when((core == 0) & (odd == 1))
    def _():
        emit(chip_slice(far_ref, 1, far_ref.shape[0] // 2), core_slice(0))

    @pl.when((core == 1) & (odd == 0))
    def _():
        emit(core_slice(1), chip_slice(second_ref, 0))

    @pl.when((core == 1) & (odd == 1))
    def _():
        emit(core_slice(1), chip_slice(first_ref, 0))


def last_kernel(arrived_ref, passed_ref, prior_ref, out_hbm, total, sems):
    part, strip, row = total.shape
    copies = []
    step = part // sems.shape[0]
    for k in range(sems.shape[0]):
        here = slice(k * step, (k + 1) * step)
        for y in range(strip):
            cols = slice(y * row, (y + 1) * row)
            total[here, y, :] = (arrived_ref[here, cols] + passed_ref[here, cols]) + prior_ref[
                here, cols
            ]
        copies.append(pltpu.make_async_copy(total.at[here], out_hbm.at[here], sems.at[k]))
        copies[-1].start()
    for copy in copies:
        copy.wait()


def shards(volume, footprint, measured, angle_index, cover, offset, count):
    local_blocks, slab, strip, row = volume.shape
    views, det_rows, channels = measured.shape
    tables = footprint.shape[0]
    slots = cover.shape[1]
    plane = strip * row
    devices = lax.axis_size(AXES)
    position = lax.axis_index(AXES)
    swap, first, second = exchange_pairs(devices)
    back = lambda pairs: [(b, a) for a, b in pairs]
    send = lambda value, pairs: lax.ppermute(value, AXES, pairs)
    part = local_blocks * slab
    piece = 2 * part
    flat = volume.reshape(part, strip, row)
    table = footprint.reshape(tables, plane, channels)
    vmem = pl.BlockSpec(memory_space=pltpu.VMEM)
    smem = pl.BlockSpec(memory_space=pltpu.SMEM)
    shape = jax.ShapeDtypeStruct
    room = lambda mib: pltpu.CompilerParams(vmem_limit_bytes=mib * 1024 * 1024)
    cost = lambda flops, size: pl.CostEstimate(flops=flops, bytes_accessed=size, transcendentals=0)

    here = lambda: lax.axis_index("grp") * lax.axis_size("view") + lax.axis_index("view")
    hbm = pl.BlockSpec(memory_space=pltpu.HBM)
    stay = lambda value: pltpu.with_memory_space_constraint(value, pltpu.HBM)

    other = send(flat, swap)
    mine, packed = pl.pallas_call(
        load_kernel,
        out_shape=(shape(flat.shape, flat.dtype), shape((part, plane), jnp.bfloat16)),
        in_specs=[hbm],
        out_specs=(vmem, vmem),
        scratch_shapes=[pltpu.SemaphoreType.DMA],
        compiler_params=room(4),
        cost_estimate=cost(1, 1),
        name="load",
    )(stay(flat))
    other, mine, packed = lax.optimization_barrier((other, mine, packed))
    sent = shape((plane // 128 * (piece + 2), 128), jnp.bfloat16)
    for_first, for_second = pl.pallas_call(
        functools.partial(join_kernel, here=here),
        out_shape=(sent, sent),
        in_specs=[vmem] * 3,
        out_specs=(vmem, vmem),
        compiler_params=room(4),
        name="join",
    )(mine, packed, other)
    got_second = send(for_second, second)
    got_first = send(for_first, first)

    sino_shape = shape((channels // 128, views * det_rows, 128), jnp.float32)
    lists_shape = (Pairs.ROWS * Pairs.GROUPS, views * slots)
    table_vmem, turned, lists, sino, decay = pl.pallas_call(
        functools.partial(
            early_kernel,
            piece=piece,
            chips=devices // 2,
            local_blocks=local_blocks,
            slab=slab,
            here=here,
        ),
        out_shape=(
            shape((plane, tables * channels), table.dtype),
            shape((tables * channels, plane), table.dtype),
            shape(lists_shape, jnp.int32),
            sino_shape,
            sino_shape,
        ),
        in_specs=[vmem] + [hbm] * 6,
        out_specs=(vmem,) * 5,
        scratch_shapes=[
            pltpu.VMEM(measured.shape, measured.dtype),
            pltpu.VMEM((slots, views), jnp.int32),
            pltpu.VMEM((slots, views), jnp.int32),
            pltpu.VMEM((1, views), jnp.int32),
            pltpu.VMEM((1, views), jnp.int32),
            pltpu.VMEM((2 * slots + 2, views), jnp.int32),
            pltpu.SMEM((2 * slots + 2, views), jnp.int32),
            pltpu.SMEM(lists_shape, jnp.int32),
            pltpu.SMEM((5 * piece // slab, tables), jnp.int32),
            pltpu.SMEM((5 * piece // slab,), jnp.int32),
            pltpu.SMEM((5 * piece // slab, views * slots), jnp.int32),
            pltpu.VMEM((piece, plane), jnp.bfloat16),
            pltpu.VMEM((piece, tables * channels), jnp.float32),
            pltpu.SemaphoreType.DMA((5 + tables,)),
        ],
        compiler_params=room(16),
        cost_estimate=cost(1, 1),
        name="early",
    )(
        for_second,
        stay(table),
        stay(measured),
        stay(cover.T),
        stay(offset.T),
        stay(count.reshape(1, views)),
        stay(angle_index.reshape(1, views)),
    )
    got_second, got_first, table_vmem, turned, lists, sino, decay = lax.optimization_barrier(
        (got_second, got_first, table_vmem, turned, lists, sino, decay)
    )
    index = [pltpu.SMEM((Pairs.ROWS, views * slots), jnp.int32)]
    waits = [pltpu.SemaphoreType.DMA]
    rows_of = lambda rows: [pltpu.VMEM((rows, tables * channels), jnp.float32)]
    window = [pltpu.VMEM((2 * piece, plane), jnp.bfloat16)]
    picks_of = lambda blocks: [
        pltpu.VMEM(((max(views * slots, blocks) + MORE) * slab, tables * channels), jnp.bfloat16),
        pltpu.VMEM((blocks * slab, plane), jnp.float32),
    ]

    far = send(jnp.concatenate([got_first, got_second], axis=0), swap)
    sino = pl.pallas_call(
        functools.partial(middle_kernel, slab=slab),
        out_shape=sino_shape,
        in_specs=[vmem] * 5,
        out_specs=vmem,
        scratch_shapes=index + window + rows_of(2 * piece) + waits,
        compiler_params=room(16),
        cost_estimate=cost(1, 1),
        name="middle",
    )(lists, got_first, got_second, table_vmem, sino)
    far, sino = lax.optimization_barrier((far, sino))
    sino, give = pl.pallas_call(
        functools.partial(main_kernel, slab=slab),
        out_shape=(sino_shape, shape((2 * piece, plane), jnp.float32)),
        in_specs=[vmem] * 6,
        out_specs=(vmem, vmem),
        scratch_shapes=index + window + rows_of(2 * piece) + picks_of(STATIC) + waits,
        compiler_params=room(16),
        cost_estimate=cost(1, 1),
        name="main",
    )(lists, far, table_vmem, turned, sino, decay)
    taken = send(give, swap)
    keep = pl.pallas_call(
        functools.partial(rest_kernel, group=0, slab=slab),
        out_shape=shape((2 * piece, plane), jnp.float32),
        in_specs=[vmem] * 4,
        out_specs=vmem,
        scratch_shapes=index + picks_of(STATIC) + waits,
        compiler_params=room(16),
        cost_estimate=cost(1, 1),
        name="rest",
    )(lists, turned, sino, decay)
    taken, keep = lax.optimization_barrier((taken, keep))
    wire = lambda rows: (keep[rows] + taken[rows]).astype(jnp.bfloat16)
    back_second = send(wire(slice(piece, 2 * piece)), back(second))
    back_first = send(wire(slice(0, piece)), back(first))

    home = pl.pallas_call(
        functools.partial(rest_kernel, group=2, slab=slab),
        out_shape=shape((piece, plane), jnp.float32),
        in_specs=[vmem] * 4,
        out_specs=vmem,
        scratch_shapes=index + picks_of(8) + waits,
        compiler_params=room(16),
        cost_estimate=cost(1, 1),
        name="home",
    )(lists, turned, sino, decay)
    prior = pl.pallas_call(
        functools.partial(prior_kernel, devices=devices, here=here),
        out_shape=shape((part, plane), jnp.float32),
        in_specs=[vmem] * 5,
        out_specs=vmem,
        compiler_params=room(8),
        cost_estimate=cost(1, 1),
        name="prior",
    )(mine, other, got_first, got_second, far)
    back_second, back_first, home, prior = lax.optimization_barrier(
        (back_second, back_first, home, prior)
    )

    arrived = lambda rows: (
        back_second[rows].astype(jnp.float32) + back_first[rows].astype(jnp.float32)
    ) + home[rows]
    passed = send(arrived(slice(part, piece)), swap)
    out = pl.pallas_call(
        last_kernel,
        out_shape=shape((part, strip, row), jnp.float32),
        in_specs=[vmem] * 3,
        out_specs=hbm,
        scratch_shapes=[
            pltpu.VMEM((part, strip, row), jnp.float32),
            pltpu.SemaphoreType.DMA((4,)),
        ],
        compiler_params=room(4),
        name="last",
    )(arrived(slice(0, part)), passed, prior)
    return out.reshape(volume.shape)


def solution(mesh):
    in_specs = (
        P(AXES, None, None, None),
        P(AXES, None, None, None),
        P(AXES, None, None),
        P(AXES),
        P(AXES, None),
        P(AXES, None),
        P(AXES),
    )
    out_specs = P(AXES, None, None, None)
    return jax.shard_map(shards, mesh=mesh, in_specs=in_specs, out_specs=out_specs, check_vma=False)
```

```python
import functools

import jax
import jax.numpy as jnp
from jax import lax
from jax.experimental import pallas as pl
from jax.experimental.pallas import tpu as pltpu
from jax.sharding import PartitionSpec as P

AXES = ("grp", "view")
STATIC = 16
LEVELS = (8, 10, 12)
MORE = 4
DELTA = 0.5
PRIOR_WEIGHT = 2.0


def both_ways(pairs):
    return pairs + [(b, a) for a, b in pairs]


def exchange_pairs(devices):
    chips = devices // 2
    swap = [(i, i ^ 1) for i in range(devices)]
    edge_y = [(i, i + 1) for i in range(0, chips, 2)]
    edge_d = [(i, i + 1) for i in range(1, chips - 1, 2)]
    edge_a = [(i + j, i + j + 2) for i in range(0, chips, 4) for j in (0, 1)]
    edge_b = [(i + j, i + j + 2) for i in range(2, chips - 2, 4) for j in (0, 1)]
    idle = [(0, 1), (chips - 2, chips - 1)]
    on_core = lambda edges, core: [(2 * a + core, 2 * b + core) for a, b in edges]
    last = devices - 1
    ends = [(0, 4), (4, 1), (1, 0), (last - 1, last - 5), (last - 5, last), (last, last - 1)]
    first = both_ways(on_core(edge_a[1:-1], 0) + on_core(edge_d, 1)) + ends
    second = both_ways(on_core(edge_b + idle, 0) + on_core(edge_y, 1))
    return swap, first, second


def load_kernel(source, target, own_ref, sem):
    copy = pltpu.make_async_copy(source, target, sem)
    copy.start()
    copy.wait()
    strip, row = target.shape[1:]
    for y in range(strip):
        own_ref[:, y * row : (y + 1) * row] = target[:, y, :].astype(jnp.bfloat16)


def join_kernel(mine_ref, own_ref, other_ref, first_ref, second_ref, *, here):
    slices, strip, row = other_ref.shape
    tiles = strip * row // 128
    part = slices
    rest = {}
    for name, ref in (("mine", mine_ref), ("other", other_ref)):
        for at in (0, slices - 1):
            for y in range(strip):
                whole = ref[at : at + 1, y, :]
                left = whole - whole.astype(jnp.bfloat16).astype(jnp.float32)
                mid = left.astype(jnp.bfloat16).astype(jnp.float32)
                rest[name, at, y] = (mid, left - mid)
    position = here()
    core = lax.rem(position, 2)
    odd = lax.rem(position // 2, 2)
    for y in range(strip):
        packed = other_ref[:, y, :].astype(jnp.bfloat16)
        for k in range(row // 128):
            tile = y * (row // 128) + k
            cols = slice(k * 128, (k + 1) * 128)
            for ref in (first_ref, second_ref):
                ref[tile * 2 * part : tile * 2 * part + part, :] = own_ref[
                    :, tile * 128 : (tile + 1) * 128
                ]
                ref[tile * 2 * part + part : (tile + 1) * 2 * part, :] = packed[:, cols]
    top, bottom = [], []
    for y in range(strip):
        for k in range(row // 128):
            cols = slice(k * 128, (k + 1) * 128)
            for which in range(2):
                a = rest["mine", 0, y][which][:, cols]
                b = rest["other", 0, y][which][:, cols]
                top.append(jnp.where(core == 0, a, b))
                a = rest["mine", slices - 1, y][which][:, cols]
                b = rest["other", slices - 1, y][which][:, cols]
                bottom.append(jnp.where(core == 1, a, b))
    top = jnp.concatenate(top, axis=0)
    bottom = jnp.concatenate(bottom, axis=0)
    tail = slice(tiles * 2 * part, tiles * 2 * part + 2 * tiles)
    first_ref[tail, :] = jnp.where(odd == 1, bottom, top).astype(jnp.bfloat16)
    second_ref[tail, :] = jnp.where(odd == 1, top, bottom).astype(jnp.bfloat16)


def unfold(ref, begin, window, first_row, piece):
    for j in range(window.shape[1] // 128):
        window[first_row : first_row + piece, j * 128 : (j + 1) * 128] = ref[
            begin + j * piece : begin + (j + 1) * piece, :
        ]


def window_rows(block, position, chips, local_blocks, slab):
    part = local_blocks * slab
    piece = 2 * part
    core = lax.rem(position, 2)
    chip = position // 2
    owner = block // local_blocks
    owner_core = lax.rem(owner, 2)
    delta = owner // 2 - chip
    flag = lambda what: jnp.where(what, 1, 0)
    up = flag(delta > 0)
    nearer = jnp.abs(delta) == 1
    is_y = flag(up == 1 - lax.rem(chip, 2))
    is_a = flag(up == flag(lax.rem(chip, 4) < 2))
    second = jnp.where(nearer, is_y, 1 - is_a)
    via = flag(nearer)
    end = flag((chip == 0) | (chip == chips - 1))
    held = jnp.where(nearer, 1, is_a * end)
    away = (2 * jnp.abs(held - core) + second) * piece + jnp.abs(owner_core - via) * part
    here = 4 * piece + jnp.abs(owner_core - core) * part
    return jnp.where(delta == 0, here, away) + lax.rem(block, local_blocks) * slab


class Pairs:
    ROWS = 8
    GROUPS = 3

    def __init__(self, ref, first=0):
        self.ref = ref
        self.first = first

    def each(self, do):
        def body(i, carry):
            do(*(self.ref[self.first + k, i] for k in range(4)))
            return carry

        lax.fori_loop(0, self.ref[self.first + 5, 0], body, 0)

    def gathered(self):
        return self.ref[self.first + 5, 1]

    def target(self, i):
        return self.ref[self.first + 4, i]


def list_pairs(scal, lists, seen, height, held, near_rows, det_rows, tables, slab):
    slots = (scal.shape[0] - 2) // 2
    most = held.shape[1]
    fields, groups = Pairs.ROWS, Pairs.GROUPS

    def clear(i, carry):
        height[i] = jnp.int32(0)
        for table in range(tables):
            seen[i, table] = jnp.int32(0)
        return carry

    lax.fori_loop(0, height.shape[0], clear, 0)
    for k in range(groups):
        lists[fields * k + 5, 0] = jnp.int32(0)
        lists[fields * k + 5, 1] = jnp.int32(0)

    def body(view, carry):
        count = scal[2 * slots, view]
        table = scal[2 * slots + 1, view]
        for slot in range(slots):

            @pl.when(slot < count)
            def _():
                row = scal[slot, view]
                block = row // slab
                group = jnp.minimum(row // near_rows, groups - 1)
                local = row - group * near_rows
                first = fields * group
                at = lists[first + 5, 0]
                used = lists[first + 5, 1]
                rank = seen[block, table]
                top = height[block]
                fresh = rank >= top
                mine = jnp.where(fresh, used, held[block, rank])
                held[block, rank] = mine
                seen[block, table] = rank + 1
                height[block] = jnp.where(fresh, rank + 1, top)
                lists[first, at] = view * det_rows + scal[slots + slot, view]
                lists[first + 1, at] = table
                lists[first + 2, at] = local
                lists[first + 3, at] = mine * slab
                lists[first + 4, mine] = local
                lists[first + 5, 0] = at + 1
                lists[first + 5, 1] = used + jnp.where(fresh, 1, 0)

        return carry

    lax.fori_loop(0, scal.shape[1], body, 0)


def place(pairs, sino, proj, slab):
    width = sino.shape[0] * 128

    def add(target, table, local, dest):
        source = pl.ds(pl.multiple_of(local, slab), slab)
        for tile in range(sino.shape[0]):
            cols = pl.ds(pl.multiple_of(table * width + tile * 128, 128), 128)
            sino[tile, pl.ds(target, slab), :] += proj[source, cols]

    pairs.each(add)


def clear_rows(picked, static_rows):
    picked[0:static_rows, :] = jnp.zeros((static_rows, picked.shape[1]), picked.dtype)


def gather(pairs, sino, decay, picked, static_rows, slab):
    width = sino.shape[0] * 128
    chunk = MORE * slab

    def clear(i, carry):
        here = pl.ds(pl.multiple_of(static_rows + i * chunk, chunk), chunk)
        picked[here, :] = jnp.zeros((chunk, picked.shape[1]), picked.dtype)
        return carry

    more = pairs.gathered() * slab - static_rows
    lax.fori_loop(0, (more + chunk - 1) // chunk, clear, 0)

    def take(source, table, local, dest):
        target = pl.ds(pl.multiple_of(dest, slab), slab)
        here = pl.ds(source, slab)
        for tile in range(sino.shape[0]):
            cols = pl.ds(pl.multiple_of(table * width + tile * 128, 128), 128)
            value = decay[tile, here, :] * sino[tile, here, :]
            picked[target, cols] = value.astype(jnp.bfloat16)

    pairs.each(take)


def back_project(pairs, picked, turned_ref, spread, out_ref, slab):
    static_rows = spread.shape[0]
    static = static_rows // slab
    blocks = pairs.gathered()
    out_ref[...] = jnp.zeros_like(out_ref)

    def add_from(begin):
        def add(i, carry):
            target = pl.ds(pl.multiple_of(pairs.target(i), slab), slab)
            source = pl.ds(pl.multiple_of((i - begin) * slab, slab), slab)
            out_ref[target, :] += spread[source, :]
            return carry

        return add

    least = -1
    for most in [m for m in LEVELS if m < static] + [static]:
        rows = most * slab

        @pl.when((blocks > least) & ((blocks <= most) | (most == static)))
        def _():
            spread[0:rows, :] = jnp.dot(
                picked[0:rows, :], turned_ref[...], preferred_element_type=jnp.float32
            )

        least = most
    lax.fori_loop(0, jnp.minimum(blocks, static), add_from(0), 0)

    def further(c, carry):
        begin = static + c * MORE
        here = pl.ds(pl.multiple_of(begin * slab, MORE * slab), MORE * slab)
        spread[0 : MORE * slab, :] = jnp.dot(
            picked[here, :], turned_ref[...], preferred_element_type=jnp.float32
        )
        lax.fori_loop(begin, jnp.minimum(blocks, begin + MORE), add_from(begin), 0)
        return carry

    lax.fori_loop(0, (blocks - static + MORE - 1) // MORE, further, 0)


def early_kernel(
    both_ref,
    table_hbm,
    measured_hbm,
    cover_hbm,
    offset_hbm,
    count_hbm,
    angle_hbm,
    table_ref,
    turned_ref,
    lists_ref,
    sino_ref,
    decay_ref,
    measured,
    cover,
    offset,
    count,
    angle,
    index,
    scal,
    lists,
    seen,
    height,
    held,
    window,
    proj,
    sems,
    *,
    piece,
    chips,
    local_blocks,
    slab,
    here,
):
    views, det_rows, channels = measured.shape
    slots = cover.shape[0]
    tables = table_hbm.shape[0]
    small = [(cover_hbm, cover), (offset_hbm, offset), (count_hbm, count), (angle_hbm, angle)]
    unfold(both_ref, 0, window, 0, piece)
    copies = [pltpu.make_async_copy(a, b, sems.at[i]) for i, (a, b) in enumerate(small)]
    copies.append(pltpu.make_async_copy(measured_hbm, measured, sems.at[4]))
    for table in range(tables):
        to = table_ref.at[:, table * channels : (table + 1) * channels]
        copies.append(pltpu.make_async_copy(table_hbm.at[table], to, sems.at[5 + table]))
    for copy in copies:
        copy.start()
    for copy in copies[:4]:
        copy.wait()
    index[0:slots, :] = window_rows(cover[...], here(), chips, local_blocks, slab)
    index[slots : 2 * slots, :] = offset[...]
    index[2 * slots : 2 * slots + 1, :] = count[...]
    index[2 * slots + 1 : 2 * slots + 2, :] = angle[...]
    load = fetch(index, scal, sems.at[0])
    copies[4].wait()

    def fade(view, carry):
        rows = pl.ds(pl.multiple_of(view * det_rows, det_rows), det_rows)
        for tile in range(sino_ref.shape[0]):
            value = measured[view, :, tile * 128 : (tile + 1) * 128].astype(jnp.float32)
            decay_ref[tile, rows, :] = jnp.exp(-value)
            sino_ref[tile, rows, :] = -value
        return carry

    lax.fori_loop(0, views, fade, 0)
    load.wait()
    list_pairs(scal, lists, seen, height, held, 2 * piece, det_rows, tables, slab)
    save = fetch(lists, lists_ref, sems.at[0])
    for copy in copies[5:]:
        copy.wait()
    proj[...] = jnp.dot(window[...], table_ref[...], preferred_element_type=jnp.float32)
    for at in range(0, tables * channels, 128):
        turned_ref[at : at + 128, :] = table_ref[:, at : at + 128].T
    place(Pairs(lists, 2 * Pairs.ROWS), sino_ref, proj, slab)
    save.wait()


def fetch_group(lists_ref, group, lists, sem):
    return fetch(lists_ref.at[pl.ds(group * Pairs.ROWS, Pairs.ROWS)], lists, sem)


def fetch(source, target, sem):
    load = pltpu.make_async_copy(source, target, sem)
    load.start()
    return load


def project(load, lists, window, table_ref, begun_ref, sino_ref, proj, slab):
    sino_ref[...] = begun_ref[...]
    proj[...] = jnp.dot(window[...], table_ref[...], preferred_element_type=jnp.float32)
    load.wait()
    place(Pairs(lists), sino_ref, proj, slab)


def middle_kernel(
    lists_ref, first_ref, second_ref, table_ref, begun_ref, sino_ref, lists, window, proj, sem, *, slab
):
    load = fetch_group(lists_ref, 0, lists, sem)
    piece = proj.shape[0] // 2
    for k, ref in enumerate((first_ref, second_ref)):
        unfold(ref, 0, window, k * piece, piece)
    project(load, lists, window, table_ref, begun_ref, sino_ref, proj, slab)


def main_kernel(
    lists_ref,
    far_ref,
    table_ref,
    turned_ref,
    begun_ref,
    decay_ref,
    sino_ref,
    give_ref,
    lists,
    window,
    proj,
    picked,
    spread,
    sem,
    *,
    slab,
):
    load = fetch_group(lists_ref, 1, lists, sem)
    clear_rows(picked, spread.shape[0])
    piece = proj.shape[0] // 2
    for k in range(2):
        unfold(far_ref, k * far_ref.shape[0] // 2, window, k * piece, piece)
    project(load, lists, window, table_ref, begun_ref, sino_ref, proj, slab)
    pairs = Pairs(lists)
    gather(pairs, sino_ref, decay_ref, picked, spread.shape[0], slab)
    back_project(pairs, picked, turned_ref, spread, give_ref, slab)


def rest_kernel(
    lists_ref, turned_ref, sino_ref, decay_ref, out_ref, lists, picked, spread, sem, *, group, slab
):
    load = fetch_group(lists_ref, group, lists, sem)
    clear_rows(picked, spread.shape[0])
    load.wait()
    pairs = Pairs(lists)
    gather(pairs, sino_ref, decay_ref, picked, spread.shape[0], slab)
    back_project(pairs, picked, turned_ref, spread, out_ref, slab)


def prior_kernel(
    vol_ref, other_ref, first_ref, second_ref, far_ref, out_ref, *, devices, here
):
    slices, strip, row = vol_ref.shape
    part = slices
    piece = 2 * part
    position = here()
    core = lax.rem(position, 2)
    odd = lax.rem(position // 2, 2)

    def chip_slice(ref, which, base=0):
        at = part if which == 0 else part - 1
        tiles = strip * row // 128

        def column(tile):
            whole = ref[base + tile * piece + at : base + tile * piece + at + 1, :]
            tail = base + tiles * piece + 2 * tile
            mid, low = ref[tail : tail + 1, :], ref[tail + 1 : tail + 2, :]
            return whole.astype(jnp.float32) + (mid.astype(jnp.float32) + low.astype(jnp.float32))

        here = row // 128
        return lambda y: jnp.concatenate([column(y * here + k) for k in range(here)], axis=1)

    def core_slice(which):
        at = (part - 1) * which
        return lambda y: other_ref[at : at + 1, y, :]

    def emit(low, high):
        for y in range(strip):
            cols = slice(y * row, (y + 1) * row)
            here = vol_ref[:, y, :]
            below = jnp.concatenate([low(y), here[:-1]], axis=0)
            above = jnp.concatenate([here[1:], high(y)], axis=0)
            level = lax.broadcasted_iota(jnp.int32, here.shape, 0)
            down = jnp.clip(here - below, -DELTA, DELTA)
            total = jnp.where((level > 0) | (position > 0), down, 0.0)
            up = jnp.clip(here - above, -DELTA, DELTA)
            total += jnp.where((level < slices - 1) | (position < devices - 1), up, 0.0)
            if y > 0:
                total += jnp.clip(here - vol_ref[:, y - 1, :], -DELTA, DELTA)
            if y + 1 < strip:
                total += jnp.clip(here - vol_ref[:, y + 1, :], -DELTA, DELTA)
            lane = lax.broadcasted_iota(jnp.int32, here.shape, 1)
            left = jnp.clip(here - pltpu.roll(here, 1, 1), -DELTA, DELTA)
            total += jnp.where(lane > 0, left, 0.0)
            right = jnp.clip(here - pltpu.roll(here, row - 1, 1), -DELTA, DELTA)
            total += jnp.where(lane < row - 1, right, 0.0)
            out_ref[:, cols] = PRIOR_WEIGHT * total

    @pl.when((core == 0) & (odd == 0))
    def _():
        emit(chip_slice(far_ref, 1), core_slice(0))

    @pl.when((core == 0) & (odd == 1))
    def _():
        emit(chip_slice(far_ref, 1, far_ref.shape[0] // 2), core_slice(0))

    @pl.when((core == 1) & (odd == 0))
    def _():
        emit(core_slice(1), chip_slice(second_ref, 0))

    @pl.when((core == 1) & (odd == 1))
    def _():
        emit(core_slice(1), chip_slice(first_ref, 0))


def last_kernel(arrived_ref, passed_ref, prior_ref, out_hbm, total, sems):
    part, strip, row = total.shape
    copies = []
    step = part // sems.shape[0]
    for k in range(sems.shape[0]):
        here = slice(k * step, (k + 1) * step)
        for y in range(strip):
            cols = slice(y * row, (y + 1) * row)
            total[here, y, :] = (arrived_ref[here, cols] + passed_ref[here, cols]) + prior_ref[
                here, cols
            ]
        copies.append(pltpu.make_async_copy(total.at[here], out_hbm.at[here], sems.at[k]))
        copies[-1].start()
    for copy in copies:
        copy.wait()


def shards(volume, footprint, measured, angle_index, cover, offset, count):
    local_blocks, slab, strip, row = volume.shape
    views, det_rows, channels = measured.shape
    tables = footprint.shape[0]
    slots = cover.shape[1]
    plane = strip * row
    devices = lax.axis_size(AXES)
    position = lax.axis_index(AXES)
    swap, first, second = exchange_pairs(devices)
    back = lambda pairs: [(b, a) for a, b in pairs]
    send = lambda value, pairs: lax.ppermute(value, AXES, pairs)
    part = local_blocks * slab
    piece = 2 * part
    flat = volume.reshape(part, strip, row)
    table = footprint.reshape(tables, plane, channels)
    vmem = pl.BlockSpec(memory_space=pltpu.VMEM)
    smem = pl.BlockSpec(memory_space=pltpu.SMEM)
    shape = jax.ShapeDtypeStruct
    room = lambda mib: pltpu.CompilerParams(vmem_limit_bytes=mib * 1024 * 1024)
    cost = lambda flops, size: pl.CostEstimate(flops=flops, bytes_accessed=size, transcendentals=0)

    here = lambda: lax.axis_index("grp") * lax.axis_size("view") + lax.axis_index("view")
    hbm = pl.BlockSpec(memory_space=pltpu.HBM)
    stay = lambda value: pltpu.with_memory_space_constraint(value, pltpu.HBM)

    other = send(flat, swap)
    mine, packed = pl.pallas_call(
        load_kernel,
        out_shape=(shape(flat.shape, flat.dtype), shape((part, plane), jnp.bfloat16)),
        in_specs=[hbm],
        out_specs=(vmem, vmem),
        scratch_shapes=[pltpu.SemaphoreType.DMA],
        compiler_params=room(4),
        cost_estimate=cost(1, 1),
        name="load",
    )(stay(flat))
    other, mine, packed = lax.optimization_barrier((other, mine, packed))
    sent = shape((plane // 128 * (piece + 2), 128), jnp.bfloat16)
    for_first, for_second = pl.pallas_call(
        functools.partial(join_kernel, here=here),
        out_shape=(sent, sent),
        in_specs=[vmem] * 3,
        out_specs=(vmem, vmem),
        compiler_params=room(4),
        name="join",
    )(mine, packed, other)
    got_second = send(for_second, second)
    got_first = send(for_first, first)

    sino_shape = shape((channels // 128, views * det_rows, 128), jnp.float32)
    lists_shape = (Pairs.ROWS * Pairs.GROUPS, views * slots)
    table_vmem, turned, lists, sino, decay = pl.pallas_call(
        functools.partial(
            early_kernel,
            piece=piece,
            chips=devices // 2,
            local_blocks=local_blocks,
            slab=slab,
            here=here,
        ),
        out_shape=(
            shape((plane, tables * channels), table.dtype),
            shape((tables * channels, plane), table.dtype),
            shape(lists_shape, jnp.int32),
            sino_shape,
            sino_shape,
        ),
        in_specs=[vmem] + [hbm] * 6,
        out_specs=(vmem,) * 5,
        scratch_shapes=[
            pltpu.VMEM(measured.shape, measured.dtype),
            pltpu.VMEM((slots, views), jnp.int32),
            pltpu.VMEM((slots, views), jnp.int32),
            pltpu.VMEM((1, views), jnp.int32),
            pltpu.VMEM((1, views), jnp.int32),
            pltpu.VMEM((2 * slots + 2, views), jnp.int32),
            pltpu.SMEM((2 * slots + 2, views), jnp.int32),
            pltpu.SMEM(lists_shape, jnp.int32),
            pltpu.SMEM((5 * piece // slab, tables), jnp.int32),
            pltpu.SMEM((5 * piece // slab,), jnp.int32),
            pltpu.SMEM((5 * piece // slab, views * slots), jnp.int32),
            pltpu.VMEM((piece, plane), jnp.bfloat16),
            pltpu.VMEM((piece, tables * channels), jnp.float32),
            pltpu.SemaphoreType.DMA((5 + tables,)),
        ],
        compiler_params=room(16),
        cost_estimate=cost(1, 1),
        name="early",
    )(
        for_second,
        stay(table),
        stay(measured),
        stay(cover.T),
        stay(offset.T),
        stay(count.reshape(1, views)),
        stay(angle_index.reshape(1, views)),
    )
    got_second, got_first, table_vmem, turned, lists, sino, decay = lax.optimization_barrier(
        (got_second, got_first, table_vmem, turned, lists, sino, decay)
    )
    index = [pltpu.SMEM((Pairs.ROWS, views * slots), jnp.int32)]
    waits = [pltpu.SemaphoreType.DMA]
    rows_of = lambda rows: [pltpu.VMEM((rows, tables * channels), jnp.float32)]
    window = [pltpu.VMEM((2 * piece, plane), jnp.bfloat16)]
    picks_of = lambda blocks: [
        pltpu.VMEM(((max(views * slots, blocks) + MORE) * slab, tables * channels), jnp.bfloat16),
        pltpu.VMEM((blocks * slab, plane), jnp.float32),
    ]

    far = send(jnp.concatenate([got_first, got_second], axis=0), swap)
    sino = pl.pallas_call(
        functools.partial(middle_kernel, slab=slab),
        out_shape=sino_shape,
        in_specs=[vmem] * 5,
        out_specs=vmem,
        scratch_shapes=index + window + rows_of(2 * piece) + waits,
        compiler_params=room(16),
        cost_estimate=cost(1, 1),
        name="middle",
    )(lists, got_first, got_second, table_vmem, sino)
    far, sino = lax.optimization_barrier((far, sino))
    sino, give = pl.pallas_call(
        functools.partial(main_kernel, slab=slab),
        out_shape=(sino_shape, shape((2 * piece, plane), jnp.float32)),
        in_specs=[vmem] * 6,
        out_specs=(vmem, vmem),
        scratch_shapes=index + window + rows_of(2 * piece) + picks_of(STATIC) + waits,
        compiler_params=room(16),
        cost_estimate=cost(1, 1),
        name="main",
    )(lists, far, table_vmem, turned, sino, decay)
    taken = send(give, swap)
    keep = pl.pallas_call(
        functools.partial(rest_kernel, group=0, slab=slab),
        out_shape=shape((2 * piece, plane), jnp.float32),
        in_specs=[vmem] * 4,
        out_specs=vmem,
        scratch_shapes=index + picks_of(STATIC) + waits,
        compiler_params=room(16),
        cost_estimate=cost(1, 1),
        name="rest",
    )(lists, turned, sino, decay)
    taken, keep = lax.optimization_barrier((taken, keep))
    wire = lambda rows: (keep[rows] + taken[rows]).astype(jnp.bfloat16)
    back_second = send(wire(slice(piece, 2 * piece)), back(second))
    back_first = send(wire(slice(0, piece)), back(first))

    home = pl.pallas_call(
        functools.partial(rest_kernel, group=2, slab=slab),
        out_shape=shape((piece, plane), jnp.float32),
        in_specs=[vmem] * 4,
        out_specs=vmem,
        scratch_shapes=index + picks_of(8) + waits,
        compiler_params=room(16),
        cost_estimate=cost(1, 1),
        name="home",
    )(lists, turned, sino, decay)
    prior = pl.pallas_call(
        functools.partial(prior_kernel, devices=devices, here=here),
        out_shape=shape((part, plane), jnp.float32),
        in_specs=[vmem] * 5,
        out_specs=vmem,
        compiler_params=room(8),
        cost_estimate=cost(1, 1),
        name="prior",
    )(mine, other, got_first, got_second, far)
    back_second, back_first, home, prior = lax.optimization_barrier(
        (back_second, back_first, home, prior)
    )

    arrived = lambda rows: (
        back_second[rows].astype(jnp.float32) + back_first[rows].astype(jnp.float32)
    ) + home[rows]
    passed = send(arrived(slice(part, piece)), swap)
    out = pl.pallas_call(
        last_kernel,
        out_shape=shape((part, strip, row), jnp.float32),
        in_specs=[vmem] * 3,
        out_specs=hbm,
        scratch_shapes=[
            pltpu.VMEM((part, strip, row), jnp.float32),
            pltpu.SemaphoreType.DMA((4,)),
        ],
        compiler_params=room(4),
        name="last",
    )(arrived(slice(0, part)), passed, prior)
    return out.reshape(volume.shape)


def solution(mesh):
    in_specs = (
        P(AXES, None, None, None),
        P(AXES, None, None, None),
        P(AXES, None, None),
        P(AXES),
        P(AXES, None),
        P(AXES, None),
        P(AXES),
    )
    out_specs = P(AXES, None, None, None)
    return jax.shard_map(shards, mesh=mesh, in_specs=in_specs, out_specs=out_specs, check_vma=False)
```

```python
import functools

import jax
import jax.numpy as jnp
from jax import lax
from jax.experimental import pallas as pl
from jax.experimental.pallas import tpu as pltpu
from jax.sharding import PartitionSpec as P

AXES = ("grp", "view")
STATIC = 16
LEVELS = (8, 10, 12)
MORE = 4
DELTA = 0.5
PRIOR_WEIGHT = 2.0


def both_ways(pairs):
    return pairs + [(b, a) for a, b in pairs]


def exchange_pairs(devices):
    chips = devices // 2
    swap = [(i, i ^ 1) for i in range(devices)]
    edge_y = [(i, i + 1) for i in range(0, chips, 2)]
    edge_d = [(i, i + 1) for i in range(1, chips - 1, 2)]
    edge_a = [(i + j, i + j + 2) for i in range(0, chips, 4) for j in (0, 1)]
    edge_b = [(i + j, i + j + 2) for i in range(2, chips - 2, 4) for j in (0, 1)]
    idle = [(0, 1), (chips - 2, chips - 1)]
    on_core = lambda edges, core: [(2 * a + core, 2 * b + core) for a, b in edges]
    last = devices - 1
    ends = [(0, 4), (4, 1), (1, 0), (last - 1, last - 5), (last - 5, last), (last, last - 1)]
    first = both_ways(on_core(edge_a[1:-1], 0) + on_core(edge_d, 1)) + ends
    second = both_ways(on_core(edge_b + idle, 0) + on_core(edge_y, 1))
    return swap, first, second


def load_kernel(source, target, own_ref, sem):
    copy = pltpu.make_async_copy(source, target, sem)
    copy.start()
    copy.wait()
    strip, row = target.shape[1:]
    for y in range(strip):
        own_ref[:, y * row : (y + 1) * row] = target[:, y, :].astype(jnp.bfloat16)


def join_kernel(mine_ref, own_ref, other_ref, first_ref, second_ref, *, here):
    slices, strip, row = other_ref.shape
    tiles = strip * row // 128
    part = slices
    rest = {}
    for name, ref in (("mine", mine_ref), ("other", other_ref)):
        for at in (0, slices - 1):
            for y in range(strip):
                whole = ref[at : at + 1, y, :]
                left = whole - whole.astype(jnp.bfloat16).astype(jnp.float32)
                mid = left.astype(jnp.bfloat16).astype(jnp.float32)
                rest[name, at, y] = (mid, left - mid)
    position = here()
    core = lax.rem(position, 2)
    odd = lax.rem(position // 2, 2)
    for y in range(strip):
        packed = other_ref[:, y, :].astype(jnp.bfloat16)
        for k in range(row // 128):
            tile = y * (row // 128) + k
            cols = slice(k * 128, (k + 1) * 128)
            for ref in (first_ref, second_ref):
                ref[tile * 2 * part : tile * 2 * part + part, :] = own_ref[
                    :, tile * 128 : (tile + 1) * 128
                ]
                ref[tile * 2 * part + part : (tile + 1) * 2 * part, :] = packed[:, cols]
    top, bottom = [], []
    for y in range(strip):
        for k in range(row // 128):
            cols = slice(k * 128, (k + 1) * 128)
            for which in range(2):
                a = rest["mine", 0, y][which][:, cols]
                b = rest["other", 0, y][which][:, cols]
                top.append(jnp.where(core == 0, a, b))
                a = rest["mine", slices - 1, y][which][:, cols]
                b = rest["other", slices - 1, y][which][:, cols]
                bottom.append(jnp.where(core == 1, a, b))
    top = jnp.concatenate(top, axis=0)
    bottom = jnp.concatenate(bottom, axis=0)
    tail = slice(tiles * 2 * part, tiles * 2 * part + 2 * tiles)
    first_ref[tail, :] = jnp.where(odd == 1, bottom, top).astype(jnp.bfloat16)
    second_ref[tail, :] = jnp.where(odd == 1, top, bottom).astype(jnp.bfloat16)


def unfold(ref, begin, window, first_row, piece):
    for j in range(window.shape[1] // 128):
        window[first_row : first_row + piece, j * 128 : (j + 1) * 128] = ref[
            begin + j * piece : begin + (j + 1) * piece, :
        ]


def window_rows(block, position, chips, local_blocks, slab):
    part = local_blocks * slab
    piece = 2 * part
    core = lax.rem(position, 2)
    chip = position // 2
    owner = block // local_blocks
    owner_core = lax.rem(owner, 2)
    delta = owner // 2 - chip
    flag = lambda what: jnp.where(what, 1, 0)
    up = flag(delta > 0)
    nearer = jnp.abs(delta) == 1
    is_y = flag(up == 1 - lax.rem(chip, 2))
    is_a = flag(up == flag(lax.rem(chip, 4) < 2))
    second = jnp.where(nearer, is_y, 1 - is_a)
    via = flag(nearer)
    end = flag((chip == 0) | (chip == chips - 1))
    held = jnp.where(nearer, 1, is_a * end)
    away = (2 * jnp.abs(held - core) + second) * piece + jnp.abs(owner_core - via) * part
    here = 4 * piece + jnp.abs(owner_core - core) * part
    return jnp.where(delta == 0, here, away) + lax.rem(block, local_blocks) * slab


class Pairs:
    ROWS = 8
    GROUPS = 3

    def __init__(self, ref, first=0):
        self.ref = ref
        self.first = first

    def each(self, do):
        def body(i, carry):
            do(*(self.ref[self.first + k, i] for k in range(4)))
            return carry

        lax.fori_loop(0, self.ref[self.first + 5, 0], body, 0)

    def gathered(self):
        return self.ref[self.first + 5, 1]

    def target(self, i):
        return self.ref[self.first + 4, i]


def list_pairs(scal, lists, seen, height, held, near_rows, det_rows, tables, slab):
    slots = (scal.shape[0] - 2) // 2
    most = held.shape[1]
    fields, groups = Pairs.ROWS, Pairs.GROUPS

    def clear(i, carry):
        height[i] = jnp.int32(0)
        for table in range(tables):
            seen[i, table] = jnp.int32(0)
        return carry

    lax.fori_loop(0, height.shape[0], clear, 0)
    for k in range(groups):
        lists[fields * k + 5, 0] = jnp.int32(0)
        lists[fields * k + 5, 1] = jnp.int32(0)

    def body(view, carry):
        count = scal[2 * slots, view]
        table = scal[2 * slots + 1, view]
        for slot in range(slots):

            @pl.when(slot < count)
            def _():
                row = scal[slot, view]
                block = row // slab
                group = jnp.minimum(row // near_rows, groups - 1)
                local = row - group * near_rows
                first = fields * group
                at = lists[first + 5, 0]
                used = lists[first + 5, 1]
                rank = seen[block, table]
                top = height[block]
                fresh = rank >= top
                mine = jnp.where(fresh, used, held[block, rank])
                held[block, rank] = mine
                seen[block, table] = rank + 1
                height[block] = jnp.where(fresh, rank + 1, top)
                lists[first, at] = view * det_rows + scal[slots + slot, view]
                lists[first + 1, at] = table
                lists[first + 2, at] = local
                lists[first + 3, at] = mine * slab
                lists[first + 4, mine] = local
                lists[first + 5, 0] = at + 1
                lists[first + 5, 1] = used + jnp.where(fresh, 1, 0)

        return carry

    lax.fori_loop(0, scal.shape[1], body, 0)


def place(pairs, sino, proj, slab):
    width = sino.shape[0] * 128

    def add(target, table, local, dest):
        source = pl.ds(pl.multiple_of(local, slab), slab)
        for tile in range(sino.shape[0]):
            cols = pl.ds(pl.multiple_of(table * width + tile * 128, 128), 128)
            sino[tile, pl.ds(target, slab), :] += proj[source, cols]

    pairs.each(add)


def clear_rows(picked, static_rows):
    picked[0:static_rows, :] = jnp.zeros((static_rows, picked.shape[1]), picked.dtype)


def gather(pairs, sino, decay, picked, static_rows, slab):
    width = sino.shape[0] * 128
    chunk = MORE * slab

    def clear(i, carry):
        here = pl.ds(pl.multiple_of(static_rows + i * chunk, chunk), chunk)
        picked[here, :] = jnp.zeros((chunk, picked.shape[1]), picked.dtype)
        return carry

    more = pairs.gathered() * slab - static_rows
    lax.fori_loop(0, (more + chunk - 1) // chunk, clear, 0)

    def take(source, table, local, dest):
        target = pl.ds(pl.multiple_of(dest, slab), slab)
        here = pl.ds(source, slab)
        for tile in range(sino.shape[0]):
            cols = pl.ds(pl.multiple_of(table * width + tile * 128, 128), 128)
            value = decay[tile, here, :] * sino[tile, here, :]
            picked[target, cols] = value.astype(jnp.bfloat16)

    pairs.each(take)


def back_project(pairs, picked, turned_ref, spread, out_ref, slab):
    static_rows = spread.shape[0]
    static = static_rows // slab
    blocks = pairs.gathered()
    out_ref[...] = jnp.zeros_like(out_ref)

    def add_from(begin):
        def add(i, carry):
            target = pl.ds(pl.multiple_of(pairs.target(i), slab), slab)
            source = pl.ds(pl.multiple_of((i - begin) * slab, slab), slab)
            out_ref[target, :] += spread[source, :]
            return carry

        return add

    least = -1
    for most in [m for m in LEVELS if m < static] + [static]:
        rows = most * slab

        @pl.when((blocks > least) & ((blocks <= most) | (most == static)))
        def _():
            spread[0:rows, :] = jnp.dot(
                picked[0:rows, :], turned_ref[...], preferred_element_type=jnp.float32
            )

        least = most
    lax.fori_loop(0, jnp.minimum(blocks, static), add_from(0), 0)

    def further(c, carry):
        begin = static + c * MORE
        here = pl.ds(pl.multiple_of(begin * slab, MORE * slab), MORE * slab)
        spread[0 : MORE * slab, :] = jnp.dot(
            picked[here, :], turned_ref[...], preferred_element_type=jnp.float32
        )
        lax.fori_loop(begin, jnp.minimum(blocks, begin + MORE), add_from(begin), 0)
        return carry

    lax.fori_loop(0, (blocks - static + MORE - 1) // MORE, further, 0)


def early_kernel(
    both_ref,
    table_hbm,
    measured_hbm,
    cover_hbm,
    offset_hbm,
    count_hbm,
    angle_hbm,
    table_ref,
    turned_ref,
    lists_ref,
    sino_ref,
    decay_ref,
    measured,
    cover,
    offset,
    count,
    angle,
    index,
    scal,
    lists,
    seen,
    height,
    held,
    window,
    proj,
    sems,
    *,
    piece,
    chips,
    local_blocks,
    slab,
    here,
):
    views, det_rows, channels = measured.shape
    slots = cover.shape[0]
    tables = table_hbm.shape[0]
    small = [(cover_hbm, cover), (offset_hbm, offset), (count_hbm, count), (angle_hbm, angle)]
    unfold(both_ref, 0, window, 0, piece)
    copies = [pltpu.make_async_copy(a, b, sems.at[i]) for i, (a, b) in enumerate(small)]
    copies.append(pltpu.make_async_copy(measured_hbm, measured, sems.at[4]))
    for table in range(tables):
        to = table_ref.at[:, table * channels : (table + 1) * channels]
        copies.append(pltpu.make_async_copy(table_hbm.at[table], to, sems.at[5 + table]))
    for copy in copies:
        copy.start()
    for copy in copies[:4]:
        copy.wait()
    index[0:slots, :] = window_rows(cover[...], here(), chips, local_blocks, slab)
    index[slots : 2 * slots, :] = offset[...]
    index[2 * slots : 2 * slots + 1, :] = count[...]
    index[2 * slots + 1 : 2 * slots + 2, :] = angle[...]
    load = fetch(index, scal, sems.at[0])
    load.wait()
    list_pairs(scal, lists, seen, height, held, 2 * piece, det_rows, tables, slab)
    save = fetch(lists, lists_ref, sems.at[0])
    copies[4].wait()

    def fade(view, carry):
        rows = pl.ds(pl.multiple_of(view * det_rows, det_rows), det_rows)
        for tile in range(sino_ref.shape[0]):
            value = measured[view, :, tile * 128 : (tile + 1) * 128].astype(jnp.float32)
            decay_ref[tile, rows, :] = jnp.exp(-value)
            sino_ref[tile, rows, :] = -value
        return carry

    lax.fori_loop(0, views, fade, 0)
    for copy in copies[5:]:
        copy.wait()
    proj[...] = jnp.dot(window[...], table_ref[...], preferred_element_type=jnp.float32)
    for at in range(0, tables * channels, 128):
        turned_ref[at : at + 128, :] = table_ref[:, at : at + 128].T
    place(Pairs(lists, 2 * Pairs.ROWS), sino_ref, proj, slab)
    save.wait()


def fetch_group(lists_ref, group, lists, sem):
    return fetch(lists_ref.at[pl.ds(group * Pairs.ROWS, Pairs.ROWS)], lists, sem)


def fetch(source, target, sem):
    load = pltpu.make_async_copy(source, target, sem)
    load.start()
    return load


def project(load, lists, window, table_ref, begun_ref, sino_ref, proj, slab):
    sino_ref[...] = begun_ref[...]
    proj[...] = jnp.dot(window[...], table_ref[...], preferred_element_type=jnp.float32)
    load.wait()
    place(Pairs(lists), sino_ref, proj, slab)


def middle_kernel(
    lists_ref, first_ref, second_ref, table_ref, begun_ref, sino_ref, lists, window, proj, sem, *, slab
):
    load = fetch_group(lists_ref, 0, lists, sem)
    piece = proj.shape[0] // 2
    for k, ref in enumerate((first_ref, second_ref)):
        unfold(ref, 0, window, k * piece, piece)
    project(load, lists, window, table_ref, begun_ref, sino_ref, proj, slab)


def main_kernel(
    lists_ref,
    far_ref,
    table_ref,
    turned_ref,
    begun_ref,
    decay_ref,
    sino_ref,
    give_ref,
    lists,
    window,
    proj,
    picked,
    spread,
    sem,
    *,
    slab,
):
    load = fetch_group(lists_ref, 1, lists, sem)
    clear_rows(picked, spread.shape[0])
    piece = proj.shape[0] // 2
    for k in range(2):
        unfold(far_ref, k * far_ref.shape[0] // 2, window, k * piece, piece)
    project(load, lists, window, table_ref, begun_ref, sino_ref, proj, slab)
    pairs = Pairs(lists)
    gather(pairs, sino_ref, decay_ref, picked, spread.shape[0], slab)
    back_project(pairs, picked, turned_ref, spread, give_ref, slab)


def rest_kernel(
    lists_ref, turned_ref, sino_ref, decay_ref, out_ref, lists, picked, spread, sem, *, group, slab
):
    load = fetch_group(lists_ref, group, lists, sem)
    clear_rows(picked, spread.shape[0])
    load.wait()
    pairs = Pairs(lists)
    gather(pairs, sino_ref, decay_ref, picked, spread.shape[0], slab)
    back_project(pairs, picked, turned_ref, spread, out_ref, slab)


def prior_kernel(
    vol_ref, other_ref, first_ref, second_ref, far_ref, out_ref, *, devices, here
):
    slices, strip, row = vol_ref.shape
    part = slices
    piece = 2 * part
    position = here()
    core = lax.rem(position, 2)
    odd = lax.rem(position // 2, 2)

    def chip_slice(ref, which, base=0):
        at = part if which == 0 else part - 1
        tiles = strip * row // 128

        def column(tile):
            whole = ref[base + tile * piece + at : base + tile * piece + at + 1, :]
            tail = base + tiles * piece + 2 * tile
            mid, low = ref[tail : tail + 1, :], ref[tail + 1 : tail + 2, :]
            return whole.astype(jnp.float32) + (mid.astype(jnp.float32) + low.astype(jnp.float32))

        here = row // 128
        return lambda y: jnp.concatenate([column(y * here + k) for k in range(here)], axis=1)

    def core_slice(which):
        at = (part - 1) * which
        return lambda y: other_ref[at : at + 1, y, :]

    def emit(low, high):
        for y in range(strip):
            cols = slice(y * row, (y + 1) * row)
            here = vol_ref[:, y, :]
            below = jnp.concatenate([low(y), here[:-1]], axis=0)
            above = jnp.concatenate([here[1:], high(y)], axis=0)
            level = lax.broadcasted_iota(jnp.int32, here.shape, 0)
            down = jnp.clip(here - below, -DELTA, DELTA)
            total = jnp.where((level > 0) | (position > 0), down, 0.0)
            up = jnp.clip(here - above, -DELTA, DELTA)
            total += jnp.where((level < slices - 1) | (position < devices - 1), up, 0.0)
            if y > 0:
                total += jnp.clip(here - vol_ref[:, y - 1, :], -DELTA, DELTA)
            if y + 1 < strip:
                total += jnp.clip(here - vol_ref[:, y + 1, :], -DELTA, DELTA)
            lane = lax.broadcasted_iota(jnp.int32, here.shape, 1)
            left = jnp.clip(here - pltpu.roll(here, 1, 1), -DELTA, DELTA)
            total += jnp.where(lane > 0, left, 0.0)
            right = jnp.clip(here - pltpu.roll(here, row - 1, 1), -DELTA, DELTA)
            total += jnp.where(lane < row - 1, right, 0.0)
            out_ref[:, cols] = PRIOR_WEIGHT * total

    @pl.when((core == 0) & (odd == 0))
    def _():
        emit(chip_slice(far_ref, 1), core_slice(0))

    @pl.when((core == 0) & (odd == 1))
    def _():
        emit(chip_slice(far_ref, 1, far_ref.shape[0] // 2), core_slice(0))

    @pl.when((core == 1) & (odd == 0))
    def _():
        emit(core_slice(1), chip_slice(second_ref, 0))

    @pl.when((core == 1) & (odd == 1))
    def _():
        emit(core_slice(1), chip_slice(first_ref, 0))


def last_kernel(arrived_ref, passed_ref, prior_ref, out_hbm, total, sems):
    part, strip, row = total.shape
    copies = []
    step = part // sems.shape[0]
    for k in range(sems.shape[0]):
        here = slice(k * step, (k + 1) * step)
        for y in range(strip):
            cols = slice(y * row, (y + 1) * row)
            total[here, y, :] = (arrived_ref[here, cols] + passed_ref[here, cols]) + prior_ref[
                here, cols
            ]
        copies.append(pltpu.make_async_copy(total.at[here], out_hbm.at[here], sems.at[k]))
        copies[-1].start()
    for copy in copies:
        copy.wait()


def shards(volume, footprint, measured, angle_index, cover, offset, count):
    local_blocks, slab, strip, row = volume.shape
    views, det_rows, channels = measured.shape
    tables = footprint.shape[0]
    slots = cover.shape[1]
    plane = strip * row
    devices = lax.axis_size(AXES)
    position = lax.axis_index(AXES)
    swap, first, second = exchange_pairs(devices)
    back = lambda pairs: [(b, a) for a, b in pairs]
    send = lambda value, pairs: lax.ppermute(value, AXES, pairs)
    part = local_blocks * slab
    piece = 2 * part
    flat = volume.reshape(part, strip, row)
    table = footprint.reshape(tables, plane, channels)
    vmem = pl.BlockSpec(memory_space=pltpu.VMEM)
    smem = pl.BlockSpec(memory_space=pltpu.SMEM)
    shape = jax.ShapeDtypeStruct
    room = lambda mib: pltpu.CompilerParams(vmem_limit_bytes=mib * 1024 * 1024)
    cost = lambda flops, size: pl.CostEstimate(flops=flops, bytes_accessed=size, transcendentals=0)

    here = lambda: lax.axis_index("grp") * lax.axis_size("view") + lax.axis_index("view")
    hbm = pl.BlockSpec(memory_space=pltpu.HBM)
    stay = lambda value: pltpu.with_memory_space_constraint(value, pltpu.HBM)

    other = send(flat, swap)
    mine, packed = pl.pallas_call(
        load_kernel,
        out_shape=(shape(flat.shape, flat.dtype), shape((part, plane), jnp.bfloat16)),
        in_specs=[hbm],
        out_specs=(vmem, vmem),
        scratch_shapes=[pltpu.SemaphoreType.DMA],
        compiler_params=room(4),
        cost_estimate=cost(1, 1),
        name="load",
    )(stay(flat))
    other, mine, packed = lax.optimization_barrier((other, mine, packed))
    sent = shape((plane // 128 * (piece + 2), 128), jnp.bfloat16)
    for_first, for_second = pl.pallas_call(
        functools.partial(join_kernel, here=here),
        out_shape=(sent, sent),
        in_specs=[vmem] * 3,
        out_specs=(vmem, vmem),
        compiler_params=room(4),
        name="join",
    )(mine, packed, other)
    got_second = send(for_second, second)
    got_first = send(for_first, first)

    sino_shape = shape((channels // 128, views * det_rows, 128), jnp.float32)
    lists_shape = (Pairs.ROWS * Pairs.GROUPS, views * slots)
    table_vmem, turned, lists, sino, decay = pl.pallas_call(
        functools.partial(
            early_kernel,
            piece=piece,
            chips=devices // 2,
            local_blocks=local_blocks,
            slab=slab,
            here=here,
        ),
        out_shape=(
            shape((plane, tables * channels), table.dtype),
            shape((tables * channels, plane), table.dtype),
            shape(lists_shape, jnp.int32),
            sino_shape,
            sino_shape,
        ),
        in_specs=[vmem] + [hbm] * 6,
        out_specs=(vmem,) * 5,
        scratch_shapes=[
            pltpu.VMEM(measured.shape, measured.dtype),
            pltpu.VMEM((slots, views), jnp.int32),
            pltpu.VMEM((slots, views), jnp.int32),
            pltpu.VMEM((1, views), jnp.int32),
            pltpu.VMEM((1, views), jnp.int32),
            pltpu.VMEM((2 * slots + 2, views), jnp.int32),
            pltpu.SMEM((2 * slots + 2, views), jnp.int32),
            pltpu.SMEM(lists_shape, jnp.int32),
            pltpu.SMEM((5 * piece // slab, tables), jnp.int32),
            pltpu.SMEM((5 * piece // slab,), jnp.int32),
            pltpu.SMEM((5 * piece // slab, views * slots), jnp.int32),
            pltpu.VMEM((piece, plane), jnp.bfloat16),
            pltpu.VMEM((piece, tables * channels), jnp.float32),
            pltpu.SemaphoreType.DMA((5 + tables,)),
        ],
        compiler_params=room(16),
        cost_estimate=cost(1, 1),
        name="early",
    )(
        for_second,
        stay(table),
        stay(measured),
        stay(cover.T),
        stay(offset.T),
        stay(count.reshape(1, views)),
        stay(angle_index.reshape(1, views)),
    )
    got_second, got_first, table_vmem, turned, lists, sino, decay = lax.optimization_barrier(
        (got_second, got_first, table_vmem, turned, lists, sino, decay)
    )
    index = [pltpu.SMEM((Pairs.ROWS, views * slots), jnp.int32)]
    waits = [pltpu.SemaphoreType.DMA]
    rows_of = lambda rows: [pltpu.VMEM((rows, tables * channels), jnp.float32)]
    window = [pltpu.VMEM((2 * piece, plane), jnp.bfloat16)]
    picks_of = lambda blocks: [
        pltpu.VMEM(((max(views * slots, blocks) + MORE) * slab, tables * channels), jnp.bfloat16),
        pltpu.VMEM((blocks * slab, plane), jnp.float32),
    ]

    far = send(jnp.concatenate([got_first, got_second], axis=0), swap)
    sino = pl.pallas_call(
        functools.partial(middle_kernel, slab=slab),
        out_shape=sino_shape,
        in_specs=[vmem] * 5,
        out_specs=vmem,
        scratch_shapes=index + window + rows_of(2 * piece) + waits,
        compiler_params=room(16),
        cost_estimate=cost(1, 1),
        name="middle",
    )(lists, got_first, got_second, table_vmem, sino)
    far, sino = lax.optimization_barrier((far, sino))
    sino, give = pl.pallas_call(
        functools.partial(main_kernel, slab=slab),
        out_shape=(sino_shape, shape((2 * piece, plane), jnp.float32)),
        in_specs=[vmem] * 6,
        out_specs=(vmem, vmem),
        scratch_shapes=index + window + rows_of(2 * piece) + picks_of(STATIC) + waits,
        compiler_params=room(16),
        cost_estimate=cost(1, 1),
        name="main",
    )(lists, far, table_vmem, turned, sino, decay)
    taken = send(give, swap)
    keep = pl.pallas_call(
        functools.partial(rest_kernel, group=0, slab=slab),
        out_shape=shape((2 * piece, plane), jnp.float32),
        in_specs=[vmem] * 4,
        out_specs=vmem,
        scratch_shapes=index + picks_of(STATIC) + waits,
        compiler_params=room(16),
        cost_estimate=cost(1, 1),
        name="rest",
    )(lists, turned, sino, decay)
    taken, keep = lax.optimization_barrier((taken, keep))
    wire = lambda rows: (keep[rows] + taken[rows]).astype(jnp.bfloat16)
    back_second = send(wire(slice(piece, 2 * piece)), back(second))
    back_first = send(wire(slice(0, piece)), back(first))

    home = pl.pallas_call(
        functools.partial(rest_kernel, group=2, slab=slab),
        out_shape=shape((piece, plane), jnp.float32),
        in_specs=[vmem] * 4,
        out_specs=vmem,
        scratch_shapes=index + picks_of(8) + waits,
        compiler_params=room(16),
        cost_estimate=cost(1, 1),
        name="home",
    )(lists, turned, sino, decay)
    prior = pl.pallas_call(
        functools.partial(prior_kernel, devices=devices, here=here),
        out_shape=shape((part, plane), jnp.float32),
        in_specs=[vmem] * 5,
        out_specs=vmem,
        compiler_params=room(8),
        cost_estimate=cost(1, 1),
        name="prior",
    )(mine, other, got_first, got_second, far)
    back_second, back_first, home, prior = lax.optimization_barrier(
        (back_second, back_first, home, prior)
    )

    arrived = lambda rows: (
        back_second[rows].astype(jnp.float32) + back_first[rows].astype(jnp.float32)
    ) + home[rows]
    passed = send(arrived(slice(part, piece)), swap)
    out = pl.pallas_call(
        last_kernel,
        out_shape=shape((part, strip, row), jnp.float32),
        in_specs=[vmem] * 3,
        out_specs=hbm,
        scratch_shapes=[
            pltpu.VMEM((part, strip, row), jnp.float32),
            pltpu.SemaphoreType.DMA((4,)),
        ],
        compiler_params=room(4),
        name="last",
    )(arrived(slice(0, part)), passed, prior)
    return out.reshape(volume.shape)


def solution(mesh):
    in_specs = (
        P(AXES, None, None, None),
        P(AXES, None, None, None),
        P(AXES, None, None),
        P(AXES),
        P(AXES, None),
        P(AXES, None),
        P(AXES),
    )
    out_specs = P(AXES, None, None, None)
    return jax.shard_map(shards, mesh=mesh, in_specs=in_specs, out_specs=out_specs, check_vma=False)
```
